256 devices in a mesh: lat: 16 (over y_lo, x, core), lon: 16 (over z, y_hi).
Axes of the slice: x: 4, y: 4 (y_hi: 2, y_lo: 2; y = y_hi * 2 + y_lo), z: 8, core: 2. Of those that a mesh axis runs over, the one named last changes fastest.
Arguments:
- field: bfloat16 [1, 64, 512, 2048], P(None, None, 'lat', 'lon'), may hold values from -6 to 6
- kernel: bfloat16 [3, 3, 64, 64], replicated, may hold values from -0.25 to 0.25
- cotangent: bfloat16 [1, 64, 512, 2048], P(None, None, 'lat', 'lon'), may hold values from -6 to 6
Outputs:
- output: bfloat16 [1, 64, 512, 2048], P(None, None, 'lat', 'lon')
- grad_input: bfloat16 [1, 64, 512, 2048], P(None, None, 'lat', 'lon')
- grad_kernel: float32 [3, 3, 64, 64], replicated
The draws below stay inside these ranges and needn't reach their ends.
All inputs are finite; a program needn't handle non-finite values.
Results may differ from the reference program's by a relative error of at most 0.0039.
Values may be sent and summed in bfloat16 or wider, within the bound.
No kernel may reach another device: no remote copies, remote signals or barrier semaphores. Data moves between devices by JAX's collectives and lax.ppermute only.
A program may use at most 64 MiB of HBM per device.

```python
import math
import jax
import jax.numpy as jnp
from jax import lax

CHANNELS = 64
SAMPLES = 1
NLAT = 512
NLON = 2048


def levels(key, dims, split, smallest, largest):
    def one(axis_at, shards_of):
        heights = jax.random.uniform(jax.random.fold_in(jax.random.fold_in(key, 6), axis_at), (shards_of,), jnp.float32, smallest / len(split), largest / len(split))
        return jnp.repeat(jnp.exp(heights), dims[axis_at] // shards_of).reshape((-1,) + (1,) * (len(dims) - axis_at - 1))

    loudness = one(*split[0])
    for cut in split[1:]:
        loudness = loudness * one(*cut)
    return loudness


def centred(rng, extent, scale, most, pieces=(), held_as=jnp.bfloat16):
    factor_of = levels(rng, extent, pieces, -0.22, 0.18) if pieces else 1.0
    drawn = jax.random.normal(rng, extent, jnp.float32) * scale * factor_of
    return jnp.minimum(jnp.maximum(drawn, -most), most).astype(held_as)


def setup_inputs(seed: int = 0) -> dict:
    key_of = jax.random.split(jax.random.key(seed), 4)
    return {
        "field": centred(key_of[0], (SAMPLES, CHANNELS, NLAT, NLON), 1.0, 6.0, ((2, 16), (3, 16))),
        "kernel": centred(key_of[1], (3, 3, CHANNELS, CHANNELS), (9 * CHANNELS) ** -0.5, 0.25),
        "cotangent": centred(key_of[2], (SAMPLES, CHANNELS, NLAT, NLON), 1.0, 6.0, ((2, 16), (3, 16))),
    }


gelu_scale = math.sqrt(2.0 / math.pi)

def gelu_parts(hidden):
    cubic = hidden * hidden * hidden
    tangent = jnp.tanh(gelu_scale * (hidden + 0.044715 * cubic))
    value = 0.5 * hidden * (1.0 + tangent)
    slope = 0.5 * (1.0 + tangent) + 0.5 * hidden * (1.0 - tangent * tangent) * gelu_scale * (1.0 + 3.0 * 0.044715 * hidden * hidden)
    return (value, slope)

def pole_pad(plane):
    half = plane.shape[2] // 2
    upper = jnp.roll(plane[:, :1], half, axis=2)
    lower = jnp.roll(plane[:, -1:], half, axis=2)
    tall = jnp.concatenate([upper, plane, lower], 1)
    return jnp.concatenate([tall[:, :, -1:], tall, tall[:, :, :1]], 2)

def convolve(plane, weights):
    stacked = pole_pad(plane)[None]
    result = lax.conv_general_dilated(stacked, jnp.transpose(weights, (2, 3, 0, 1)), (1, 1), 'VALID', dimension_numbers=('NCHW', 'OIHW', 'NCHW'))
    return result[0]

def reference(field, kernel, cotangent):
    weights = kernel.astype(jnp.float32)

    def one_sample(pair):
        plane, cot_plane = pair
        plane_wide = plane.astype(jnp.float32)
        hidden, pullback = jax.vjp(convolve, plane_wide, weights)
        value, slope = gelu_parts(hidden)
        output = (plane_wide + value).astype(jnp.bfloat16)
        delta = (cot_plane.astype(jnp.float32) * slope).astype(jnp.bfloat16)
        delta = lax.optimization_barrier(delta)
        back, grad_w = pullback(delta.astype(jnp.float32))
        grad_in = (cot_plane.astype(jnp.float32) + back).astype(jnp.bfloat16)
        return (output, grad_in, grad_w)
    outputs, grads, kernel_terms = lax.map(one_sample, (field, cotangent))
    scale = float(SAMPLES * NLAT * NLON) ** (-0.5)
    return (outputs, grads, lax.optimization_barrier(jnp.sum(kernel_terms, 0)) * scale)
```

```python
import math

import jax
import jax.numpy as jnp
from jax import lax
from jax.experimental import pallas as pl
from jax.experimental.pallas import tpu as pltpu
from jax.sharding import Mesh
from jax.sharding import PartitionSpec as P

gelu_scale = math.sqrt(2.0 / math.pi)
ROWS, COLS, CH = 32, 128, 64
TAPS = 3 * CH
PIECES = 4
ROW_SLOTS = ({0: (0,), 1: (1,), ROWS - 1: (3,), ROWS - 2: (4,)}, {0: (2,), ROWS - 1: (5,)})
f32, bf16 = jnp.float32, jnp.bfloat16
LON = ("z", "side")
PLANE = ("lat", "side")
EVERY = ("lat", "z", "side")


def gelu_parts(hidden):
    square = hidden * hidden
    half = 0.5 + 0.5 * jnp.tanh(gelu_scale * hidden * (1.0 + 0.044715 * square))
    steep = gelu_scale * (1.0 + 3.0 * 0.044715 * square)
    return (hidden * half, half + 2.0 * hidden * half * (1.0 - half) * steep)


def roll(x, shift):
    return pltpu.roll(x, shift % x.shape[1], 1)


def lanes(width=COLS):
    return lax.broadcasted_iota(jnp.int32, (CH, width), 1)


def call(body, out_shape, args, scratch=(), flops=0, space=pltpu.VMEM, limit=24):
    outs = [jax.ShapeDtypeStruct(s, d) for s, d in out_shape]
    size = sum(a.size * a.dtype.itemsize for a in list(args) + outs)
    return pl.pallas_call(
        body,
        out_shape=outs,
        in_specs=[pl.BlockSpec(memory_space=space)] * len(args),
        out_specs=[pl.BlockSpec(memory_space=pltpu.VMEM)] * len(outs),
        scratch_shapes=list(scratch),
        cost_estimate=pl.CostEstimate(flops=flops, bytes_accessed=size, transcendentals=0),
        compiler_params=pltpu.CompilerParams(vmem_limit_bytes=limit * 2**20),
    )(*args)


def pack_body(f_hbm, g_hbm, edge_ref, rows_ref, wide, f_ref, g_ref, sems):
    lane = lanes()
    part = CH * ROWS // PIECES
    copies = [
        [
            pltpu.make_async_copy(src.at[pl.ds(i * part, part)], dst.at[pl.ds(i * part, part)], sems.at[at, i])
            for i in range(PIECES)
        ]
        for at, (src, dst) in enumerate(((f_hbm, f_ref), (g_hbm, g_ref)))
    ]
    for copy in copies[0] + copies[1]:
        copy.start()
    for at, src in enumerate((f_ref, g_ref)):
        for i, copy in enumerate(copies[at]):
            copy.wait()
            wide[pl.ds(i * part, part), :] = src[pl.ds(i * part, part), :].astype(f32)
        edge = jnp.zeros((CH, COLS), f32)
        for r in range(ROWS):
            row = wide[pl.ds(r, CH, stride=ROWS), :]
            edge = jnp.where((lane >= 4 * r) & (lane < 4 * r + 4), roll(row, 4 * r + 2), edge)
            for slot in ROW_SLOTS[at].get(r, ()):
                rows_ref[pl.ds(slot * CH, CH), :] = row.astype(bf16)
        edge_ref[pl.ds(at * CH, CH), :] = edge.astype(bf16)


def turn_body(f_ref, g_ref, fr_ref, gr_ref, wide):
    for src, dst in ((f_ref, fr_ref), (g_ref, gr_ref)):
        wide[...] = src[...].astype(f32)
        for r in range(ROWS):
            dst[r] = wide[pl.ds(r, CH, stride=ROWS), :].astype(bf16)


def strip(west_ref, east_ref, part):
    at = pl.ds(part * CH, CH)
    return jnp.where(lanes() % 4 < 2, west_ref[at, :].astype(f32), east_ref[at, :].astype(f32))


def ring_body(rows_ref, west_ref, east_ref, ahead_ref, behind_ref):
    rising = lax.axis_index("z") < lax.axis_size("z") // 2
    lane = lanes()
    s = strip(west_ref, east_ref, 0)
    gs = strip(west_ref, east_ref, 1)
    top = jnp.where(lane < 8, s, roll(gs, 8))
    bottom = jnp.where(lane < 4, roll(s, 4), jnp.where(lane < 8, roll(s, 12), roll(gs, 12)))
    half = pl.ds(0, TAPS)
    first = rows_ref[pl.ds(0, TAPS), :]
    last = rows_ref[pl.ds(TAPS, TAPS), :]
    ahead_ref[half, :] = jnp.where(rising, last, first)
    behind_ref[half, :] = jnp.where(rising, first, last)
    corner = pl.ds(TAPS, CH)
    ahead_ref[corner, :] = jnp.where(rising, bottom, top).astype(bf16)
    behind_ref[corner, :] = jnp.where(rising, top, bottom).astype(bf16)


def stack_taps(out_ref, at, own, halo, lane):
    out_ref[at, pl.ds(0, CH), :] = roll(jnp.where(lane == COLS - 1, halo, own), 1).astype(bf16)
    out_ref[at, pl.ds(CH, CH), :] = own.astype(bf16)
    out_ref[at, pl.ds(2 * CH, CH), :] = roll(jnp.where(lane == 0, halo, own), -1).astype(bf16)


def dot(a, b):
    return jnp.dot(a, b, preferred_element_type=f32)


def forward_body(
    fr_ref, gr_ref, edge_ref, west_ref, east_ref, ahead_ref, behind_ref, w_ref, w3_ref, wa_ref,
    out_ref, delta_ref, dstrip_ref, grad_ref, xs, wide,
):
    lat = lax.axis_index("lat")
    at_top = lat == 0
    at_bottom = lat == lax.axis_size("lat") - 1
    rising = lax.axis_index("z") < lax.axis_size("z") // 2
    lane = lanes()
    north = jnp.where(rising, ahead_ref[...], behind_ref[...]).astype(f32)
    south = jnp.where(rising, behind_ref[...], ahead_ref[...]).astype(f32)
    n_near, n_far, n_cot, n_corner = [north[i * CH : (i + 1) * CH] for i in range(4)]
    s_near, s_far, s_cot, s_corner = [south[i * CH : (i + 1) * CH] for i in range(4)]

    s = strip(west_ref, east_ref, 0)
    beyond = jnp.where(
        lane < 64, s_corner, jnp.where(lane >= 124, roll(n_corner, 124), roll(n_corner, 116))
    )
    gs = strip(west_ref, east_ref, 1)
    gbeyond = jnp.where(lane < 64, roll(s_corner, 120), roll(n_corner, 116))

    stack_taps(xs, 0, n_far, roll(beyond, -122), lane)
    stack_taps(xs, 1, n_near, roll(beyond, -126), lane)
    for r in range(ROWS):
        stack_taps(xs, r + 2, fr_ref[r].astype(f32), roll(s, -(4 * r + 2)), lane)
    stack_taps(xs, ROWS + 2, s_near, roll(beyond, -2), lane)
    stack_taps(xs, ROWS + 3, s_far, roll(beyond, -6), lane)

    weights = w_ref[...]
    for r in range(0, ROWS, 2):
        window = jnp.concatenate(
            [xs[r + 1 : r + 4].reshape(3 * TAPS, COLS), xs[r + 2 : r + 5].reshape(3 * TAPS, COLS)], 1
        )
        value, slope = gelu_parts(dot(weights, window))
        for k in range(2):
            cut = slice(k * COLS, (k + 1) * COLS)
            wide[pl.ds(r + k, CH, stride=ROWS), :] = fr_ref[r + k].astype(f32) + value[:, cut]
            delta_ref[r + k + 1] = (gr_ref[r + k].astype(f32) * slope[:, cut]).astype(bf16)
    out_ref[...] = wide[...].astype(bf16)

    def outer(inside, near, far, flip, cot, up):
        ends = (far, inside) if up else (inside, far)
        first = jnp.where(flip, xs[ends[1]], xs[ends[0]])
        last = jnp.where(flip, xs[ends[0]], xs[ends[1]])
        total = dot(w3_ref[0], first) + dot(w3_ref[1], xs[near]) + dot(w3_ref[2], last)
        return (cot * gelu_parts(total)[1]).astype(bf16)

    delta_ref[0] = outer(2, 1, 0, at_top, n_cot, True)
    delta_ref[ROWS + 1] = outer(ROWS + 1, ROWS + 2, ROWS + 3, at_bottom, s_cot, False)

    own_beyond = jnp.where(
        lane < 64,
        jnp.where(lane < 4, roll(s_near, 2), roll(s_far, 6)),
        jnp.where(lane >= 124, roll(n_near, 126), roll(n_far, 122)),
    )
    halo = jnp.concatenate([s, beyond], 1)
    own = jnp.concatenate([edge_ref[pl.ds(0, CH), :].astype(f32), own_beyond], 1)
    wide_lane = lanes(2 * COLS)
    kind = wide_lane % 4
    columns = jnp.concatenate(
        [roll(jnp.where(kind == 0, halo, own), 1), halo, roll(jnp.where(kind == 3, halo, own), -1)], 0
    ).astype(bf16)
    y = dot(wa_ref[...], columns)
    y0, y1, y2 = [y[i * CH : (i + 1) * CH] for i in range(3)]
    straight = roll(y0, 4) + y1 + roll(y2, -4)
    turned = roll(y2, 4) + y1 + roll(y0, -4)
    flip = ((wide_lane >= 252) & at_top) | ((wide_lane >= 128) & (wide_lane < 132) & at_bottom)
    slope = gelu_parts(jnp.where(flip, turned, straight))[1]
    dstrip_ref[...] = (jnp.concatenate([gs, gbeyond], 1) * slope).astype(bf16)

    total = None
    group = 8
    for r in range(0, ROWS, group):
        left = jnp.concatenate([delta_ref[r + k + 1] for k in range(group)], 1)
        right = jnp.concatenate([xs[r + k + 1 : r + k + 4].reshape(3 * TAPS, COLS) for k in range(group)], 1)
        term = lax.dot_general(left, right, (((1,), (1,)), ((), ())), preferred_element_type=f32)
        total = term if total is None else total + term
    total = total * grad_scale()
    pieces = [total[:, p * COLS : (p + 1) * COLS] for p in range(4)] + [total[:, 4 * COLS :]]
    count = grad_ref.shape[0]
    for at, piece in enumerate(pieces):
        for j in range(CH // count):
            width = piece.shape[1]
            start = at * COLS * CH // count + j * width
            grad_ref[:, 0, pl.ds(start, width)] = piece[j * count : (j + 1) * count]


def grad_scale():
    return float(ROWS * COLS * lax.axis_size(EVERY)) ** (-0.5)


def backward_body(delta_ref, dstrip_ref, gr_ref, wb_ref, wb3_ref, out_ref, xs, wide):
    lat = lax.axis_index("lat")
    at_top = lat == 0
    at_bottom = lat == lax.axis_size("lat") - 1
    lane = lanes()
    s = dstrip_ref[:, :COLS].astype(f32)
    beyond = dstrip_ref[:, COLS:].astype(f32)
    stack_taps(xs, 0, delta_ref[0].astype(f32), roll(beyond, -126), lane)
    for r in range(ROWS):
        stack_taps(xs, r + 1, delta_ref[r + 1].astype(f32), roll(s, -(4 * r + 2)), lane)
    stack_taps(xs, ROWS + 1, delta_ref[ROWS + 1].astype(f32), roll(beyond, -2), lane)
    weights = wb_ref[...]

    def put(r, back):
        wide[pl.ds(r, CH, stride=ROWS), :] = gr_ref[r].astype(f32) + back

    upper = jnp.where(at_top, wb3_ref[2], wb3_ref[0])
    lower = jnp.where(at_bottom, wb3_ref[0], wb3_ref[2])
    put(0, dot(upper, xs[0]) + dot(wb3_ref[1], xs[1]) + dot(wb3_ref[2], xs[2]))
    end = ROWS - 1
    put(end, dot(wb3_ref[0], xs[end]) + dot(wb3_ref[1], xs[end + 1]) + dot(lower, xs[end + 2]))
    for r in range(1, ROWS - 1, 2):
        window = jnp.concatenate(
            [xs[r : r + 3].reshape(3 * TAPS, COLS), xs[r + 1 : r + 4].reshape(3 * TAPS, COLS)], 1
        )
        back = dot(weights, window)
        put(r, back[:, :COLS])
        put(r + 1, back[:, COLS:])
    out_ref[...] = wide[...].astype(bf16)


def fold_body(parts_ref, out_ref):
    total = jnp.sum(parts_ref[...], 0)
    for i in range(out_ref.shape[0]):
        out_ref[i] = total


def unpack_body(parts_ref, out_ref):
    count = parts_ref.shape[0]
    for tap in range(9):
        at = tap // 2
        width = min(COLS, 9 * CH - at * COLS)
        for j in range(CH // count):
            start = at * COLS * CH // count + j * width + (tap % 2) * CH
            out_ref[tap, pl.ds(j * count, count), :] = parts_ref[:, 0, pl.ds(start, CH)]


def ring_pairs(lat_count, lon_count):
    half = lon_count // 2
    pairs = []
    for l in range(lat_count):
        for m in range(lon_count):
            if m < half:
                to = (l + 1, m) if l + 1 < lat_count else (l, m + half)
            else:
                to = (l - 1, m) if l > 0 else (l, m - half)
            pairs.append((l * lon_count + m, to[0] * lon_count + to[1]))
    return pairs


def on_device(field, kernel, cotangent):
    lat_count = lax.axis_size("lat")
    lon_count = lax.axis_size(LON)
    plane = lax.axis_size(PLANE)
    flat = (CH * ROWS, COLS)
    rows_shape = (ROWS, CH, COLS)

    flat_field, flat_cotangent = field.reshape(flat), cotangent.reshape(flat)
    edge, rows = call(
        pack_body,
        [((2 * CH, COLS), bf16), ((2 * TAPS, COLS), bf16)],
        (flat_field, flat_cotangent),
        [
            pltpu.VMEM(flat, f32),
            pltpu.VMEM(flat, bf16),
            pltpu.VMEM(flat, bf16),
            pltpu.SemaphoreType.DMA((2, PIECES)),
        ],
        space=pl.ANY,
        limit=56,
    )
    fr, gr = call(
        turn_body, [(rows_shape, bf16)] * 2, (flat_field, flat_cotangent), [pltpu.VMEM(flat, f32)]
    )
    right = [(i, (i + 1) % lon_count) for i in range(lon_count)]
    left = [(b, a) for a, b in right]
    west = lax.ppermute(edge, LON, right)
    east = lax.ppermute(edge, LON, left)

    ahead, behind = call(
        ring_body, [((4 * CH, COLS), bf16), ((4 * CH, COLS), bf16)], (rows, west, east)
    )
    ring = ring_pairs(lat_count, lon_count)
    ahead = lax.ppermute(ahead, EVERY, ring)
    behind = lax.ppermute(behind, EVERY, [(b, a) for a, b in ring])

    w3 = jnp.transpose(kernel, (0, 2, 1, 3)).reshape(3, CH, TAPS)
    w = jnp.transpose(kernel, (2, 0, 1, 3)).reshape(CH, 3 * TAPS)
    turned = kernel[::-1, ::-1]
    wb3 = jnp.transpose(turned, (0, 3, 1, 2)).reshape(3, CH, TAPS)
    wb = jnp.transpose(turned, (3, 0, 1, 2)).reshape(CH, 3 * TAPS)

    conv_flops = 2 * 9 * CH * CH * ROWS * COLS
    output, delta, dstrip, grad = call(
        forward_body,
        [
            (flat, bf16),
            ((ROWS + 2, CH, COLS), bf16),
            ((CH, 2 * COLS), bf16),
            ((plane, 1, 9 * CH * CH // plane), f32),
        ],
        (fr, gr, edge, west, east, ahead, behind, w, w3, w3.reshape(TAPS, TAPS)),
        [pltpu.VMEM((ROWS + 4, TAPS, COLS), bf16), pltpu.VMEM(flat, f32)],
        2 * conv_flops,
    )

    def spread(parts, count):
        return call(fold_body, [((count,) + parts.shape[1:], f32)], (parts,))[0]

    parts = lax.all_to_all(grad, PLANE, 0, 0)
    parts = lax.all_to_all(spread(parts, lax.axis_size("z")), "z", 0, 0)
    (grad_input,) = call(
        backward_body,
        [(flat, bf16)],
        (delta, dstrip, gr, wb, wb3),
        [pltpu.VMEM((ROWS + 2, TAPS, COLS), bf16), pltpu.VMEM(flat, f32)],
        conv_flops,
    )
    parts = lax.all_to_all(spread(parts, plane), PLANE, 0, 0)
    (grad_kernel,) = call(unpack_body, [((9, CH, CH), f32)], (parts,))
    shape = field.shape
    return (output.reshape(shape), grad_input.reshape(shape), grad_kernel.reshape(kernel.shape))


def solution(mesh):
    lat_count, lon_count = mesh.devices.shape
    split = Mesh(mesh.devices.reshape(lat_count, lon_count // 2, 2), EVERY)
    block = P(None, None, "lat", LON)
    return jax.shard_map(
        on_device,
        mesh=split,
        in_specs=(block, P(), block),
        out_specs=(block, block, P()),
        check_vma=False,
    )
```

```python
import math

import jax
import jax.numpy as jnp
from jax import lax
from jax.experimental import pallas as pl
from jax.experimental.pallas import tpu as pltpu
from jax.sharding import Mesh
from jax.sharding import PartitionSpec as P

gelu_scale = math.sqrt(2.0 / math.pi)
ROWS, COLS, CH = 32, 128, 64
TAPS = 3 * CH
PIECES = 4
f32, bf16 = jnp.float32, jnp.bfloat16
LON = ("z", "side")
LAT = ("low", "x", "core")
EVERY = LAT + LON
STAGES = (("x", "core"), ("low", "side"), ("z",))


def gelu_parts(hidden):
    square = hidden * hidden
    half = 0.5 + 0.5 * jnp.tanh(gelu_scale * hidden * (1.0 + 0.044715 * square))
    steep = gelu_scale * (1.0 + 3.0 * 0.044715 * square)
    return (hidden * half, half + 2.0 * hidden * half * (1.0 - half) * steep)


def roll(x, shift):
    return pltpu.roll(x, shift % x.shape[1], 1)


def lanes(width=COLS):
    return lax.broadcasted_iota(jnp.int32, (CH, width), 1)


def call(body, out_shape, args, scratch=(), flops=0, space=pltpu.VMEM, limit=24):
    outs = [jax.ShapeDtypeStruct(s, d) for s, d in out_shape]
    size = sum(a.size * a.dtype.itemsize for a in list(args) + outs)
    return pl.pallas_call(
        body,
        out_shape=outs,
        in_specs=[pl.BlockSpec(memory_space=space)] * len(args),
        out_specs=[pl.BlockSpec(memory_space=pltpu.VMEM)] * len(outs),
        scratch_shapes=list(scratch),
        cost_estimate=pl.CostEstimate(flops=flops, bytes_accessed=size, transcendentals=0),
        compiler_params=pltpu.CompilerParams(vmem_limit_bytes=int(limit * 2**20)),
    )(*args)


def pack_body(f_hbm, g_hbm, edge_ref, f_ref, g_ref, wide, sems):
    lane = lanes()
    part = CH * ROWS // PIECES
    copies = [
        [
            pltpu.make_async_copy(src.at[pl.ds(i * part, part)], dst.at[pl.ds(i * part, part)], sems.at[at, i])
            for i in range(PIECES)
        ]
        for at, (src, dst) in enumerate(((f_hbm, f_ref), (g_hbm, g_ref)))
    ]
    for copy in copies[0] + copies[1]:
        copy.start()
    for at, src in enumerate((f_ref, g_ref)):
        for i, copy in enumerate(copies[at]):
            copy.wait()
            wide[pl.ds(i * part, part), :] = src[pl.ds(i * part, part), :].astype(f32)
        edge = jnp.zeros((CH, COLS), f32)
        for r in range(ROWS):
            row = wide[pl.ds(r, CH, stride=ROWS), :]
            edge = jnp.where((lane >= 4 * r) & (lane < 4 * r + 4), roll(row, 4 * r + 2), edge)
        edge_ref[pl.ds(at * CH, CH), :] = edge.astype(bf16)


def turn_body(f_ref, g_ref, fr_ref, gr_ref, wide):
    for src, dst in ((f_ref, fr_ref), (g_ref, gr_ref)):
        wide[...] = src[...].astype(f32)
        for r in range(ROWS):
            dst[r] = wide[pl.ds(r, CH, stride=ROWS), :].astype(bf16)


def strip(west_ref, east_ref, part):
    at = pl.ds(part * CH, CH)
    return jnp.where(lanes() % 4 < 2, west_ref[at, :].astype(f32), east_ref[at, :].astype(f32))


def ring_body(fr_ref, gr_ref, west_ref, east_ref, ahead_ref, behind_ref):
    rising = lax.axis_index("z") < lax.axis_size("z") // 2
    lane = lanes()
    s = strip(west_ref, east_ref, 0)
    gs = strip(west_ref, east_ref, 1)
    top = jnp.where(lane < 8, s, roll(gs, 8))
    bottom = jnp.where(lane < 4, roll(s, 4), jnp.where(lane < 8, roll(s, 12), roll(gs, 12)))
    end = ROWS - 1
    pairs = ((fr_ref, 0, end), (fr_ref, 1, end - 1), (gr_ref, 0, end))
    for at, (src, low, high) in enumerate(pairs):
        part = pl.ds(at * CH, CH)
        ahead_ref[part, :] = jnp.where(rising, src[high], src[low])
        behind_ref[part, :] = jnp.where(rising, src[low], src[high])
    corner = pl.ds(TAPS, CH)
    ahead_ref[corner, :] = jnp.where(rising, bottom, top).astype(bf16)
    behind_ref[corner, :] = jnp.where(rising, top, bottom).astype(bf16)


def stack_taps(out_ref, at, own, halo, lane):
    out_ref[at, pl.ds(0, CH), :] = roll(jnp.where(lane == COLS - 1, halo, own), 1).astype(bf16)
    out_ref[at, pl.ds(CH, CH), :] = own.astype(bf16)
    out_ref[at, pl.ds(2 * CH, CH), :] = roll(jnp.where(lane == 0, halo, own), -1).astype(bf16)


def dot(a, b):
    return jnp.dot(a, b, preferred_element_type=f32)


def forward_body(
    fr_ref, gr_ref, edge_ref, west_ref, east_ref, ahead_ref, behind_ref, w_ref, w3_ref, wa_ref,
    out_ref, delta_ref, dstrip_ref, grad_ref, xs,
):
    lat = lax.axis_index(LAT)
    at_top = lat == 0
    at_bottom = lat == lax.axis_size(LAT) - 1
    rising = lax.axis_index("z") < lax.axis_size("z") // 2
    lane = lanes()
    north = jnp.where(rising, ahead_ref[...], behind_ref[...]).astype(f32)
    south = jnp.where(rising, behind_ref[...], ahead_ref[...]).astype(f32)
    n_near, n_far, n_cot, n_corner = [north[i * CH : (i + 1) * CH] for i in range(4)]
    s_near, s_far, s_cot, s_corner = [south[i * CH : (i + 1) * CH] for i in range(4)]

    s = strip(west_ref, east_ref, 0)
    beyond = jnp.where(
        lane < 64, s_corner, jnp.where(lane >= 124, roll(n_corner, 124), roll(n_corner, 116))
    )
    gs = strip(west_ref, east_ref, 1)
    gbeyond = jnp.where(lane < 64, roll(s_corner, 120), roll(n_corner, 116))

    stack_taps(xs, 0, n_far, roll(beyond, -122), lane)
    stack_taps(xs, 1, n_near, roll(beyond, -126), lane)
    for r in range(ROWS):
        stack_taps(xs, r + 2, fr_ref[r].astype(f32), roll(s, -(4 * r + 2)), lane)
    stack_taps(xs, ROWS + 2, s_near, roll(beyond, -2), lane)
    stack_taps(xs, ROWS + 3, s_far, roll(beyond, -6), lane)

    weights = w_ref[...]
    for r in range(0, ROWS, 2):
        window = jnp.concatenate(
            [xs[r + 1 : r + 4].reshape(3 * TAPS, COLS), xs[r + 2 : r + 5].reshape(3 * TAPS, COLS)], 1
        )
        value, slope = gelu_parts(dot(weights, window))
        for k in range(2):
            cut = slice(k * COLS, (k + 1) * COLS)
            out_ref[r + k] = (fr_ref[r + k].astype(f32) + value[:, cut]).astype(bf16)
            delta_ref[r + k + 1] = (gr_ref[r + k].astype(f32) * slope[:, cut]).astype(bf16)

    def outer(inside, near, far, flip, cot, up):
        ends = (far, inside) if up else (inside, far)
        first = jnp.where(flip, xs[ends[1]], xs[ends[0]])
        last = jnp.where(flip, xs[ends[0]], xs[ends[1]])
        total = dot(w3_ref[0], first) + dot(w3_ref[1], xs[near]) + dot(w3_ref[2], last)
        return (cot * gelu_parts(total)[1]).astype(bf16)

    delta_ref[0] = outer(2, 1, 0, at_top, n_cot, True)
    delta_ref[ROWS + 1] = outer(ROWS + 1, ROWS + 2, ROWS + 3, at_bottom, s_cot, False)

    own_beyond = jnp.where(
        lane < 64,
        jnp.where(lane < 4, roll(s_near, 2), roll(s_far, 6)),
        jnp.where(lane >= 124, roll(n_near, 126), roll(n_far, 122)),
    )
    halo = jnp.concatenate([s, beyond], 1)
    own = jnp.concatenate([edge_ref[pl.ds(0, CH), :].astype(f32), own_beyond], 1)
    wide_lane = lanes(2 * COLS)
    kind = wide_lane % 4
    columns = jnp.concatenate(
        [roll(jnp.where(kind == 0, halo, own), 1), halo, roll(jnp.where(kind == 3, halo, own), -1)], 0
    ).astype(bf16)
    y = dot(wa_ref[...], columns)
    y0, y1, y2 = [y[i * CH : (i + 1) * CH] for i in range(3)]
    straight = roll(y0, 4) + y1 + roll(y2, -4)
    turned = roll(y2, 4) + y1 + roll(y0, -4)
    flip = ((wide_lane >= 252) & at_top) | ((wide_lane >= 128) & (wide_lane < 132) & at_bottom)
    slope = gelu_parts(jnp.where(flip, turned, straight))[1]
    dstrip_ref[...] = (jnp.concatenate([gs, gbeyond], 1) * slope).astype(bf16)

    total = None
    group = 8
    for r in range(0, ROWS, group):
        left = jnp.concatenate([delta_ref[r + k + 1] for k in range(group)], 1)
        right = jnp.concatenate([xs[r + k + 1 : r + k + 4].reshape(3 * TAPS, COLS) for k in range(group)], 1)
        term = lax.dot_general(left, right, (((1,), (1,)), ((), ())), preferred_element_type=f32)
        total = term if total is None else total + term
    total = total * grad_scale()
    for p in range(4):
        grad_ref[pl.ds(p * CH, CH), :] = total[:, p * COLS : (p + 1) * COLS]
    tail = total[:, 4 * COLS :]
    grad_ref[pl.ds(4 * CH, CH // 2), :] = jnp.concatenate([tail[: CH // 2], tail[CH // 2 :]], 1)


def restore_body(rows_ref, out_ref, wide):
    for r in range(ROWS):
        wide[pl.ds(r, CH, stride=ROWS), :] = rows_ref[r].astype(f32)
    out_ref[...] = wide[...].astype(bf16)


def grad_scale():
    return float(ROWS * COLS * lax.axis_size(EVERY)) ** (-0.5)


def backward_body(delta_ref, dstrip_ref, gr_ref, wb_ref, wb3_ref, out_ref, xs, wide):
    lat = lax.axis_index(LAT)
    at_top = lat == 0
    at_bottom = lat == lax.axis_size(LAT) - 1
    lane = lanes()
    s = dstrip_ref[:, :COLS].astype(f32)
    beyond = dstrip_ref[:, COLS:].astype(f32)
    stack_taps(xs, 0, delta_ref[0].astype(f32), roll(beyond, -126), lane)
    for r in range(ROWS):
        stack_taps(xs, r + 1, delta_ref[r + 1].astype(f32), roll(s, -(4 * r + 2)), lane)
    stack_taps(xs, ROWS + 1, delta_ref[ROWS + 1].astype(f32), roll(beyond, -2), lane)
    weights = wb_ref[...]

    def put(r, back):
        wide[pl.ds(r, CH, stride=ROWS), :] = gr_ref[r].astype(f32) + back

    upper = jnp.where(at_top, wb3_ref[2], wb3_ref[0])
    lower = jnp.where(at_bottom, wb3_ref[0], wb3_ref[2])
    put(0, dot(upper, xs[0]) + dot(wb3_ref[1], xs[1]) + dot(wb3_ref[2], xs[2]))
    end = ROWS - 1
    put(end, dot(wb3_ref[0], xs[end]) + dot(wb3_ref[1], xs[end + 1]) + dot(lower, xs[end + 2]))
    for r in range(1, ROWS - 1, 2):
        window = jnp.concatenate(
            [xs[r : r + 3].reshape(3 * TAPS, COLS), xs[r + 1 : r + 4].reshape(3 * TAPS, COLS)], 1
        )
        back = dot(weights, window)
        put(r, back[:, :COLS])
        put(r + 1, back[:, COLS:])
    out_ref[...] = wide[...].astype(bf16)


def unpack_body(parts_ref, out_ref):
    for p in range(4):
        block = parts_ref[pl.ds(p * CH, CH), :]
        out_ref[2 * p] = block[:, :CH]
        out_ref[2 * p + 1] = block[:, CH:]
    tail = parts_ref[pl.ds(4 * CH, CH // 2), :]
    out_ref[8, pl.ds(0, CH // 2), :] = tail[:, :CH]
    out_ref[8, pl.ds(CH // 2, CH // 2), :] = tail[:, CH:]


def ring_pairs(lat_count, lon_count):
    half = lon_count // 2
    pairs = []
    for l in range(lat_count):
        for m in range(lon_count):
            if m < half:
                to = (l + 1, m) if l + 1 < lat_count else (l, m + half)
            else:
                to = (l - 1, m) if l > 0 else (l, m - half)
            pairs.append((l * lon_count + m, to[0] * lon_count + to[1]))
    return pairs


def on_device(field, kernel, cotangent):
    lat_count = lax.axis_size(LAT)
    lon_count = lax.axis_size(LON)
    flat = (CH * ROWS, COLS)
    rows_shape = (ROWS, CH, COLS)

    flat_field, flat_cotangent = field.reshape(flat), cotangent.reshape(flat)
    edge, f_near, g_near = call(
        pack_body,
        [((2 * CH, COLS), bf16), (flat, bf16), (flat, bf16)],
        (flat_field, flat_cotangent),
        [
            pltpu.VMEM(flat, f32),
            pltpu.SemaphoreType.DMA((2, PIECES)),
        ],
        space=pl.ANY,
        limit=52.5,
    )
    fr, gr = call(
        turn_body, [(rows_shape, bf16)] * 2, (f_near, g_near), [pltpu.VMEM(flat, f32)]
    )
    right = [(i, (i + 1) % lon_count) for i in range(lon_count)]
    left = [(b, a) for a, b in right]
    west = lax.ppermute(edge, LON, right)
    east = lax.ppermute(edge, LON, left)

    ahead, behind = call(
        ring_body, [((4 * CH, COLS), bf16), ((4 * CH, COLS), bf16)], (fr, gr, west, east)
    )
    ring = ring_pairs(lat_count, lon_count)
    ahead = lax.ppermute(ahead, EVERY, ring)
    behind = lax.ppermute(behind, EVERY, [(b, a) for a, b in ring])

    w3 = jnp.transpose(kernel, (0, 2, 1, 3)).reshape(3, CH, TAPS)
    w = jnp.transpose(kernel, (2, 0, 1, 3)).reshape(CH, 3 * TAPS)
    turned = kernel[::-1, ::-1]
    wb3 = jnp.transpose(turned, (0, 3, 1, 2)).reshape(3, CH, TAPS)
    wb = jnp.transpose(turned, (3, 0, 1, 2)).reshape(CH, 3 * TAPS)

    conv_flops = 2 * 9 * CH * CH * ROWS * COLS
    out_rows, delta, dstrip, grad = call(
        forward_body,
        [
            (rows_shape, bf16),
            ((ROWS + 2, CH, COLS), bf16),
            ((CH, 2 * COLS), bf16),
            ((9 * CH * CH // COLS, COLS), f32),
        ],
        (fr, gr, edge, west, east, ahead, behind, w, w3, w3.reshape(TAPS, TAPS)),
        [pltpu.VMEM((ROWS + 4, TAPS, COLS), bf16)],
        2 * conv_flops,
    )

    (output,) = call(restore_body, [(flat, bf16)], (out_rows,), [pltpu.VMEM(flat, f32)])
    (grad_input,) = call(
        backward_body,
        [(flat, bf16)],
        (delta, dstrip, gr, wb, wb3),
        [pltpu.VMEM((ROWS + 2, TAPS, COLS), bf16), pltpu.VMEM(flat, f32)],
        conv_flops,
    )
    for stage in STAGES:
        grad = lax.optimization_barrier(lax.psum(grad, stage))
    (grad_kernel,) = call(unpack_body, [((9, CH, CH), f32)], (grad,))
    shape = field.shape
    return (output.reshape(shape), grad_input.reshape(shape), grad_kernel.reshape(kernel.shape))


def solution(mesh):
    lat_count, lon_count = mesh.devices.shape
    x = min(4, lat_count // 2)
    split = Mesh(mesh.devices.reshape(lat_count // (2 * x), x, 2, lon_count // 2, 2), EVERY)
    block = P(None, None, LAT, LON)
    return jax.shard_map(
        on_device,
        mesh=split,
        in_specs=(block, P(), block),
        out_specs=(block, block, P()),
        check_vma=False,
    )
```

```python
import math

import jax
import jax.numpy as jnp
from jax import lax
from jax.experimental import pallas as pl
from jax.experimental.pallas import tpu as pltpu
from jax.sharding import Mesh
from jax.sharding import PartitionSpec as P

gelu_scale = math.sqrt(2.0 / math.pi)
ROWS, COLS, CH = 32, 128, 64
TAPS = 3 * CH
PIECES = 4
f32, bf16 = jnp.float32, jnp.bfloat16
LON = ("z", "side")
PLANE = ("lat", "side")
EVERY = ("lat", "z", "side")


def gelu_parts(hidden):
    square = hidden * hidden
    half = 0.5 + 0.5 * jnp.tanh(gelu_scale * hidden * (1.0 + 0.044715 * square))
    steep = gelu_scale * (1.0 + 3.0 * 0.044715 * square)
    return (hidden * half, half + 2.0 * hidden * half * (1.0 - half) * steep)


def roll(x, shift):
    return pltpu.roll(x, shift % x.shape[1], 1)


def lanes(width=COLS):
    return lax.broadcasted_iota(jnp.int32, (CH, width), 1)


def call(body, out_shape, args, scratch=(), flops=0, space=pltpu.VMEM, limit=24):
    outs = [jax.ShapeDtypeStruct(s, d) for s, d in out_shape]
    size = sum(a.size * a.dtype.itemsize for a in list(args) + outs)
    return pl.pallas_call(
        body,
        out_shape=outs,
        in_specs=[pl.BlockSpec(memory_space=space)] * len(args),
        out_specs=[pl.BlockSpec(memory_space=pltpu.VMEM)] * len(outs),
        scratch_shapes=list(scratch),
        cost_estimate=pl.CostEstimate(flops=flops, bytes_accessed=size, transcendentals=0),
        compiler_params=pltpu.CompilerParams(vmem_limit_bytes=int(limit * 2**20)),
    )(*args)


def pack_body(f_hbm, g_hbm, ahead_ref, behind_ref, f_ref, g_ref, wide, sems):
    part = CH * ROWS // PIECES
    copies = [
        [
            pltpu.make_async_copy(src.at[pl.ds(i * part, part)], dst.at[pl.ds(i * part, part)], sems.at[at, i])
            for i in range(PIECES)
        ]
        for at, (src, dst) in enumerate(((f_hbm, f_ref), (g_hbm, g_ref)))
    ]
    for copy in copies[0] + copies[1]:
        copy.start()
    rising = lax.axis_index("z") < lax.axis_size("z") // 2
    end = ROWS - 1
    slots = (((0, 0, end), (1, 1, end - 1)), ((2, 0, end),))
    for at, src in enumerate((f_ref, g_ref)):
        for i, copy in enumerate(copies[at]):
            copy.wait()
            wide[pl.ds(i * part, part), :] = src[pl.ds(i * part, part), :].astype(f32)
        for slot, low, high in slots[at]:
            first = wide[pl.ds(low, CH, stride=ROWS), :]
            last = wide[pl.ds(high, CH, stride=ROWS), :]
            ahead_ref[pl.ds(slot * CH, CH), :] = jnp.where(rising, last, first).astype(bf16)
            behind_ref[pl.ds(slot * CH, CH), :] = jnp.where(rising, first, last).astype(bf16)


def turn_body(f_ref, g_ref, fr_ref, gr_ref, edge_ref, wide):
    lane = lanes()
    for at, (src, dst) in enumerate(((f_ref, fr_ref), (g_ref, gr_ref))):
        wide[...] = src[...].astype(f32)
        edge = jnp.zeros((CH, COLS), f32)
        for r in range(ROWS):
            row = wide[pl.ds(r, CH, stride=ROWS), :]
            edge = jnp.where((lane >= 4 * r) & (lane < 4 * r + 4), roll(row, 4 * r + 2), edge)
            dst[r] = row.astype(bf16)
        edge_ref[pl.ds(at * CH, CH), :] = edge.astype(bf16)


def row_halos(ahead_ref, behind_ref):
    rising = lax.axis_index("z") < lax.axis_size("z") // 2
    north = jnp.where(rising, ahead_ref[...], behind_ref[...]).astype(f32)
    south = jnp.where(rising, behind_ref[...], ahead_ref[...]).astype(f32)
    return [half[i * CH : (i + 1) * CH] for half in (north, south) for i in range(3)]


def edge_body(edge_ref, ahead_ref, behind_ref, out_ref):
    n_near, n_far, n_cot, s_near, s_far, s_cot = row_halos(ahead_ref, behind_ref)
    lane = lanes()
    low = jnp.where(lane < 4, roll(s_near, 2), jnp.where(lane < 8, roll(s_far, 6), roll(s_cot, 10)))
    high = jnp.where(
        lane >= 124, roll(n_near, 126), jnp.where(lane >= 120, roll(n_far, 122), roll(n_cot, 118))
    )
    out_ref[pl.ds(0, 2 * CH), :] = edge_ref[...]
    out_ref[pl.ds(2 * CH, CH), :] = jnp.where(lane < 64, low, high).astype(bf16)


def strip(west_ref, east_ref, part):
    at = pl.ds(part * CH, CH)
    return jnp.where(lanes() % 4 < 2, west_ref[at, :].astype(f32), east_ref[at, :].astype(f32))


def stack_taps(out_ref, at, own, halo, lane):
    out_ref[at, pl.ds(0, CH), :] = roll(jnp.where(lane == COLS - 1, halo, own), 1).astype(bf16)
    out_ref[at, pl.ds(CH, CH), :] = own.astype(bf16)
    out_ref[at, pl.ds(2 * CH, CH), :] = roll(jnp.where(lane == 0, halo, own), -1).astype(bf16)


def dot(a, b):
    return jnp.dot(a, b, preferred_element_type=f32)


def forward_body(
    fr_ref, gr_ref, edge_ref, west_ref, east_ref, ahead_ref, behind_ref, w_ref, w3_ref, wa_ref,
    out_ref, delta_ref, dstrip_ref, grad_ref, xs,
):
    lat = lax.axis_index("lat")
    at_top = lat == 0
    at_bottom = lat == lax.axis_size("lat") - 1
    lane = lanes()
    n_near, n_far, n_cot, s_near, s_far, s_cot = row_halos(ahead_ref, behind_ref)

    s = strip(west_ref, east_ref, 0)
    gs = strip(west_ref, east_ref, 1)
    beyond = strip(west_ref, east_ref, 2)
    gbeyond = jnp.where(lane < 64, roll(beyond, 120), roll(beyond, 8))

    stack_taps(xs, 0, n_far, roll(beyond, -122), lane)
    stack_taps(xs, 1, n_near, roll(beyond, -126), lane)
    for r in range(ROWS):
        stack_taps(xs, r + 2, fr_ref[r].astype(f32), roll(s, -(4 * r + 2)), lane)
    stack_taps(xs, ROWS + 2, s_near, roll(beyond, -2), lane)
    stack_taps(xs, ROWS + 3, s_far, roll(beyond, -6), lane)

    weights = w_ref[...]
    for r in range(0, ROWS, 2):
        window = jnp.concatenate(
            [xs[r + 1 : r + 4].reshape(3 * TAPS, COLS), xs[r + 2 : r + 5].reshape(3 * TAPS, COLS)], 1
        )
        value, slope = gelu_parts(dot(weights, window))
        for k in range(2):
            cut = slice(k * COLS, (k + 1) * COLS)
            out_ref[r + k] = (fr_ref[r + k].astype(f32) + value[:, cut]).astype(bf16)
            delta_ref[r + k + 1] = (gr_ref[r + k].astype(f32) * slope[:, cut]).astype(bf16)

    def outer(inside, near, far, flip, cot, up):
        ends = (far, inside) if up else (inside, far)
        first = jnp.where(flip, xs[ends[1]], xs[ends[0]])
        last = jnp.where(flip, xs[ends[0]], xs[ends[1]])
        total = dot(w3_ref[0], first) + dot(w3_ref[1], xs[near]) + dot(w3_ref[2], last)
        return (cot * gelu_parts(total)[1]).astype(bf16)

    delta_ref[0] = outer(2, 1, 0, at_top, n_cot, True)
    delta_ref[ROWS + 1] = outer(ROWS + 1, ROWS + 2, ROWS + 3, at_bottom, s_cot, False)

    halo = jnp.concatenate([s, beyond], 1)
    own = jnp.concatenate(
        [edge_ref[pl.ds(0, CH), :].astype(f32), edge_ref[pl.ds(2 * CH, CH), :].astype(f32)], 1
    )
    wide_lane = lanes(2 * COLS)
    kind = wide_lane % 4
    columns = jnp.concatenate(
        [roll(jnp.where(kind == 0, halo, own), 1), halo, roll(jnp.where(kind == 3, halo, own), -1)], 0
    ).astype(bf16)
    y = dot(wa_ref[...], columns)
    y0, y1, y2 = [y[i * CH : (i + 1) * CH] for i in range(3)]
    straight = roll(y0, 4) + y1 + roll(y2, -4)
    turned = roll(y2, 4) + y1 + roll(y0, -4)
    flip = ((wide_lane >= 252) & at_top) | ((wide_lane >= 128) & (wide_lane < 132) & at_bottom)
    slope = gelu_parts(jnp.where(flip, turned, straight))[1]
    dstrip_ref[...] = (jnp.concatenate([gs, gbeyond], 1) * slope).astype(bf16)

    total = None
    group = 8
    for r in range(0, ROWS, group):
        left = jnp.concatenate([delta_ref[r + k + 1] for k in range(group)], 1)
        right = jnp.concatenate([xs[r + k + 1 : r + k + 4].reshape(3 * TAPS, COLS) for k in range(group)], 1)
        term = lax.dot_general(left, right, (((1,), (1,)), ((), ())), preferred_element_type=f32)
        total = term if total is None else total + term
    total = total * grad_scale()
    pieces = [total[:, p * COLS : (p + 1) * COLS] for p in range(4)] + [total[:, 4 * COLS :]]
    count = grad_ref.shape[0]
    for at, piece in enumerate(pieces):
        for j in range(CH // count):
            width = piece.shape[1]
            start = at * COLS * CH // count + j * width
            grad_ref[:, 0, pl.ds(start, width)] = piece[j * count : (j + 1) * count]


def restore_body(rows_ref, out_ref, wide):
    for r in range(ROWS):
        wide[pl.ds(r, CH, stride=ROWS), :] = rows_ref[r].astype(f32)
    out_ref[...] = wide[...].astype(bf16)


def grad_scale():
    return float(ROWS * COLS * lax.axis_size(EVERY)) ** (-0.5)


def backward_body(after_ref, delta_ref, dstrip_ref, gr_ref, wb_ref, wb3_ref, out_ref, xs, wide):
    lat = lax.axis_index("lat")
    at_top = lat == 0
    at_bottom = lat == lax.axis_size("lat") - 1
    lane = lanes()
    s = dstrip_ref[:, :COLS].astype(f32)
    beyond = dstrip_ref[:, COLS:].astype(f32)
    stack_taps(xs, 0, delta_ref[0].astype(f32), roll(beyond, -126), lane)
    for r in range(ROWS):
        stack_taps(xs, r + 1, delta_ref[r + 1].astype(f32), roll(s, -(4 * r + 2)), lane)
    stack_taps(xs, ROWS + 1, delta_ref[ROWS + 1].astype(f32), roll(beyond, -2), lane)
    weights = wb_ref[...]

    def put(r, back):
        wide[pl.ds(r, CH, stride=ROWS), :] = gr_ref[r].astype(f32) + back

    upper = jnp.where(at_top, wb3_ref[2], wb3_ref[0])
    lower = jnp.where(at_bottom, wb3_ref[0], wb3_ref[2])
    put(0, dot(upper, xs[0]) + dot(wb3_ref[1], xs[1]) + dot(wb3_ref[2], xs[2]))
    end = ROWS - 1
    put(end, dot(wb3_ref[0], xs[end]) + dot(wb3_ref[1], xs[end + 1]) + dot(lower, xs[end + 2]))
    for r in range(1, ROWS - 1, 2):
        window = jnp.concatenate(
            [xs[r : r + 3].reshape(3 * TAPS, COLS), xs[r + 1 : r + 4].reshape(3 * TAPS, COLS)], 1
        )
        back = dot(weights, window)
        put(r, back[:, :COLS])
        put(r + 1, back[:, COLS:])
    out_ref[...] = wide[...].astype(bf16)


def fold_body(parts_ref, out_ref):
    total = jnp.sum(parts_ref[...], 0)
    for i in range(out_ref.shape[0]):
        out_ref[i] = total


def unpack_body(parts_ref, out_ref):
    count = parts_ref.shape[0]
    for tap in range(9):
        at = tap // 2
        width = min(COLS, 9 * CH - at * COLS)
        for j in range(CH // count):
            start = at * COLS * CH // count + j * width + (tap % 2) * CH
            out_ref[tap, pl.ds(j * count, count), :] = parts_ref[:, 0, pl.ds(start, CH)]


def ring_pairs(lat_count, lon_count):
    half = lon_count // 2
    pairs = []
    for l in range(lat_count):
        for m in range(lon_count):
            if m < half:
                to = (l + 1, m) if l + 1 < lat_count else (l, m + half)
            else:
                to = (l - 1, m) if l > 0 else (l, m - half)
            pairs.append((l * lon_count + m, to[0] * lon_count + to[1]))
    return pairs


def on_device(field, kernel, cotangent):
    lat_count = lax.axis_size("lat")
    lon_count = lax.axis_size(LON)
    plane = lax.axis_size(PLANE)
    flat = (CH * ROWS, COLS)
    rows_shape = (ROWS, CH, COLS)

    flat_field, flat_cotangent = field.reshape(flat), cotangent.reshape(flat)
    ahead, behind, f_near, g_near = call(
        pack_body,
        [((TAPS, COLS), bf16), ((TAPS, COLS), bf16), (flat, bf16), (flat, bf16)],
        (flat_field, flat_cotangent),
        [pltpu.VMEM(flat, f32), pltpu.SemaphoreType.DMA((2, PIECES))],
        space=pl.ANY,
        limit=52.5,
    )
    ring = ring_pairs(lat_count, lon_count)
    ahead = lax.ppermute(ahead, EVERY, ring)
    behind = lax.ppermute(behind, EVERY, [(b, a) for a, b in ring])
    fr, gr, edge = call(
        turn_body,
        [(rows_shape, bf16), (rows_shape, bf16), ((2 * CH, COLS), bf16)],
        (f_near, g_near),
        [pltpu.VMEM(flat, f32)],
    )

    (edge,) = call(edge_body, [((TAPS, COLS), bf16)], (edge, ahead, behind))
    right = [(i, (i + 1) % lon_count) for i in range(lon_count)]
    west = lax.ppermute(edge, LON, right)
    east = lax.ppermute(edge, LON, [(b, a) for a, b in right])

    w3 = jnp.transpose(kernel, (0, 2, 1, 3)).reshape(3, CH, TAPS)
    w = jnp.transpose(kernel, (2, 0, 1, 3)).reshape(CH, 3 * TAPS)
    turned = kernel[::-1, ::-1]
    wb3 = jnp.transpose(turned, (0, 3, 1, 2)).reshape(3, CH, TAPS)
    wb = jnp.transpose(turned, (3, 0, 1, 2)).reshape(CH, 3 * TAPS)

    conv_flops = 2 * 9 * CH * CH * ROWS * COLS
    out_rows, delta, dstrip, grad = call(
        forward_body,
        [
            (rows_shape, bf16),
            ((ROWS + 2, CH, COLS), bf16),
            ((CH, 2 * COLS), bf16),
            ((plane, 1, 9 * CH * CH // plane), f32),
        ],
        (fr, gr, edge, west, east, ahead, behind, w, w3, w3.reshape(TAPS, TAPS)),
        [pltpu.VMEM((ROWS + 4, TAPS, COLS), bf16)],
        2 * conv_flops,
    )

    def spread(parts, count):
        return call(fold_body, [((count,) + parts.shape[1:], f32)], (parts,))[0]

    parts = lax.all_to_all(grad, PLANE, 0, 0)
    (output,) = call(restore_body, [(flat, bf16)], (out_rows,), [pltpu.VMEM(flat, f32)])
    parts = lax.all_to_all(spread(parts, lax.axis_size("z")), "z", 0, 0)
    (grad_input,) = call(
        backward_body,
        [(flat, bf16)],
        (parts, delta, dstrip, gr, wb, wb3),
        [pltpu.VMEM((ROWS + 2, TAPS, COLS), bf16), pltpu.VMEM(flat, f32)],
        conv_flops,
    )
    parts = lax.all_to_all(spread(parts, plane), PLANE, 0, 0)
    (grad_kernel,) = call(unpack_body, [((9, CH, CH), f32)], (parts,))
    shape = field.shape
    return (output.reshape(shape), grad_input.reshape(shape), grad_kernel.reshape(kernel.shape))


def solution(mesh):
    lat_count, lon_count = mesh.devices.shape
    split = Mesh(mesh.devices.reshape(lat_count, lon_count // 2, 2), EVERY)
    block = P(None, None, "lat", LON)
    return jax.shard_map(
        on_device,
        mesh=split,
        in_specs=(block, P(), block),
        out_specs=(block, block, P()),
        check_vma=False,
    )
```

```python
import math

import jax
import jax.numpy as jnp
from jax import lax
from jax.experimental import pallas as pl
from jax.experimental.pallas import tpu as pltpu
from jax.sharding import Mesh
from jax.sharding import PartitionSpec as P

gelu_scale = math.sqrt(2.0 / math.pi)
ROWS, COLS, CH = 32, 128, 64
TAPS = 3 * CH
PIECES = 4
f32, bf16 = jnp.float32, jnp.bfloat16
LON = ("z", "side")
PLANE = ("lat", "side")
EVERY = ("lat", "z", "side")


def gelu_parts(hidden):
    square = hidden * hidden
    half = 0.5 + 0.5 * jnp.tanh(gelu_scale * hidden * (1.0 + 0.044715 * square))
    steep = gelu_scale * (1.0 + 3.0 * 0.044715 * square)
    return (hidden * half, half + 2.0 * hidden * half * (1.0 - half) * steep)


def roll(x, shift):
    return pltpu.roll(x, shift % x.shape[1], 1)


def lanes(width=COLS):
    return lax.broadcasted_iota(jnp.int32, (CH, width), 1)


def call(body, out_shape, args, scratch=(), flops=0, space=pltpu.VMEM, limit=24):
    outs = [jax.ShapeDtypeStruct(s, d) for s, d in out_shape]
    size = sum(a.size * a.dtype.itemsize for a in list(args) + outs)
    return pl.pallas_call(
        body,
        out_shape=outs,
        in_specs=[pl.BlockSpec(memory_space=space)] * len(args),
        out_specs=[pl.BlockSpec(memory_space=pltpu.VMEM)] * len(outs),
        scratch_shapes=list(scratch),
        cost_estimate=pl.CostEstimate(flops=flops, bytes_accessed=size, transcendentals=0),
        compiler_params=pltpu.CompilerParams(vmem_limit_bytes=int(limit * 2**20)),
    )(*args)


def pack_body(f_hbm, g_hbm, outer_ref, inner_ref, f_ref, g_ref, wide, sems):
    part = CH * ROWS // PIECES
    copies = [
        [
            pltpu.make_async_copy(src.at[pl.ds(i * part, part)], dst.at[pl.ds(i * part, part)], sems.at[at, i])
            for i in range(PIECES)
        ]
        for at, (src, dst) in enumerate(((f_hbm, f_ref), (g_hbm, g_ref)))
    ]
    for copy in copies[0] + copies[1]:
        copy.start()
    even = lax.axis_index("lat") % 2 == 0
    end = ROWS - 1
    slots = (((0, 0, end), (1, 1, end - 1)), ((2, 0, end),))
    for at, src in enumerate((f_ref, g_ref)):
        for i, copy in enumerate(copies[at]):
            copy.wait()
            wide[pl.ds(i * part, part), :] = src[pl.ds(i * part, part), :].astype(f32)
        for slot, low, high in slots[at]:
            first = wide[pl.ds(low, CH, stride=ROWS), :]
            last = wide[pl.ds(high, CH, stride=ROWS), :]
            outer_ref[pl.ds(slot * CH, CH), :] = jnp.where(even, first, last).astype(bf16)
            inner_ref[pl.ds(slot * CH, CH), :] = jnp.where(even, last, first).astype(bf16)


def turn_body(f_ref, g_ref, fr_ref, gr_ref, edge_ref, wide):
    lane = lanes()
    for at, (src, dst) in enumerate(((f_ref, fr_ref), (g_ref, gr_ref))):
        wide[...] = src[...].astype(f32)
        edge = jnp.zeros((CH, COLS), f32)
        for r in range(ROWS):
            row = wide[pl.ds(r, CH, stride=ROWS), :]
            edge = jnp.where((lane >= 4 * r) & (lane < 4 * r + 4), roll(row, 4 * r + 2), edge)
            dst[r] = row.astype(bf16)
        edge_ref[pl.ds(at * CH, CH), :] = edge.astype(bf16)


def row_halos(outer_ref, inner_ref):
    even = lax.axis_index("lat") % 2 == 0
    north = jnp.where(even, outer_ref[...], inner_ref[...]).astype(f32)
    south = jnp.where(even, inner_ref[...], outer_ref[...]).astype(f32)
    return [half[i * CH : (i + 1) * CH] for half in (north, south) for i in range(3)]


def edge_body(edge_ref, outer_ref, inner_ref, out_ref):
    n_near, n_far, n_cot, s_near, s_far, s_cot = row_halos(outer_ref, inner_ref)
    lane = lanes()
    low = jnp.where(lane < 4, roll(s_near, 2), jnp.where(lane < 8, roll(s_far, 6), roll(s_cot, 10)))
    high = jnp.where(
        lane >= 124, roll(n_near, 126), jnp.where(lane >= 120, roll(n_far, 122), roll(n_cot, 118))
    )
    out_ref[pl.ds(0, 2 * CH), :] = edge_ref[...]
    out_ref[pl.ds(2 * CH, CH), :] = jnp.where(lane < 64, low, high).astype(bf16)


def strip(near_ref, far_ref, part):
    at = pl.ds(part * CH, CH)
    near = near_ref[at, :].astype(f32)
    far = far_ref[at, :].astype(f32)
    even = lax.axis_index("side") == 0
    return jnp.where(lanes() % 4 < 2, jnp.where(even, far, near), jnp.where(even, near, far))


def stack_taps(out_ref, at, own, halo, lane):
    out_ref[at, pl.ds(0, CH), :] = roll(jnp.where(lane == COLS - 1, halo, own), 1).astype(bf16)
    out_ref[at, pl.ds(CH, CH), :] = own.astype(bf16)
    out_ref[at, pl.ds(2 * CH, CH), :] = roll(jnp.where(lane == 0, halo, own), -1).astype(bf16)


def dot(a, b):
    return jnp.dot(a, b, preferred_element_type=f32)


def forward_body(
    fr_ref, gr_ref, edge_ref, near_ref, far_ref, outer_ref, inner_ref, w_ref, w3_ref, wa_ref,
    out_ref, delta_ref, dstrip_ref, grad_ref, xs,
):
    lat = lax.axis_index("lat")
    at_top = lat == 0
    at_bottom = lat == lax.axis_size("lat") - 1
    lane = lanes()
    n_near, n_far, n_cot, s_near, s_far, s_cot = row_halos(outer_ref, inner_ref)

    s = strip(near_ref, far_ref, 0)
    gs = strip(near_ref, far_ref, 1)
    beyond = strip(near_ref, far_ref, 2)
    gbeyond = jnp.where(lane < 64, roll(beyond, 120), roll(beyond, 8))

    stack_taps(xs, 0, n_far, roll(beyond, -122), lane)
    stack_taps(xs, 1, n_near, roll(beyond, -126), lane)
    for r in range(ROWS):
        stack_taps(xs, r + 2, fr_ref[r].astype(f32), roll(s, -(4 * r + 2)), lane)
    stack_taps(xs, ROWS + 2, s_near, roll(beyond, -2), lane)
    stack_taps(xs, ROWS + 3, s_far, roll(beyond, -6), lane)

    weights = w_ref[...]
    for r in range(0, ROWS, 2):
        window = jnp.concatenate(
            [xs[r + 1 : r + 4].reshape(3 * TAPS, COLS), xs[r + 2 : r + 5].reshape(3 * TAPS, COLS)], 1
        )
        value, slope = gelu_parts(dot(weights, window))
        for k in range(2):
            cut = slice(k * COLS, (k + 1) * COLS)
            out_ref[r + k] = (fr_ref[r + k].astype(f32) + value[:, cut]).astype(bf16)
            delta_ref[r + k + 1] = (gr_ref[r + k].astype(f32) * slope[:, cut]).astype(bf16)

    def outer(inside, near, far, flip, cot, up):
        ends = (far, inside) if up else (inside, far)
        first = jnp.where(flip, xs[ends[1]], xs[ends[0]])
        last = jnp.where(flip, xs[ends[0]], xs[ends[1]])
        total = dot(w3_ref[0], first) + dot(w3_ref[1], xs[near]) + dot(w3_ref[2], last)
        return (cot * gelu_parts(total)[1]).astype(bf16)

    delta_ref[0] = outer(2, 1, 0, at_top, n_cot, True)
    delta_ref[ROWS + 1] = outer(ROWS + 1, ROWS + 2, ROWS + 3, at_bottom, s_cot, False)

    halo = jnp.concatenate([s, beyond], 1)
    own = jnp.concatenate(
        [edge_ref[pl.ds(0, CH), :].astype(f32), edge_ref[pl.ds(2 * CH, CH), :].astype(f32)], 1
    )
    wide_lane = lanes(2 * COLS)
    kind = wide_lane % 4
    columns = jnp.concatenate(
        [roll(jnp.where(kind == 0, halo, own), 1), halo, roll(jnp.where(kind == 3, halo, own), -1)], 0
    ).astype(bf16)
    y = dot(wa_ref[...], columns)
    y0, y1, y2 = [y[i * CH : (i + 1) * CH] for i in range(3)]
    straight = roll(y0, 4) + y1 + roll(y2, -4)
    turned = roll(y2, 4) + y1 + roll(y0, -4)
    flip = ((wide_lane >= 252) & at_top) | ((wide_lane >= 128) & (wide_lane < 132) & at_bottom)
    slope = gelu_parts(jnp.where(flip, turned, straight))[1]
    dstrip_ref[...] = (jnp.concatenate([gs, gbeyond], 1) * slope).astype(bf16)

    total = None
    group = 8
    for r in range(0, ROWS, group):
        left = jnp.concatenate([delta_ref[r + k + 1] for k in range(group)], 1)
        right = jnp.concatenate([xs[r + k + 1 : r + k + 4].reshape(3 * TAPS, COLS) for k in range(group)], 1)
        term = lax.dot_general(left, right, (((1,), (1,)), ((), ())), preferred_element_type=f32)
        total = term if total is None else total + term
    total = total * grad_scale()
    pieces = [total[:, p * COLS : (p + 1) * COLS] for p in range(4)] + [total[:, 4 * COLS :]]
    count = grad_ref.shape[0]
    for at, piece in enumerate(pieces):
        for j in range(CH // count):
            width = piece.shape[1]
            start = at * COLS * CH // count + j * width
            grad_ref[:, 0, pl.ds(start, width)] = piece[j * count : (j + 1) * count]


def restore_body(rows_ref, out_ref, wide):
    for r in range(ROWS):
        wide[pl.ds(r, CH, stride=ROWS), :] = rows_ref[r].astype(f32)
    out_ref[...] = wide[...].astype(bf16)


def grad_scale():
    return float(ROWS * COLS * lax.axis_size(EVERY)) ** (-0.5)


def backward_body(after_ref, delta_ref, dstrip_ref, gr_ref, wb_ref, wb3_ref, out_ref, xs, wide):
    lat = lax.axis_index("lat")
    at_top = lat == 0
    at_bottom = lat == lax.axis_size("lat") - 1
    lane = lanes()
    s = dstrip_ref[:, :COLS].astype(f32)
    beyond = dstrip_ref[:, COLS:].astype(f32)
    stack_taps(xs, 0, delta_ref[0].astype(f32), roll(beyond, -126), lane)
    for r in range(ROWS):
        stack_taps(xs, r + 1, delta_ref[r + 1].astype(f32), roll(s, -(4 * r + 2)), lane)
    stack_taps(xs, ROWS + 1, delta_ref[ROWS + 1].astype(f32), roll(beyond, -2), lane)
    weights = wb_ref[...]

    def put(r, back):
        wide[pl.ds(r, CH, stride=ROWS), :] = gr_ref[r].astype(f32) + back

    upper = jnp.where(at_top, wb3_ref[2], wb3_ref[0])
    lower = jnp.where(at_bottom, wb3_ref[0], wb3_ref[2])
    put(0, dot(upper, xs[0]) + dot(wb3_ref[1], xs[1]) + dot(wb3_ref[2], xs[2]))
    end = ROWS - 1
    put(end, dot(wb3_ref[0], xs[end]) + dot(wb3_ref[1], xs[end + 1]) + dot(lower, xs[end + 2]))
    for r in range(1, ROWS - 1, 2):
        window = jnp.concatenate(
            [xs[r : r + 3].reshape(3 * TAPS, COLS), xs[r + 1 : r + 4].reshape(3 * TAPS, COLS)], 1
        )
        back = dot(weights, window)
        put(r, back[:, :COLS])
        put(r + 1, back[:, COLS:])
    out_ref[...] = wide[...].astype(bf16)


def fold_body(parts_ref, out_ref):
    total = jnp.sum(parts_ref[...], 0)
    for i in range(out_ref.shape[0]):
        out_ref[i] = total


def unpack_body(parts_ref, out_ref):
    count = parts_ref.shape[0]
    for tap in range(9):
        at = tap // 2
        width = min(COLS, 9 * CH - at * COLS)
        for j in range(CH // count):
            start = at * COLS * CH // count + j * width + (tap % 2) * CH
            out_ref[tap, pl.ds(j * count, count), :] = parts_ref[:, 0, pl.ds(start, CH)]


def outer_pairs(lat_count, lon_count):
    half = lon_count // 2
    pairs = []
    for l in range(lat_count):
        for m in range(lon_count):
            to = l - 1 if l % 2 == 0 else l + 1
            if 0 <= to < lat_count:
                pairs.append((l * lon_count + m, to * lon_count + m))
            else:
                pairs.append((l * lon_count + m, l * lon_count + (m + half) % lon_count))
    return pairs


def on_device(field, kernel, cotangent):
    lat_count = lax.axis_size("lat")
    lon_count = lax.axis_size(LON)
    plane = lax.axis_size(PLANE)
    flat = (CH * ROWS, COLS)
    rows_shape = (ROWS, CH, COLS)

    flat_field, flat_cotangent = field.reshape(flat), cotangent.reshape(flat)
    outer, inner, f_near, g_near = call(
        pack_body,
        [((TAPS, COLS), bf16), ((TAPS, COLS), bf16), (flat, bf16), (flat, bf16)],
        (flat_field, flat_cotangent),
        [pltpu.VMEM(flat, f32), pltpu.SemaphoreType.DMA((2, PIECES))],
        space=pl.ANY,
        limit=52.5,
    )
    outer = lax.ppermute(outer, EVERY, outer_pairs(lat_count, lon_count))
    inner = lax.ppermute(inner, "lat", [(i, i ^ 1) for i in range(lat_count)])
    fr, gr, edge = call(
        turn_body,
        [(rows_shape, bf16), (rows_shape, bf16), ((2 * CH, COLS), bf16)],
        (f_near, g_near),
        [pltpu.VMEM(flat, f32)],
    )

    (edge,) = call(edge_body, [((TAPS, COLS), bf16)], (edge, outer, inner))
    swaps = [(i, (i + 1 if i % 2 else i - 1) % lon_count) for i in range(lon_count)]
    far = lax.ppermute(edge, LON, swaps)
    near = lax.ppermute(edge, "side", [(0, 1), (1, 0)])

    w3 = jnp.transpose(kernel, (0, 2, 1, 3)).reshape(3, CH, TAPS)
    w = jnp.transpose(kernel, (2, 0, 1, 3)).reshape(CH, 3 * TAPS)
    turned = kernel[::-1, ::-1]
    wb3 = jnp.transpose(turned, (0, 3, 1, 2)).reshape(3, CH, TAPS)
    wb = jnp.transpose(turned, (3, 0, 1, 2)).reshape(CH, 3 * TAPS)

    conv_flops = 2 * 9 * CH * CH * ROWS * COLS
    out_rows, delta, dstrip, grad = call(
        forward_body,
        [
            (rows_shape, bf16),
            ((ROWS + 2, CH, COLS), bf16),
            ((CH, 2 * COLS), bf16),
            ((plane, 1, 9 * CH * CH // plane), f32),
        ],
        (fr, gr, edge, near, far, outer, inner, w, w3, w3.reshape(TAPS, TAPS)),
        [pltpu.VMEM((ROWS + 4, TAPS, COLS), bf16)],
        2 * conv_flops,
    )

    def spread(parts, count):
        return call(fold_body, [((count,) + parts.shape[1:], f32)], (parts,))[0]

    parts = lax.all_to_all(grad, PLANE, 0, 0)
    (output,) = call(restore_body, [(flat, bf16)], (out_rows,), [pltpu.VMEM(flat, f32)])
    parts = lax.all_to_all(spread(parts, lax.axis_size("z")), "z", 0, 0)
    (grad_input,) = call(
        backward_body,
        [(flat, bf16)],
        (parts, delta, dstrip, gr, wb, wb3),
        [pltpu.VMEM((ROWS + 2, TAPS, COLS), bf16), pltpu.VMEM(flat, f32)],
        conv_flops,
    )
    parts = lax.all_to_all(spread(parts, plane), PLANE, 0, 0)
    (grad_kernel,) = call(unpack_body, [((9, CH, CH), f32)], (parts,))
    shape = field.shape
    return (output.reshape(shape), grad_input.reshape(shape), grad_kernel.reshape(kernel.shape))


def solution(mesh):
    lat_count, lon_count = mesh.devices.shape
    split = Mesh(mesh.devices.reshape(lat_count, lon_count // 2, 2), EVERY)
    block = P(None, None, "lat", LON)
    return jax.shard_map(
        on_device,
        mesh=split,
        in_specs=(block, P(), block),
        out_specs=(block, block, P()),
        check_vma=False,
    )
```

```python
import math

import jax
import jax.numpy as jnp
from jax import lax
from jax.experimental import pallas as pl
from jax.experimental.pallas import tpu as pltpu
from jax.sharding import Mesh
from jax.sharding import PartitionSpec as P

gelu_scale = math.sqrt(2.0 / math.pi)
ROWS, COLS, CH = 32, 128, 64
TAPS = 3 * CH
PIECES = 4
f32, bf16 = jnp.float32, jnp.bfloat16
LON = ("z", "side")
LAT = ("low", "x", "core")
EVERY = LAT + LON
NEAR = ("x", "core")
ACROSS = ("low", "side")


def gelu_parts(hidden):
    square = hidden * hidden
    half = 0.5 + 0.5 * jnp.tanh(gelu_scale * hidden * (1.0 + 0.044715 * square))
    steep = gelu_scale * (1.0 + 3.0 * 0.044715 * square)
    return (hidden * half, half + 2.0 * hidden * half * (1.0 - half) * steep)


def roll(x, shift):
    return pltpu.roll(x, shift % x.shape[1], 1)


def lanes(width=COLS):
    return lax.broadcasted_iota(jnp.int32, (CH, width), 1)


def call(body, out_shape, args, scratch=(), flops=0, space=pltpu.VMEM, limit=24):
    outs = [jax.ShapeDtypeStruct(s, d) for s, d in out_shape]
    size = sum(a.size * a.dtype.itemsize for a in list(args) + outs)
    return pl.pallas_call(
        body,
        out_shape=outs,
        in_specs=[pl.BlockSpec(memory_space=space)] * len(args),
        out_specs=[pl.BlockSpec(memory_space=pltpu.VMEM)] * len(outs),
        scratch_shapes=list(scratch),
        cost_estimate=pl.CostEstimate(flops=flops, bytes_accessed=size, transcendentals=0),
        compiler_params=pltpu.CompilerParams(vmem_limit_bytes=int(limit * 2**20)),
    )(*args)


def pack_body(f_hbm, g_hbm, outer_ref, inner_ref, f_ref, g_ref, wide, sems):
    part = CH * ROWS // PIECES
    copies = [
        [
            pltpu.make_async_copy(src.at[pl.ds(i * part, part)], dst.at[pl.ds(i * part, part)], sems.at[at, i])
            for i in range(PIECES)
        ]
        for at, (src, dst) in enumerate(((f_hbm, f_ref), (g_hbm, g_ref)))
    ]
    for copy in copies[0] + copies[1]:
        copy.start()
    even = lax.axis_index("core") == 0
    end = ROWS - 1
    slots = (((0, 0, end), (1, 1, end - 1)), ((2, 0, end),))
    for at, src in enumerate((f_ref, g_ref)):
        for i, copy in enumerate(copies[at]):
            copy.wait()
            wide[pl.ds(i * part, part), :] = src[pl.ds(i * part, part), :].astype(f32)
        for slot, low, high in slots[at]:
            first = wide[pl.ds(low, CH, stride=ROWS), :]
            last = wide[pl.ds(high, CH, stride=ROWS), :]
            outer_ref[pl.ds(slot * CH, CH), :] = jnp.where(even, first, last).astype(bf16)
            inner_ref[pl.ds(slot * CH, CH), :] = jnp.where(even, last, first).astype(bf16)


def turn_body(f_ref, g_ref, fr_ref, gr_ref, edge_ref, wide):
    lane = lanes()
    for at, (src, dst) in enumerate(((f_ref, fr_ref), (g_ref, gr_ref))):
        wide[...] = src[...].astype(f32)
        edge = jnp.zeros((CH, COLS), f32)
        for r in range(ROWS):
            row = wide[pl.ds(r, CH, stride=ROWS), :]
            edge = jnp.where((lane >= 4 * r) & (lane < 4 * r + 4), roll(row, 4 * r + 2), edge)
            dst[r] = row.astype(bf16)
        edge_ref[pl.ds(at * CH, CH), :] = edge.astype(bf16)


def row_halos(outer_ref, inner_ref):
    even = lax.axis_index("core") == 0
    north = jnp.where(even, outer_ref[...], inner_ref[...]).astype(f32)
    south = jnp.where(even, inner_ref[...], outer_ref[...]).astype(f32)
    return [half[i * CH : (i + 1) * CH] for half in (north, south) for i in range(3)]


def edge_body(edge_ref, outer_ref, inner_ref, out_ref):
    n_near, n_far, n_cot, s_near, s_far, s_cot = row_halos(outer_ref, inner_ref)
    lane = lanes()
    low = jnp.where(lane < 4, roll(s_near, 2), jnp.where(lane < 8, roll(s_far, 6), roll(s_cot, 10)))
    high = jnp.where(
        lane >= 124, roll(n_near, 126), jnp.where(lane >= 120, roll(n_far, 122), roll(n_cot, 118))
    )
    out_ref[pl.ds(0, 2 * CH), :] = edge_ref[...]
    out_ref[pl.ds(2 * CH, CH), :] = jnp.where(lane < 64, low, high).astype(bf16)


def strip(near_ref, far_ref, part):
    at = pl.ds(part * CH, CH)
    near = near_ref[at, :].astype(f32)
    far = far_ref[at, :].astype(f32)
    even = lax.axis_index("side") == 0
    return jnp.where(lanes() % 4 < 2, jnp.where(even, far, near), jnp.where(even, near, far))


def stack_taps(out_ref, at, own, halo, lane):
    out_ref[at, pl.ds(0, CH), :] = roll(jnp.where(lane == COLS - 1, halo, own), 1).astype(bf16)
    out_ref[at, pl.ds(CH, CH), :] = own.astype(bf16)
    out_ref[at, pl.ds(2 * CH, CH), :] = roll(jnp.where(lane == 0, halo, own), -1).astype(bf16)


def dot(a, b):
    return jnp.dot(a, b, preferred_element_type=f32)


def forward_body(
    fr_ref, gr_ref, edge_ref, far_ref, near_ref, outer_ref, inner_ref, w_ref, w3_ref, wa_ref,
    out_ref, delta_ref, dstrip_ref, grad_ref, xs,
):
    lat = lax.axis_index(LAT)
    at_top = lat == 0
    at_bottom = lat == lax.axis_size(LAT) - 1
    lane = lanes()
    n_near, n_far, n_cot, s_near, s_far, s_cot = row_halos(outer_ref, inner_ref)

    s = strip(near_ref, far_ref, 0)
    gs = strip(near_ref, far_ref, 1)
    beyond = strip(near_ref, far_ref, 2)
    gbeyond = jnp.where(lane < 64, roll(beyond, 120), roll(beyond, 8))

    stack_taps(xs, 0, n_far, roll(beyond, -122), lane)
    stack_taps(xs, 1, n_near, roll(beyond, -126), lane)
    for r in range(ROWS):
        stack_taps(xs, r + 2, fr_ref[r].astype(f32), roll(s, -(4 * r + 2)), lane)
    stack_taps(xs, ROWS + 2, s_near, roll(beyond, -2), lane)
    stack_taps(xs, ROWS + 3, s_far, roll(beyond, -6), lane)

    weights = w_ref[...]
    for r in range(0, ROWS, 2):
        window = jnp.concatenate(
            [xs[r + 1 : r + 4].reshape(3 * TAPS, COLS), xs[r + 2 : r + 5].reshape(3 * TAPS, COLS)], 1
        )
        value, slope = gelu_parts(dot(weights, window))
        for k in range(2):
            cut = slice(k * COLS, (k + 1) * COLS)
            out_ref[r + k] = (fr_ref[r + k].astype(f32) + value[:, cut]).astype(bf16)
            delta_ref[r + k + 1] = (gr_ref[r + k].astype(f32) * slope[:, cut]).astype(bf16)

    def outer(inside, near, far, flip, cot, up):
        ends = (far, inside) if up else (inside, far)
        first = jnp.where(flip, xs[ends[1]], xs[ends[0]])
        last = jnp.where(flip, xs[ends[0]], xs[ends[1]])
        total = dot(w3_ref[0], first) + dot(w3_ref[1], xs[near]) + dot(w3_ref[2], last)
        return (cot * gelu_parts(total)[1]).astype(bf16)

    delta_ref[0] = outer(2, 1, 0, at_top, n_cot, True)
    delta_ref[ROWS + 1] = outer(ROWS + 1, ROWS + 2, ROWS + 3, at_bottom, s_cot, False)

    halo = jnp.concatenate([s, beyond], 1)
    own = jnp.concatenate(
        [edge_ref[pl.ds(0, CH), :].astype(f32), edge_ref[pl.ds(2 * CH, CH), :].astype(f32)], 1
    )
    wide_lane = lanes(2 * COLS)
    kind = wide_lane % 4
    columns = jnp.concatenate(
        [roll(jnp.where(kind == 0, halo, own), 1), halo, roll(jnp.where(kind == 3, halo, own), -1)], 0
    ).astype(bf16)
    y = dot(wa_ref[...], columns)
    y0, y1, y2 = [y[i * CH : (i + 1) * CH] for i in range(3)]
    straight = roll(y0, 4) + y1 + roll(y2, -4)
    turned = roll(y2, 4) + y1 + roll(y0, -4)
    flip = ((wide_lane >= 252) & at_top) | ((wide_lane >= 128) & (wide_lane < 132) & at_bottom)
    slope = gelu_parts(jnp.where(flip, turned, straight))[1]
    dstrip_ref[...] = (jnp.concatenate([gs, gbeyond], 1) * slope).astype(bf16)

    total = None
    group = 8
    for r in range(0, ROWS, group):
        left = jnp.concatenate([delta_ref[r + k + 1] for k in range(group)], 1)
        right = jnp.concatenate([xs[r + k + 1 : r + k + 4].reshape(3 * TAPS, COLS) for k in range(group)], 1)
        term = lax.dot_general(left, right, (((1,), (1,)), ((), ())), preferred_element_type=f32)
        total = term if total is None else total + term
    total = total * grad_scale()
    pieces = [total[:, p * COLS : (p + 1) * COLS] for p in range(4)] + [total[:, 4 * COLS :]]
    count = grad_ref.shape[0]
    for at, piece in enumerate(pieces):
        for j in range(CH // count):
            width = piece.shape[1]
            start = at * COLS * CH // count + j * width
            grad_ref[:, 0, pl.ds(start, width)] = piece[j * count : (j + 1) * count]


def restore_body(rows_ref, out_ref, token_ref, wide):
    for r in range(ROWS):
        wide[pl.ds(r, CH, stride=ROWS), :] = rows_ref[r].astype(f32)
    out_ref[...] = wide[...].astype(bf16)
    token_ref[...] = jnp.zeros(token_ref.shape, f32)


def grad_scale():
    return float(ROWS * COLS * lax.axis_size(EVERY)) ** (-0.5)


def backward_body(after_ref, delta_ref, dstrip_ref, gr_ref, wb_ref, wb3_ref, out_ref, token_ref, xs, wide):
    lat = lax.axis_index(LAT)
    at_top = lat == 0
    at_bottom = lat == lax.axis_size(LAT) - 1
    lane = lanes()
    s = dstrip_ref[:, :COLS].astype(f32)
    beyond = dstrip_ref[:, COLS:].astype(f32)
    stack_taps(xs, 0, delta_ref[0].astype(f32), roll(beyond, -126), lane)
    for r in range(ROWS):
        stack_taps(xs, r + 1, delta_ref[r + 1].astype(f32), roll(s, -(4 * r + 2)), lane)
    stack_taps(xs, ROWS + 1, delta_ref[ROWS + 1].astype(f32), roll(beyond, -2), lane)
    weights = wb_ref[...]

    def put(r, back):
        wide[pl.ds(r, CH, stride=ROWS), :] = gr_ref[r].astype(f32) + back

    upper = jnp.where(at_top, wb3_ref[2], wb3_ref[0])
    lower = jnp.where(at_bottom, wb3_ref[0], wb3_ref[2])
    put(0, dot(upper, xs[0]) + dot(wb3_ref[1], xs[1]) + dot(wb3_ref[2], xs[2]))
    end = ROWS - 1
    put(end, dot(wb3_ref[0], xs[end]) + dot(wb3_ref[1], xs[end + 1]) + dot(lower, xs[end + 2]))
    for r in range(1, ROWS - 1, 2):
        window = jnp.concatenate(
            [xs[r : r + 3].reshape(3 * TAPS, COLS), xs[r + 1 : r + 4].reshape(3 * TAPS, COLS)], 1
        )
        back = dot(weights, window)
        put(r, back[:, :COLS])
        put(r + 1, back[:, COLS:])
    out_ref[...] = wide[...].astype(bf16)
    token_ref[...] = jnp.zeros(token_ref.shape, f32)


def scatter_body(parts_ref, *rest):
    out_ref = rest[-1]
    total = jnp.sum(parts_ref[...], 0)
    width = out_ref.shape[2]
    for i in range(out_ref.shape[0]):
        out_ref[i] = total[:, i * width : (i + 1) * width]


def spread_body(parts_ref, *rest):
    out_ref = rest[-1]
    total = jnp.sum(parts_ref[...], 0)
    for i in range(out_ref.shape[0]):
        out_ref[i] = total


def join_body(parts_ref, out_ref):
    width = parts_ref.shape[2]
    for i in range(out_ref.shape[0]):
        for j in range(parts_ref.shape[0]):
            out_ref[i, :, pl.ds(j * width, width)] = parts_ref[j]


def unpack_body(parts_ref, out_ref):
    count = parts_ref.shape[0]
    for tap in range(9):
        at = tap // 2
        width = min(COLS, 9 * CH - at * COLS)
        for j in range(CH // count):
            start = at * COLS * CH // count + j * width + (tap % 2) * CH
            out_ref[tap, pl.ds(j * count, count), :] = parts_ref[:, 0, pl.ds(start, CH)]


def outer_pairs(lat_count, lon_count):
    half = lon_count // 2
    pairs = []
    for l in range(lat_count):
        for m in range(lon_count):
            to = l - 1 if l % 2 == 0 else l + 1
            if 0 <= to < lat_count:
                pairs.append((l * lon_count + m, to * lon_count + m))
            else:
                pairs.append((l * lon_count + m, l * lon_count + (m + half) % lon_count))
    return pairs


def on_device(field, kernel, cotangent):
    lat_count = lax.axis_size(LAT)
    lon_count = lax.axis_size(LON)
    near_count = lax.axis_size(NEAR)
    flat = (CH * ROWS, COLS)
    rows_shape = (ROWS, CH, COLS)

    flat_field, flat_cotangent = field.reshape(flat), cotangent.reshape(flat)
    outer, inner, f_near, g_near = call(
        pack_body,
        [((TAPS, COLS), bf16), ((TAPS, COLS), bf16), (flat, bf16), (flat, bf16)],
        (flat_field, flat_cotangent),
        [pltpu.VMEM(flat, f32), pltpu.SemaphoreType.DMA((2, PIECES))],
        space=pl.ANY,
        limit=52.5,
    )
    outer = lax.ppermute(outer, EVERY, outer_pairs(lat_count, lon_count))
    inner = lax.ppermute(inner, "core", [(0, 1), (1, 0)])
    fr, gr, edge = call(
        turn_body,
        [(rows_shape, bf16), (rows_shape, bf16), ((2 * CH, COLS), bf16)],
        (f_near, g_near),
        [pltpu.VMEM(flat, f32)],
    )

    (edge,) = call(edge_body, [((TAPS, COLS), bf16)], (edge, outer, inner))
    swaps = [(i, (i + 1 if i % 2 else i - 1) % lon_count) for i in range(lon_count)]
    far = lax.ppermute(edge, LON, swaps)
    near = lax.ppermute(edge, "side", [(0, 1), (1, 0)])

    w3 = jnp.transpose(kernel, (0, 2, 1, 3)).reshape(3, CH, TAPS)
    w = jnp.transpose(kernel, (2, 0, 1, 3)).reshape(CH, 3 * TAPS)
    turned = kernel[::-1, ::-1]
    wb3 = jnp.transpose(turned, (0, 3, 1, 2)).reshape(3, CH, TAPS)
    wb = jnp.transpose(turned, (3, 0, 1, 2)).reshape(CH, 3 * TAPS)

    conv_flops = 2 * 9 * CH * CH * ROWS * COLS
    out_rows, delta, dstrip, grad = call(
        forward_body,
        [
            (rows_shape, bf16),
            ((ROWS + 2, CH, COLS), bf16),
            ((CH, 2 * COLS), bf16),
            ((near_count, 1, 9 * CH * CH // near_count), f32),
        ],
        (fr, gr, edge, far, near, outer, inner, w, w3, w3.reshape(TAPS, TAPS)),
        [pltpu.VMEM((ROWS + 4, TAPS, COLS), bf16)],
        2 * conv_flops,
    )

    def exchange(body, count, width, axes, *args):
        (parts,) = call(body, [((count, 1, width), f32)], args)
        return lax.all_to_all(parts, axes, 0, 0)

    token = ((8, COLS), f32)
    across, deep = lax.axis_size(ACROSS), lax.axis_size("z")
    piece = grad.shape[2] // across
    parts = lax.all_to_all(grad, NEAR, 0, 0)
    output, done = call(restore_body, [(flat, bf16), token], (out_rows,), [pltpu.VMEM(flat, f32)])
    parts = exchange(scatter_body, across, piece, ACROSS, parts, done)
    grad_input, done = call(
        backward_body,
        [(flat, bf16), token],
        (parts, delta, dstrip, gr, wb, wb3),
        [pltpu.VMEM((ROWS + 2, TAPS, COLS), bf16), pltpu.VMEM(flat, f32)],
        conv_flops,
    )
    parts = exchange(spread_body, deep, piece, "z", parts)
    parts = exchange(spread_body, across, piece, ACROSS, parts, done)
    parts = exchange(join_body, near_count, piece * across, NEAR, parts)
    (grad_kernel,) = call(unpack_body, [((9, CH, CH), f32)], (parts,))
    shape = field.shape
    return (output.reshape(shape), grad_input.reshape(shape), grad_kernel.reshape(kernel.shape))


def solution(mesh):
    lat_count, lon_count = mesh.devices.shape
    x = min(4, lat_count // 2)
    split = Mesh(mesh.devices.reshape(lat_count // (2 * x), x, 2, lon_count // 2, 2), EVERY)
    block = P(None, None, LAT, LON)
    return jax.shard_map(
        on_device,
        mesh=split,
        in_specs=(block, P(), block),
        out_specs=(block, block, P()),
        check_vma=False,
    )
```

```python
import math

import jax
import jax.numpy as jnp
from jax import lax
from jax.experimental import pallas as pl
from jax.experimental.pallas import tpu as pltpu
from jax.sharding import Mesh
from jax.sharding import PartitionSpec as P

gelu_scale = math.sqrt(2.0 / math.pi)
ROWS, COLS, CH = 32, 128, 64
TAPS = 3 * CH
PIECES = 4
f32, bf16 = jnp.float32, jnp.bfloat16
LON = ("z", "side")
PLANE = ("lat", "side")
EVERY = ("lat", "z", "side")


def gelu_parts(hidden):
    square = hidden * hidden
    half = 0.5 + 0.5 * jnp.tanh(gelu_scale * hidden * (1.0 + 0.044715 * square))
    steep = gelu_scale * (1.0 + 3.0 * 0.044715 * square)
    return (hidden * half, half + 2.0 * hidden * half * (1.0 - half) * steep)


def roll(x, shift):
    return pltpu.roll(x, shift % x.shape[1], 1)


def lanes(width=COLS):
    return lax.broadcasted_iota(jnp.int32, (CH, width), 1)


def call(body, out_shape, args, scratch=(), flops=0, space=pltpu.VMEM, limit=24):
    outs = [jax.ShapeDtypeStruct(s, d) for s, d in out_shape]
    size = sum(a.size * a.dtype.itemsize for a in list(args) + outs)
    return pl.pallas_call(
        body,
        out_shape=outs,
        in_specs=[pl.BlockSpec(memory_space=space)] * len(args),
        out_specs=[pl.BlockSpec(memory_space=pltpu.VMEM)] * len(outs),
        scratch_shapes=list(scratch),
        cost_estimate=pl.CostEstimate(flops=flops, bytes_accessed=size, transcendentals=0),
        compiler_params=pltpu.CompilerParams(vmem_limit_bytes=int(limit * 2**20)),
    )(*args)


def pack_body(f_hbm, g_hbm, outer_ref, inner_ref, f_ref, g_ref, wide, sems):
    part = CH * ROWS // PIECES
    copies = [
        [
            pltpu.make_async_copy(src.at[pl.ds(i * part, part)], dst.at[pl.ds(i * part, part)], sems.at[at, i])
            for i in range(PIECES)
        ]
        for at, (src, dst) in enumerate(((f_hbm, f_ref), (g_hbm, g_ref)))
    ]
    for copy in copies[0] + copies[1]:
        copy.start()
    even = lax.axis_index("lat") % 2 == 0
    end = ROWS - 1
    slots = (((0, 0, end), (1, 1, end - 1)), ((2, 0, end),))
    for at, src in enumerate((f_ref, g_ref)):
        for i, copy in enumerate(copies[at]):
            copy.wait()
            wide[pl.ds(i * part, part), :] = src[pl.ds(i * part, part), :].astype(f32)
        for slot, low, high in slots[at]:
            first = wide[pl.ds(low, CH, stride=ROWS), :]
            last = wide[pl.ds(high, CH, stride=ROWS), :]
            outer_ref[pl.ds(slot * CH, CH), :] = jnp.where(even, first, last).astype(bf16)
            inner_ref[pl.ds(slot * CH, CH), :] = jnp.where(even, last, first).astype(bf16)


def turn_body(f_ref, g_ref, fr_ref, gr_ref, edge_ref, wide):
    lane = lanes()
    for at, (src, dst) in enumerate(((f_ref, fr_ref), (g_ref, gr_ref))):
        wide[...] = src[...].astype(f32)
        edge = jnp.zeros((CH, COLS), f32)
        for r in range(ROWS):
            row = wide[pl.ds(r, CH, stride=ROWS), :]
            edge = jnp.where((lane >= 4 * r) & (lane < 4 * r + 4), roll(row, 4 * r + 2), edge)
            dst[r] = row.astype(bf16)
        edge_ref[pl.ds(at * CH, CH), :] = edge.astype(bf16)


def row_halos(outer_ref, inner_ref):
    even = lax.axis_index("lat") % 2 == 0
    north = jnp.where(even, outer_ref[...], inner_ref[...]).astype(f32)
    south = jnp.where(even, inner_ref[...], outer_ref[...]).astype(f32)
    return [half[i * CH : (i + 1) * CH] for half in (north, south) for i in range(3)]


def edge_body(edge_ref, outer_ref, inner_ref, token_ref, out_ref):
    n_near, n_far, n_cot, s_near, s_far, s_cot = row_halos(outer_ref, inner_ref)
    lane = lanes()
    low = jnp.where(lane < 4, roll(s_near, 2), jnp.where(lane < 8, roll(s_far, 6), roll(s_cot, 10)))
    high = jnp.where(
        lane >= 124, roll(n_near, 126), jnp.where(lane >= 120, roll(n_far, 122), roll(n_cot, 118))
    )
    out_ref[pl.ds(0, 2 * CH), :] = edge_ref[...]
    out_ref[pl.ds(2 * CH, CH), :] = jnp.where(lane < 64, low, high).astype(bf16)


def strip(near_ref, far_ref, part):
    at = pl.ds(part * CH, CH)
    near = near_ref[at, :].astype(f32)
    far = far_ref[at, :].astype(f32)
    even = lax.axis_index("side") == 0
    return jnp.where(lanes() % 4 < 2, jnp.where(even, far, near), jnp.where(even, near, far))


def stack_taps(out_ref, at, own, halo, lane):
    out_ref[at, pl.ds(0, CH), :] = roll(jnp.where(lane == COLS - 1, halo, own), 1).astype(bf16)
    out_ref[at, pl.ds(CH, CH), :] = own.astype(bf16)
    out_ref[at, pl.ds(2 * CH, CH), :] = roll(jnp.where(lane == 0, halo, own), -1).astype(bf16)


def dot(a, b):
    return jnp.dot(a, b, preferred_element_type=f32)


def interior_body(fr_ref, gr_ref, w_ref, out_ref, delta_ref, grad_ref, token_ref, xs):
    lane = lanes()
    inner = (lane > 0) & (lane < COLS - 1)
    none = jnp.zeros((CH, COLS), f32)
    for r in range(ROWS):
        stack_taps(xs, r, fr_ref[r].astype(f32), none, lane)
    weights = w_ref[...]
    for r in range(1, ROWS - 1, 2):
        window = jnp.concatenate(
            [xs[r - 1 : r + 2].reshape(3 * TAPS, COLS), xs[r : r + 3].reshape(3 * TAPS, COLS)], 1
        )
        value, slope = gelu_parts(dot(weights, window))
        for k in range(2):
            cut = slice(k * COLS, (k + 1) * COLS)
            out_ref[r + k - 1] = (fr_ref[r + k].astype(f32) + value[:, cut]).astype(bf16)
            delta = gr_ref[r + k].astype(f32) * slope[:, cut]
            delta_ref[r + k - 1] = jnp.where(inner, delta, 0.0).astype(bf16)
    total = None
    group = 10
    for r in range(0, ROWS - 2, group):
        left = jnp.concatenate([delta_ref[r + k] for k in range(group)], 1)
        right = jnp.concatenate([xs[r + k : r + k + 3].reshape(3 * TAPS, COLS) for k in range(group)], 1)
        term = dot_lanes(left, right)
        total = term if total is None else total + term
    grad_ref[...] = total
    token_ref[...] = jnp.zeros(token_ref.shape, f32)


def dot_lanes(a, b):
    return lax.dot_general(a, b, (((1,), (1,)), ((), ())), preferred_element_type=f32)


def border_body(
    fr_ref, gr_ref, edge_ref, far_ref, near_ref, outer_ref, inner_ref, w_ref, wa_ref, part_ref,
    out_ref, outstrip_ref, delta_ref, dstrip_ref, grad_ref, xs,
):
    lat = lax.axis_index("lat")
    at_top = lat == 0
    at_bottom = lat == lax.axis_size("lat") - 1
    lane = lanes()
    n_near, n_far, n_cot, s_near, s_far, s_cot = row_halos(outer_ref, inner_ref)

    s = strip(near_ref, far_ref, 0)
    gs = strip(near_ref, far_ref, 1)
    beyond = strip(near_ref, far_ref, 2)
    gbeyond = jnp.where(lane < 64, roll(beyond, 120), roll(beyond, 8))

    end = ROWS - 1
    stack_taps(xs, 0, n_far, roll(beyond, -122), lane)
    stack_taps(xs, 1, n_near, roll(beyond, -126), lane)
    for at, r in ((2, 0), (3, 1), (4, end - 1), (5, end)):
        stack_taps(xs, at, fr_ref[r].astype(f32), roll(s, -(4 * r + 2)), lane)
    stack_taps(xs, 6, s_near, roll(beyond, -2), lane)
    stack_taps(xs, 7, s_far, roll(beyond, -6), lane)

    weights = w_ref[...]
    window = jnp.concatenate([xs[1:4].reshape(3 * TAPS, COLS), xs[4:7].reshape(3 * TAPS, COLS)], 1)
    value, slope = gelu_parts(dot(weights, window))
    deltas = []
    for k, r in enumerate((0, end)):
        cut = slice(k * COLS, (k + 1) * COLS)
        out_ref[k] = (fr_ref[r].astype(f32) + value[:, cut]).astype(bf16)
        deltas.append((gr_ref[r].astype(f32) * slope[:, cut]).astype(bf16))
        delta_ref[k + 1] = deltas[k]

    def turned(flip, low):
        first = jnp.where(flip, xs[low + 2], xs[low])
        last = jnp.where(flip, xs[low], xs[low + 2])
        return jnp.concatenate([first, xs[low + 1], last], 0)

    outside = jnp.concatenate([turned(at_top, 0), turned(at_bottom, 5)], 1)
    slope = gelu_parts(dot(weights, outside))[1]
    delta_ref[0] = (n_cot * slope[:, :COLS]).astype(bf16)
    delta_ref[3] = (s_cot * slope[:, COLS:]).astype(bf16)

    edge = edge_ref[pl.ds(0, CH), :].astype(f32)
    halo = jnp.concatenate([s, beyond], 1)
    own = jnp.concatenate([edge, edge_ref[pl.ds(2 * CH, CH), :].astype(f32)], 1)
    wide_lane = lanes(2 * COLS)
    kind = wide_lane % 4
    small = lane % 4
    outer_taps = jnp.concatenate(
        [roll(jnp.where(kind == 0, halo, own), 1), halo, roll(jnp.where(kind == 3, halo, own), -1)], 0
    )
    inner_taps = jnp.concatenate(
        [roll(jnp.where(small == 1, s, edge), 1), edge, roll(jnp.where(small == 2, s, edge), -1)], 0
    )
    y = dot(wa_ref[...], jnp.concatenate([outer_taps, inner_taps], 1).astype(bf16))
    y0, y1, y2 = [y[i * CH : (i + 1) * CH, : 2 * COLS] for i in range(3)]
    straight = roll(y0, 4) + y1 + roll(y2, -4)
    backward = roll(y2, 4) + y1 + roll(y0, -4)
    flip = ((wide_lane >= 252) & at_top) | ((wide_lane >= 128) & (wide_lane < 132) & at_bottom)
    y0, y1, y2 = [y[i * CH : (i + 1) * CH, 2 * COLS :] for i in range(3)]
    packed = [jnp.where(flip, backward, straight), roll(y0, 4) + y1 + roll(y2, -4)]
    value, slope = gelu_parts(jnp.concatenate(packed, 1))
    own_cot = edge_ref[pl.ds(CH, CH), :].astype(f32)
    outstrip_ref[...] = (edge + value[:, 2 * COLS :]).astype(bf16)
    dstrip = jnp.concatenate([gs, gbeyond, own_cot], 1) * slope
    dstrip_ref[...] = dstrip.astype(bf16)

    used = ((small == 1) | (small == 2)) & (lane >= 4) & (lane < 4 * end)
    side = jnp.where(used, dstrip[:, 2 * COLS :], 0.0).astype(bf16)
    shifted = jnp.concatenate([roll(inner_taps, 4), inner_taps, roll(inner_taps, -4)], 0).astype(bf16)
    left = jnp.concatenate([deltas[0], deltas[1], side], 1)
    total = part_ref[...] + dot_lanes(left, jnp.concatenate([window, shifted], 1))
    total = total * grad_scale()
    pieces = [total[:, p * COLS : (p + 1) * COLS] for p in range(4)] + [total[:, 4 * COLS :]]
    count = grad_ref.shape[0]
    for at, piece in enumerate(pieces):
        for j in range(CH // count):
            width = piece.shape[1]
            start = at * COLS * CH // count + j * width
            grad_ref[:, 0, pl.ds(start, width)] = piece[j * count : (j + 1) * count]


def patched(row, packed, r, lane):
    return jnp.where((lane == 0) | (lane == COLS - 1), roll(packed, -(4 * r + 2)), row.astype(f32))


def restore_body(mid_ref, rim_ref, strip_ref, out_ref, wide):
    lane = lanes()
    packed = strip_ref[...].astype(f32)
    wide[pl.ds(0, CH, stride=ROWS), :] = rim_ref[0].astype(f32)
    for r in range(1, ROWS - 1):
        wide[pl.ds(r, CH, stride=ROWS), :] = patched(mid_ref[r - 1], packed, r, lane)
    wide[pl.ds(ROWS - 1, CH, stride=ROWS), :] = rim_ref[1].astype(f32)
    out_ref[...] = wide[...].astype(bf16)


def grad_scale():
    return float(ROWS * COLS * lax.axis_size(EVERY)) ** (-0.5)


def backward_body(after_ref, mid_ref, rim_ref, dstrip_ref, gr_ref, wb_ref, wb3_ref, out_ref, xs, wide):
    lat = lax.axis_index("lat")
    at_top = lat == 0
    at_bottom = lat == lax.axis_size("lat") - 1
    lane = lanes()
    s = dstrip_ref[:, :COLS].astype(f32)
    beyond = dstrip_ref[:, COLS : 2 * COLS].astype(f32)
    own = dstrip_ref[:, 2 * COLS :].astype(f32)
    stack_taps(xs, 0, rim_ref[0].astype(f32), roll(beyond, -126), lane)
    stack_taps(xs, 1, rim_ref[1].astype(f32), roll(s, -2), lane)
    for r in range(1, ROWS - 1):
        stack_taps(xs, r + 1, patched(mid_ref[r - 1], own, r, lane), roll(s, -(4 * r + 2)), lane)
    stack_taps(xs, ROWS, rim_ref[2].astype(f32), roll(s, -(4 * ROWS - 2)), lane)
    stack_taps(xs, ROWS + 1, rim_ref[3].astype(f32), roll(beyond, -2), lane)
    weights = wb_ref[...]

    def put(r, back):
        wide[pl.ds(r, CH, stride=ROWS), :] = gr_ref[r].astype(f32) + back

    upper = jnp.where(at_top, wb3_ref[2], wb3_ref[0])
    lower = jnp.where(at_bottom, wb3_ref[0], wb3_ref[2])
    put(0, dot(upper, xs[0]) + dot(wb3_ref[1], xs[1]) + dot(wb3_ref[2], xs[2]))
    end = ROWS - 1
    put(end, dot(wb3_ref[0], xs[end]) + dot(wb3_ref[1], xs[end + 1]) + dot(lower, xs[end + 2]))
    for r in range(1, ROWS - 1, 2):
        window = jnp.concatenate(
            [xs[r : r + 3].reshape(3 * TAPS, COLS), xs[r + 1 : r + 4].reshape(3 * TAPS, COLS)], 1
        )
        back = dot(weights, window)
        put(r, back[:, :COLS])
        put(r + 1, back[:, COLS:])
    out_ref[...] = wide[...].astype(bf16)


def fold_body(parts_ref, out_ref):
    total = jnp.sum(parts_ref[...], 0)
    for i in range(out_ref.shape[0]):
        out_ref[i] = total


def unpack_body(parts_ref, out_ref):
    count = parts_ref.shape[0]
    for tap in range(9):
        at = tap // 2
        width = min(COLS, 9 * CH - at * COLS)
        for j in range(CH // count):
            start = at * COLS * CH // count + j * width + (tap % 2) * CH
            out_ref[tap, pl.ds(j * count, count), :] = parts_ref[:, 0, pl.ds(start, CH)]


def outer_pairs(lat_count, lon_count):
    half = lon_count // 2
    pairs = []
    for l in range(lat_count):
        for m in range(lon_count):
            to = l - 1 if l % 2 == 0 else l + 1
            if 0 <= to < lat_count:
                pairs.append((l * lon_count + m, to * lon_count + m))
            else:
                pairs.append((l * lon_count + m, l * lon_count + (m + half) % lon_count))
    return pairs


def on_device(field, kernel, cotangent):
    lat_count = lax.axis_size("lat")
    lon_count = lax.axis_size(LON)
    plane = lax.axis_size(PLANE)
    flat = (CH * ROWS, COLS)
    rows_shape = (ROWS, CH, COLS)

    flat_field, flat_cotangent = field.reshape(flat), cotangent.reshape(flat)
    outer, inner, f_near, g_near = call(
        pack_body,
        [((TAPS, COLS), bf16), ((TAPS, COLS), bf16), (flat, bf16), (flat, bf16)],
        (flat_field, flat_cotangent),
        [pltpu.VMEM(flat, f32), pltpu.SemaphoreType.DMA((2, PIECES))],
        space=pl.ANY,
        limit=52.5,
    )
    outer = lax.ppermute(outer, EVERY, outer_pairs(lat_count, lon_count))
    inner = lax.ppermute(inner, "lat", [(i, i ^ 1) for i in range(lat_count)])
    fr, gr, edge = call(
        turn_body,
        [(rows_shape, bf16), (rows_shape, bf16), ((2 * CH, COLS), bf16)],
        (f_near, g_near),
        [pltpu.VMEM(flat, f32)],
    )

    w3 = jnp.transpose(kernel, (0, 2, 1, 3)).reshape(TAPS, TAPS)
    w = jnp.transpose(kernel, (2, 0, 1, 3)).reshape(CH, 3 * TAPS)
    turned = kernel[::-1, ::-1]
    wb3 = jnp.transpose(turned, (0, 3, 1, 2)).reshape(3, CH, TAPS)
    wb = jnp.transpose(turned, (3, 0, 1, 2)).reshape(CH, 3 * TAPS)
    conv_flops = 2 * 9 * CH * CH * ROWS * COLS
    out_mid, delta_mid, grad_mid, token = call(
        interior_body,
        [
            ((ROWS - 2, CH, COLS), bf16),
            ((ROWS - 2, CH, COLS), bf16),
            ((CH, 3 * TAPS), f32),
            ((8, COLS), f32),
        ],
        (fr, gr, w),
        [pltpu.VMEM((ROWS, TAPS, COLS), bf16)],
        2 * conv_flops,
    )

    (edge,) = call(edge_body, [((TAPS, COLS), bf16)], (edge, outer, inner, token))
    swaps = [(i, (i + 1 if i % 2 else i - 1) % lon_count) for i in range(lon_count)]
    far = lax.ppermute(edge, LON, swaps)
    near = lax.ppermute(edge, "side", [(0, 1), (1, 0)])

    out_rim, out_strip, delta_rim, dstrip, grad = call(
        border_body,
        [
            ((2, CH, COLS), bf16),
            ((CH, COLS), bf16),
            ((4, CH, COLS), bf16),
            ((CH, 3 * COLS), bf16),
            ((plane, 1, 9 * CH * CH // plane), f32),
        ],
        (fr, gr, edge, far, near, outer, inner, w, w3, grad_mid),
        [pltpu.VMEM((8, TAPS, COLS), bf16)],
        conv_flops // 4,
    )

    def spread(parts, count):
        return call(fold_body, [((count,) + parts.shape[1:], f32)], (parts,))[0]

    parts = lax.all_to_all(grad, PLANE, 0, 0)
    (output,) = call(restore_body, [(flat, bf16)], (out_mid, out_rim, out_strip), [pltpu.VMEM(flat, f32)])
    parts = lax.all_to_all(spread(parts, lax.axis_size("z")), "z", 0, 0)
    (grad_input,) = call(
        backward_body,
        [(flat, bf16)],
        (parts, delta_mid, delta_rim, dstrip, gr, wb, wb3),
        [pltpu.VMEM((ROWS + 2, TAPS, COLS), bf16), pltpu.VMEM(flat, f32)],
        conv_flops,
    )
    parts = lax.all_to_all(spread(parts, plane), PLANE, 0, 0)
    (grad_kernel,) = call(unpack_body, [((9, CH, CH), f32)], (parts,))
    shape = field.shape
    return (output.reshape(shape), grad_input.reshape(shape), grad_kernel.reshape(kernel.shape))


def solution(mesh):
    lat_count, lon_count = mesh.devices.shape
    split = Mesh(mesh.devices.reshape(lat_count, lon_count // 2, 2), EVERY)
    block = P(None, None, "lat", LON)
    return jax.shard_map(
        on_device,
        mesh=split,
        in_specs=(block, P(), block),
        out_specs=(block, block, P()),
        check_vma=False,
    )
```

```python
import math

import jax
import jax.numpy as jnp
from jax import lax
from jax.experimental import pallas as pl
from jax.experimental.pallas import tpu as pltpu
from jax.sharding import Mesh
from jax.sharding import PartitionSpec as P

gelu_scale = math.sqrt(2.0 / math.pi)
ROWS, COLS, CH = 32, 128, 64
TAPS = 3 * CH
PIECES = 4
f32, bf16 = jnp.float32, jnp.bfloat16
LON = ("z", "side")
PLANE = ("lat", "side")
EVERY = ("lat", "z", "side")


def gelu_parts(hidden):
    square = hidden * hidden
    half = 0.5 + 0.5 * jnp.tanh(gelu_scale * hidden * (1.0 + 0.044715 * square))
    steep = gelu_scale * (1.0 + 3.0 * 0.044715 * square)
    return (hidden * half, half + 2.0 * hidden * half * (1.0 - half) * steep)


def roll(x, shift):
    return pltpu.roll(x, shift % x.shape[1], 1)


def lanes(width=COLS):
    return lax.broadcasted_iota(jnp.int32, (CH, width), 1)


def call(body, out_shape, args, scratch=(), flops=0, space=pltpu.VMEM, out_space=pltpu.VMEM, limit=24):
    outs = [jax.ShapeDtypeStruct(s, d) for s, d in out_shape]
    size = sum(a.size * a.dtype.itemsize for a in list(args) + outs)
    return pl.pallas_call(
        body,
        out_shape=outs,
        in_specs=[pl.BlockSpec(memory_space=space)] * len(args),
        out_specs=[pl.BlockSpec(memory_space=out_space)] * len(outs),
        scratch_shapes=list(scratch),
        cost_estimate=pl.CostEstimate(flops=flops, bytes_accessed=size, transcendentals=0),
        compiler_params=pltpu.CompilerParams(vmem_limit_bytes=int(limit * 2**20)),
    )(*args)


def pack_body(f_hbm, g_hbm, outer_ref, inner_ref, f_ref, g_ref, wide, sems):
    part = CH * ROWS // PIECES
    copies = [
        [
            pltpu.make_async_copy(src.at[pl.ds(i * part, part)], dst.at[pl.ds(i * part, part)], sems.at[at, i])
            for i in range(PIECES)
        ]
        for at, (src, dst) in enumerate(((f_hbm, f_ref), (g_hbm, g_ref)))
    ]
    for copy in copies[0] + copies[1]:
        copy.start()
    even = lax.axis_index("lat") % 2 == 0
    end = ROWS - 1
    slots = (((0, 0, end), (1, 1, end - 1)), ((2, 0, end),))
    for at, src in enumerate((f_ref, g_ref)):
        for i, copy in enumerate(copies[at]):
            copy.wait()
            wide[pl.ds(i * part, part), :] = src[pl.ds(i * part, part), :].astype(f32)
        for slot, low, high in slots[at]:
            first = wide[pl.ds(low, CH, stride=ROWS), :]
            last = wide[pl.ds(high, CH, stride=ROWS), :]
            outer_ref[pl.ds(slot * CH, CH), :] = jnp.where(even, first, last).astype(bf16)
            inner_ref[pl.ds(slot * CH, CH), :] = jnp.where(even, last, first).astype(bf16)


def turn_body(f_ref, g_ref, fr_ref, gr_ref, edge_ref, wide):
    lane = lanes()
    for at, (src, dst) in enumerate(((f_ref, fr_ref), (g_ref, gr_ref))):
        wide[...] = src[...].astype(f32)
        edge = jnp.zeros((CH, COLS), f32)
        for r in range(ROWS):
            row = wide[pl.ds(r, CH, stride=ROWS), :]
            edge = jnp.where((lane >= 4 * r) & (lane < 4 * r + 4), roll(row, 4 * r + 2), edge)
            dst[r] = row.astype(bf16)
        edge_ref[pl.ds(at * CH, CH), :] = edge.astype(bf16)


def row_halos(outer_ref, inner_ref):
    even = lax.axis_index("lat") % 2 == 0
    north = jnp.where(even, outer_ref[...], inner_ref[...]).astype(f32)
    south = jnp.where(even, inner_ref[...], outer_ref[...]).astype(f32)
    return [half[i * CH : (i + 1) * CH] for half in (north, south) for i in range(3)]


CORNERS = (
    ("s_near", 0, 0), ("s_near", 0, 1), ("s_cot", 0, 2), ("s_far", 4, 0), ("s_far", 4, 1),
    ("n_far", 120, 0), ("n_far", 120, 1), ("n_near", 124, 0), ("n_near", 124, 1), ("n_cot", 124, 2),
)


def edge_body(edge_ref, outer_ref, inner_ref, token_ref, far_ref, near_ref):
    names = ("n_near", "n_far", "n_cot", "s_near", "s_far", "s_cot")
    halos = dict(zip(names, row_halos(outer_ref, inner_ref)))
    kind = lanes() % 4
    lane = lanes()
    field = edge_ref[pl.ds(0, CH), :].astype(f32)
    cot = edge_ref[pl.ds(CH, CH), :].astype(f32)
    east = jnp.where(kind < 2, field, roll(cot, 1))
    west = jnp.where(kind >= 2, field, roll(cot, -1))
    for slot, (row, _, column) in enumerate(CORNERS):
        value = halos[row]
        to = 4 * slot + 3
        east = jnp.where(lane == to, roll(value, to - (126, 127, 127)[column]), east)
        to = 4 * slot
        west = jnp.where(lane == to, roll(value, to - (0, 1, 0)[column]), west)
    even = lax.axis_index("side") == 0
    far_ref[...] = jnp.where(even, west, east).astype(bf16)
    near_ref[...] = jnp.where(even, east, west).astype(bf16)


def column_halos(far_ref, near_ref):
    even = lax.axis_index("side") == 0
    far = far_ref[...].astype(f32)
    near = near_ref[...].astype(f32)
    west = jnp.where(even, far, near)
    east = jnp.where(even, near, far)
    lane = lanes()
    low = lane % 4 < 2
    field = jnp.where(low, west, east)
    cot = jnp.where(low, roll(west, -1), roll(east, 1))
    beyond = [jnp.zeros((CH, COLS), f32), jnp.zeros((CH, COLS), f32)]
    for slot, (_, base, column) in enumerate(CORNERS):
        at = column // 2
        for src, start, to in (
            (west, 4 * slot + 3, base + (0, 1, 1)[column]),
            (east, 4 * slot, base + (2, 3, 2)[column]),
        ):
            beyond[at] = jnp.where(lane == to, roll(src, to - start), beyond[at])
    return field, cot, beyond[0], beyond[1]


def stack_taps(out_ref, at, own, halo, lane):
    out_ref[at, pl.ds(0, CH), :] = roll(jnp.where(lane == COLS - 1, halo, own), 1).astype(bf16)
    out_ref[at, pl.ds(CH, CH), :] = own.astype(bf16)
    out_ref[at, pl.ds(2 * CH, CH), :] = roll(jnp.where(lane == 0, halo, own), -1).astype(bf16)


def dot(a, b):
    return jnp.dot(a, b, preferred_element_type=f32)


def interior_body(fr_ref, gr_ref, w_ref, out_ref, delta_ref, grad_ref, token_ref, xs):
    lane = lanes()
    inner = (lane > 0) & (lane < COLS - 1)
    none = jnp.zeros((CH, COLS), f32)
    for r in range(ROWS):
        stack_taps(xs, r, fr_ref[r].astype(f32), none, lane)
    weights = w_ref[...]
    for r in range(1, ROWS - 1, 2):
        window = jnp.concatenate(
            [xs[r - 1 : r + 2].reshape(3 * TAPS, COLS), xs[r : r + 3].reshape(3 * TAPS, COLS)], 1
        )
        value, slope = gelu_parts(dot(weights, window))
        for k in range(2):
            cut = slice(k * COLS, (k + 1) * COLS)
            out_ref[r + k - 1] = (fr_ref[r + k].astype(f32) + value[:, cut]).astype(bf16)
            delta = gr_ref[r + k].astype(f32) * slope[:, cut]
            delta_ref[r + k - 1] = jnp.where(inner, delta, 0.0).astype(bf16)
    total = None
    group = 10
    for r in range(0, ROWS - 2, group):
        left = jnp.concatenate([delta_ref[r + k] for k in range(group)], 1)
        right = jnp.concatenate([xs[r + k : r + k + 3].reshape(3 * TAPS, COLS) for k in range(group)], 1)
        term = dot_lanes(left, right)
        total = term if total is None else total + term
    grad_ref[...] = total
    token_ref[...] = jnp.zeros(token_ref.shape, f32)


def dot_lanes(a, b):
    return lax.dot_general(a, b, (((1,), (1,)), ((), ())), preferred_element_type=f32)


def border_body(
    fr_ref, gr_ref, edge_ref, far_ref, near_ref, outer_ref, inner_ref, w_ref, wa_ref, part_ref,
    out_ref, outstrip_ref, delta_ref, dstrip_ref, grad_ref, xs,
):
    lat = lax.axis_index("lat")
    at_top = lat == 0
    at_bottom = lat == lax.axis_size("lat") - 1
    lane = lanes()
    n_near, n_far, n_cot, s_near, s_far, s_cot = row_halos(outer_ref, inner_ref)

    s, gs, beyond, gbeyond = column_halos(far_ref, near_ref)

    end = ROWS - 1
    stack_taps(xs, 0, n_far, roll(beyond, -122), lane)
    stack_taps(xs, 1, n_near, roll(beyond, -126), lane)
    for at, r in ((2, 0), (3, 1), (4, end - 1), (5, end)):
        stack_taps(xs, at, fr_ref[r].astype(f32), roll(s, -(4 * r + 2)), lane)
    stack_taps(xs, 6, s_near, roll(beyond, -2), lane)
    stack_taps(xs, 7, s_far, roll(beyond, -6), lane)

    weights = w_ref[...]
    window = jnp.concatenate([xs[1:4].reshape(3 * TAPS, COLS), xs[4:7].reshape(3 * TAPS, COLS)], 1)
    value, slope = gelu_parts(dot(weights, window))
    deltas = []
    for k, r in enumerate((0, end)):
        cut = slice(k * COLS, (k + 1) * COLS)
        out_ref[k] = (fr_ref[r].astype(f32) + value[:, cut]).astype(bf16)
        deltas.append((gr_ref[r].astype(f32) * slope[:, cut]).astype(bf16))
        delta_ref[k + 1] = deltas[k]

    def turned(flip, low):
        first = jnp.where(flip, xs[low + 2], xs[low])
        last = jnp.where(flip, xs[low], xs[low + 2])
        return jnp.concatenate([first, xs[low + 1], last], 0)

    outside = jnp.concatenate([turned(at_top, 0), turned(at_bottom, 5)], 1)
    slope = gelu_parts(dot(weights, outside))[1]
    delta_ref[0] = (n_cot * slope[:, :COLS]).astype(bf16)
    delta_ref[3] = (s_cot * slope[:, COLS:]).astype(bf16)

    edge = edge_ref[pl.ds(0, CH), :].astype(f32)
    halo = jnp.concatenate([s, beyond], 1)
    low = jnp.where(lane < 4, roll(s_near, 2), roll(s_far, 6))
    high = jnp.where(lane >= 124, roll(n_near, 126), roll(n_far, 122))
    own = jnp.concatenate([edge, jnp.where(lane < 64, low, high)], 1)
    wide_lane = lanes(2 * COLS)
    kind = wide_lane % 4
    small = lane % 4
    outer_taps = jnp.concatenate(
        [roll(jnp.where(kind == 0, halo, own), 1), halo, roll(jnp.where(kind == 3, halo, own), -1)], 0
    )
    inner_taps = jnp.concatenate(
        [roll(jnp.where(small == 1, s, edge), 1), edge, roll(jnp.where(small == 2, s, edge), -1)], 0
    )
    y = dot(wa_ref[...], jnp.concatenate([outer_taps, inner_taps], 1).astype(bf16))
    y0, y1, y2 = [y[i * CH : (i + 1) * CH, : 2 * COLS] for i in range(3)]
    straight = roll(y0, 4) + y1 + roll(y2, -4)
    backward = roll(y2, 4) + y1 + roll(y0, -4)
    flip = ((wide_lane >= 252) & at_top) | ((wide_lane >= 128) & (wide_lane < 132) & at_bottom)
    y0, y1, y2 = [y[i * CH : (i + 1) * CH, 2 * COLS :] for i in range(3)]
    packed = [jnp.where(flip, backward, straight), roll(y0, 4) + y1 + roll(y2, -4)]
    value, slope = gelu_parts(jnp.concatenate(packed, 1))
    own_cot = edge_ref[pl.ds(CH, CH), :].astype(f32)
    outstrip_ref[...] = (edge + value[:, 2 * COLS :]).astype(bf16)
    dstrip = jnp.concatenate([gs, gbeyond, own_cot], 1) * slope
    dstrip_ref[...] = dstrip.astype(bf16)

    used = ((small == 1) | (small == 2)) & (lane >= 4) & (lane < 4 * end)
    side = jnp.where(used, dstrip[:, 2 * COLS :], 0.0).astype(bf16)
    shifted = jnp.concatenate([roll(inner_taps, 4), inner_taps, roll(inner_taps, -4)], 0).astype(bf16)
    left = jnp.concatenate([deltas[0], deltas[1], side], 1)
    total = part_ref[...] + dot_lanes(left, jnp.concatenate([window, shifted], 1))
    total = total * grad_scale()
    pieces = [total[:, p * COLS : (p + 1) * COLS] for p in range(4)] + [total[:, 4 * COLS :]]
    count = grad_ref.shape[0]
    for at, piece in enumerate(pieces):
        for j in range(CH // count):
            width = piece.shape[1]
            start = at * COLS * CH // count + j * width
            grad_ref[:, 0, pl.ds(start, width)] = piece[j * count : (j + 1) * count]


def patched(row, packed, r, lane):
    return jnp.where((lane == 0) | (lane == COLS - 1), roll(packed, -(4 * r + 2)), row.astype(f32))


def restore_body(mid_ref, rim_ref, strip_ref, out_ref, wide):
    lane = lanes()
    packed = strip_ref[...].astype(f32)
    wide[pl.ds(0, CH, stride=ROWS), :] = rim_ref[0].astype(f32)
    for r in range(1, ROWS - 1):
        wide[pl.ds(r, CH, stride=ROWS), :] = patched(mid_ref[r - 1], packed, r, lane)
    wide[pl.ds(ROWS - 1, CH, stride=ROWS), :] = rim_ref[1].astype(f32)
    out_ref[...] = wide[...].astype(bf16)


def grad_scale():
    return float(ROWS * COLS * lax.axis_size(EVERY)) ** (-0.5)


def backward_body(after_ref, mid_ref, rim_ref, dstrip_ref, gr_ref, wb_ref, wb3_ref, out_ref, xs, wide):
    lat = lax.axis_index("lat")
    at_top = lat == 0
    at_bottom = lat == lax.axis_size("lat") - 1
    lane = lanes()
    s = dstrip_ref[:, :COLS].astype(f32)
    beyond = dstrip_ref[:, COLS : 2 * COLS].astype(f32)
    own = dstrip_ref[:, 2 * COLS :].astype(f32)
    stack_taps(xs, 0, rim_ref[0].astype(f32), roll(beyond, -126), lane)
    stack_taps(xs, 1, rim_ref[1].astype(f32), roll(s, -2), lane)
    for r in range(1, ROWS - 1):
        stack_taps(xs, r + 1, patched(mid_ref[r - 1], own, r, lane), roll(s, -(4 * r + 2)), lane)
    stack_taps(xs, ROWS, rim_ref[2].astype(f32), roll(s, -(4 * ROWS - 2)), lane)
    stack_taps(xs, ROWS + 1, rim_ref[3].astype(f32), roll(beyond, -2), lane)
    weights = wb_ref[...]

    def put(r, back):
        wide[pl.ds(r, CH, stride=ROWS), :] = gr_ref[r].astype(f32) + back

    upper = jnp.where(at_top, wb3_ref[2], wb3_ref[0])
    lower = jnp.where(at_bottom, wb3_ref[0], wb3_ref[2])
    put(0, dot(upper, xs[0]) + dot(wb3_ref[1], xs[1]) + dot(wb3_ref[2], xs[2]))
    end = ROWS - 1
    put(end, dot(wb3_ref[0], xs[end]) + dot(wb3_ref[1], xs[end + 1]) + dot(lower, xs[end + 2]))
    for r in range(1, ROWS - 1, 2):
        window = jnp.concatenate(
            [xs[r : r + 3].reshape(3 * TAPS, COLS), xs[r + 1 : r + 4].reshape(3 * TAPS, COLS)], 1
        )
        back = dot(weights, window)
        put(r, back[:, :COLS])
        put(r + 1, back[:, COLS:])
    out_ref[...] = wide[...].astype(bf16)


def fold_body(parts_ref, out_ref):
    total = jnp.sum(parts_ref[...], 0)
    for i in range(out_ref.shape[0]):
        out_ref[i] = total


def unpack_body(parts_ref, out_hbm, out_ref, sems):
    count = parts_ref.shape[0]
    copies = []
    for tap in range(9):
        at = tap // 2
        width = min(COLS, 9 * CH - at * COLS)
        for j in range(CH // count):
            start = at * COLS * CH // count + j * width + (tap % 2) * CH
            out_ref[tap, pl.ds(j * count, count), :] = parts_ref[:, 0, pl.ds(start, CH)]
        copies.append(pltpu.make_async_copy(out_ref.at[tap], out_hbm.at[tap], sems.at[tap]))
        copies[-1].start()
    for copy in copies:
        copy.wait()


def outer_pairs(lat_count, lon_count):
    half = lon_count // 2
    pairs = []
    for l in range(lat_count):
        for m in range(lon_count):
            to = l - 1 if l % 2 == 0 else l + 1
            if 0 <= to < lat_count:
                pairs.append((l * lon_count + m, to * lon_count + m))
            else:
                pairs.append((l * lon_count + m, l * lon_count + (m + half) % lon_count))
    return pairs


def on_device(field, kernel, cotangent):
    lat_count = lax.axis_size("lat")
    lon_count = lax.axis_size(LON)
    plane = lax.axis_size(PLANE)
    flat = (CH * ROWS, COLS)
    rows_shape = (ROWS, CH, COLS)

    flat_field, flat_cotangent = field.reshape(flat), cotangent.reshape(flat)
    outer, inner, f_near, g_near = call(
        pack_body,
        [((TAPS, COLS), bf16), ((TAPS, COLS), bf16), (flat, bf16), (flat, bf16)],
        (flat_field, flat_cotangent),
        [pltpu.VMEM(flat, f32), pltpu.SemaphoreType.DMA((2, PIECES))],
        space=pl.ANY,
        limit=52.5,
    )
    outer = lax.ppermute(outer, EVERY, outer_pairs(lat_count, lon_count))
    inner = lax.ppermute(inner, "lat", [(i, i ^ 1) for i in range(lat_count)])
    fr, gr, edge = call(
        turn_body,
        [(rows_shape, bf16), (rows_shape, bf16), ((2 * CH, COLS), bf16)],
        (f_near, g_near),
        [pltpu.VMEM(flat, f32)],
    )

    w3 = jnp.transpose(kernel, (0, 2, 1, 3)).reshape(TAPS, TAPS)
    w = jnp.transpose(kernel, (2, 0, 1, 3)).reshape(CH, 3 * TAPS)
    turned = kernel[::-1, ::-1]
    wb3 = jnp.transpose(turned, (0, 3, 1, 2)).reshape(3, CH, TAPS)
    wb = jnp.transpose(turned, (3, 0, 1, 2)).reshape(CH, 3 * TAPS)
    conv_flops = 2 * 9 * CH * CH * ROWS * COLS
    out_mid, delta_mid, grad_mid, token = call(
        interior_body,
        [
            ((ROWS - 2, CH, COLS), bf16),
            ((ROWS - 2, CH, COLS), bf16),
            ((CH, 3 * TAPS), f32),
            ((8, COLS), f32),
        ],
        (fr, gr, w),
        [pltpu.VMEM((ROWS, TAPS, COLS), bf16)],
        2 * conv_flops,
    )

    far, near = call(edge_body, [((CH, COLS), bf16)] * 2, (edge, outer, inner, token))
    swaps = [(i, (i + 1 if i % 2 else i - 1) % lon_count) for i in range(lon_count)]
    far = lax.ppermute(far, LON, swaps)
    near = lax.ppermute(near, "side", [(0, 1), (1, 0)])

    out_rim, out_strip, delta_rim, dstrip, grad = call(
        border_body,
        [
            ((2, CH, COLS), bf16),
            ((CH, COLS), bf16),
            ((4, CH, COLS), bf16),
            ((CH, 3 * COLS), bf16),
            ((plane, 1, 9 * CH * CH // plane), f32),
        ],
        (fr, gr, edge, far, near, outer, inner, w, w3, grad_mid),
        [pltpu.VMEM((8, TAPS, COLS), bf16)],
        conv_flops // 4,
    )

    def spread(parts, count):
        return call(fold_body, [((count,) + parts.shape[1:], f32)], (parts,))[0]

    parts = lax.all_to_all(grad, PLANE, 0, 0)
    (output,) = call(restore_body, [(flat, bf16)], (out_mid, out_rim, out_strip), [pltpu.VMEM(flat, f32)])
    parts = lax.all_to_all(spread(parts, lax.axis_size("z")), "z", 0, 0)
    (grad_input,) = call(
        backward_body,
        [(flat, bf16)],
        (parts, delta_mid, delta_rim, dstrip, gr, wb, wb3),
        [pltpu.VMEM((ROWS + 2, TAPS, COLS), bf16), pltpu.VMEM(flat, f32)],
        conv_flops,
    )
    parts = lax.all_to_all(spread(parts, plane), PLANE, 0, 0)
    (grad_kernel,) = call(
        unpack_body,
        [((9, CH, CH), f32)],
        (parts,),
        [pltpu.VMEM((9, CH, CH), f32), pltpu.SemaphoreType.DMA((9,))],
        out_space=pl.ANY,
    )
    shape = field.shape
    return (output.reshape(shape), grad_input.reshape(shape), grad_kernel.reshape(kernel.shape))


def solution(mesh):
    lat_count, lon_count = mesh.devices.shape
    split = Mesh(mesh.devices.reshape(lat_count, lon_count // 2, 2), EVERY)
    block = P(None, None, "lat", LON)
    return jax.shard_map(
        on_device,
        mesh=split,
        in_specs=(block, P(), block),
        out_specs=(block, block, P()),
        check_vma=False,
    )
```

```python
import math

import jax
import jax.numpy as jnp
from jax import lax
from jax.experimental import pallas as pl
from jax.experimental.pallas import tpu as pltpu
from jax.sharding import Mesh
from jax.sharding import PartitionSpec as P

gelu_scale = math.sqrt(2.0 / math.pi)
ROWS, COLS, CH = 32, 128, 64
TAPS = 3 * CH
PIECES = 4
f32, bf16 = jnp.float32, jnp.bfloat16
LON = ("z", "side")
PLANE = ("lat", "side")
EVERY = ("lat", "z", "side")


def gelu_parts(hidden):
    square = hidden * hidden
    half = 0.5 + 0.5 * jnp.tanh(gelu_scale * hidden * (1.0 + 0.044715 * square))
    steep = gelu_scale * (1.0 + 3.0 * 0.044715 * square)
    return (hidden * half, half + 2.0 * hidden * half * (1.0 - half) * steep)


def roll(x, shift):
    return pltpu.roll(x, shift % x.shape[1], 1)


def lanes(width=COLS):
    return lax.broadcasted_iota(jnp.int32, (CH, width), 1)


def call(body, out_shape, args, scratch=(), flops=0, space=pltpu.VMEM, out_space=pltpu.VMEM, limit=24):
    outs = [jax.ShapeDtypeStruct(s, d) for s, d in out_shape]
    size = sum(a.size * a.dtype.itemsize for a in list(args) + outs)
    return pl.pallas_call(
        body,
        out_shape=outs,
        in_specs=[pl.BlockSpec(memory_space=space)] * len(args),
        out_specs=[pl.BlockSpec(memory_space=out_space)] * len(outs),
        scratch_shapes=list(scratch),
        cost_estimate=pl.CostEstimate(flops=flops, bytes_accessed=size, transcendentals=0),
        compiler_params=pltpu.CompilerParams(vmem_limit_bytes=int(limit * 2**20)),
    )(*args)


def pack_body(f_hbm, g_hbm, outer_ref, inner_ref, f_ref, g_ref, wide, sems):
    part = CH * ROWS // PIECES
    copies = [
        [
            pltpu.make_async_copy(src.at[pl.ds(i * part, part)], dst.at[pl.ds(i * part, part)], sems.at[at, i])
            for i in range(PIECES)
        ]
        for at, (src, dst) in enumerate(((f_hbm, f_ref), (g_hbm, g_ref)))
    ]
    for copy in copies[0] + copies[1]:
        copy.start()
    even = lax.axis_index("lat") % 2 == 0
    end = ROWS - 1
    slots = (((0, 0, end), (1, 1, end - 1)), ((2, 0, end),))
    for at, src in enumerate((f_ref, g_ref)):
        for i, copy in enumerate(copies[at]):
            copy.wait()
            wide[pl.ds(i * part, part), :] = src[pl.ds(i * part, part), :].astype(f32)
        for slot, low, high in slots[at]:
            first = wide[pl.ds(low, CH, stride=ROWS), :]
            last = wide[pl.ds(high, CH, stride=ROWS), :]
            outer_ref[pl.ds(slot * CH, CH), :] = jnp.where(even, first, last).astype(bf16)
            inner_ref[pl.ds(slot * CH, CH), :] = jnp.where(even, last, first).astype(bf16)


def turn_body(f_ref, g_ref, fr_ref, gr_ref, edge_ref, wide):
    lane = lanes()
    for at, (src, dst) in enumerate(((f_ref, fr_ref), (g_ref, gr_ref))):
        wide[...] = src[...].astype(f32)
        edge = jnp.zeros((CH, COLS), f32)
        for r in range(ROWS):
            row = wide[pl.ds(r, CH, stride=ROWS), :]
            edge = jnp.where((lane >= 4 * r) & (lane < 4 * r + 4), roll(row, 4 * r + 2), edge)
            dst[r] = row.astype(bf16)
        edge_ref[pl.ds(at * CH, CH), :] = edge.astype(bf16)


def row_halos(outer_ref, inner_ref):
    even = lax.axis_index("lat") % 2 == 0
    north = jnp.where(even, outer_ref[...], inner_ref[...]).astype(f32)
    south = jnp.where(even, inner_ref[...], outer_ref[...]).astype(f32)
    return [half[i * CH : (i + 1) * CH] for half in (north, south) for i in range(3)]


CORNERS = (
    ("s_near", 0, 0), ("s_near", 0, 1), ("s_cot", 0, 2), ("s_far", 4, 0), ("s_far", 4, 1),
    ("n_far", 120, 0), ("n_far", 120, 1), ("n_near", 124, 0), ("n_near", 124, 1), ("n_cot", 124, 2),
)


def edge_body(edge_ref, outer_ref, inner_ref, token_ref, far_ref, near_ref):
    names = ("n_near", "n_far", "n_cot", "s_near", "s_far", "s_cot")
    halos = dict(zip(names, row_halos(outer_ref, inner_ref)))
    kind = lanes() % 4
    lane = lanes()
    field = edge_ref[pl.ds(0, CH), :].astype(f32)
    cot = edge_ref[pl.ds(CH, CH), :].astype(f32)
    east = jnp.where(kind < 2, field, roll(cot, 1))
    west = jnp.where(kind >= 2, field, roll(cot, -1))
    for slot, (row, _, column) in enumerate(CORNERS):
        value = halos[row]
        to = 4 * slot + 3
        east = jnp.where(lane == to, roll(value, to - (126, 127, 127)[column]), east)
        to = 4 * slot
        west = jnp.where(lane == to, roll(value, to - (0, 1, 0)[column]), west)
    even = lax.axis_index("side") == 0
    far_ref[...] = jnp.where(even, west, east).astype(bf16)
    near_ref[...] = jnp.where(even, east, west).astype(bf16)


def column_halos(far_ref, near_ref):
    even = lax.axis_index("side") == 0
    far = far_ref[...].astype(f32)
    near = near_ref[...].astype(f32)
    west = jnp.where(even, far, near)
    east = jnp.where(even, near, far)
    lane = lanes()
    low = lane % 4 < 2
    field = jnp.where(low, west, east)
    cot = jnp.where(low, roll(west, -1), roll(east, 1))
    beyond = [jnp.zeros((CH, COLS), f32), jnp.zeros((CH, COLS), f32)]
    for slot, (_, base, column) in enumerate(CORNERS):
        at = column // 2
        for src, start, to in (
            (west, 4 * slot + 3, base + (0, 1, 1)[column]),
            (east, 4 * slot, base + (2, 3, 2)[column]),
        ):
            beyond[at] = jnp.where(lane == to, roll(src, to - start), beyond[at])
    return field, cot, beyond[0], beyond[1]


def stack_taps(out_ref, at, own, halo, lane):
    out_ref[at, pl.ds(0, CH), :] = roll(jnp.where(lane == COLS - 1, halo, own), 1).astype(bf16)
    out_ref[at, pl.ds(CH, CH), :] = own.astype(bf16)
    out_ref[at, pl.ds(2 * CH, CH), :] = roll(jnp.where(lane == 0, halo, own), -1).astype(bf16)


def dot(a, b):
    return jnp.dot(a, b, preferred_element_type=f32)


def interior_body(fr_ref, gr_ref, w_ref, out_ref, delta_ref, grad_ref, token_ref, xs):
    lane = lanes()
    inner = (lane > 0) & (lane < COLS - 1)
    none = jnp.zeros((CH, COLS), f32)
    for r in range(ROWS):
        stack_taps(xs, r, fr_ref[r].astype(f32), none, lane)
    weights = w_ref[...]
    for r in range(1, ROWS - 1, 2):
        window = jnp.concatenate(
            [xs[r - 1 : r + 2].reshape(3 * TAPS, COLS), xs[r : r + 3].reshape(3 * TAPS, COLS)], 1
        )
        value, slope = gelu_parts(dot(weights, window))
        for k in range(2):
            cut = slice(k * COLS, (k + 1) * COLS)
            out_ref[r + k - 1] = (fr_ref[r + k].astype(f32) + value[:, cut]).astype(bf16)
            delta = gr_ref[r + k].astype(f32) * slope[:, cut]
            delta_ref[r + k - 1] = jnp.where(inner, delta, 0.0).astype(bf16)
    total = None
    group = 10
    for r in range(0, ROWS - 2, group):
        left = jnp.concatenate([delta_ref[r + k] for k in range(group)], 1)
        right = jnp.concatenate([xs[r + k : r + k + 3].reshape(3 * TAPS, COLS) for k in range(group)], 1)
        term = dot_lanes(left, right)
        total = term if total is None else total + term
    grad_ref[...] = total
    token_ref[...] = jnp.zeros(token_ref.shape, f32)


def dot_lanes(a, b):
    return lax.dot_general(a, b, (((1,), (1,)), ((), ())), preferred_element_type=f32)


def border_body(
    fr_ref, gr_ref, edge_ref, far_ref, near_ref, outer_ref, inner_ref, w_ref, wa_ref, part_ref,
    out_ref, outstrip_ref, delta_ref, dstrip_ref, grad_ref, xs,
):
    lat = lax.axis_index("lat")
    at_top = lat == 0
    at_bottom = lat == lax.axis_size("lat") - 1
    lane = lanes()
    n_near, n_far, n_cot, s_near, s_far, s_cot = row_halos(outer_ref, inner_ref)

    s, gs, beyond, gbeyond = column_halos(far_ref, near_ref)

    end = ROWS - 1
    stack_taps(xs, 0, n_far, roll(beyond, -122), lane)
    stack_taps(xs, 1, n_near, roll(beyond, -126), lane)
    for at, r in ((2, 0), (3, 1), (4, end - 1), (5, end)):
        stack_taps(xs, at, fr_ref[r].astype(f32), roll(s, -(4 * r + 2)), lane)
    stack_taps(xs, 6, s_near, roll(beyond, -2), lane)
    stack_taps(xs, 7, s_far, roll(beyond, -6), lane)

    weights = w_ref[...]
    window = jnp.concatenate([xs[1:4].reshape(3 * TAPS, COLS), xs[4:7].reshape(3 * TAPS, COLS)], 1)
    value, slope = gelu_parts(dot(weights, window))
    deltas = []
    for k, r in enumerate((0, end)):
        cut = slice(k * COLS, (k + 1) * COLS)
        out_ref[k] = (fr_ref[r].astype(f32) + value[:, cut]).astype(bf16)
        deltas.append((gr_ref[r].astype(f32) * slope[:, cut]).astype(bf16))
        delta_ref[k + 1] = deltas[k]

    def turned(flip, low):
        first = jnp.where(flip, xs[low + 2], xs[low])
        last = jnp.where(flip, xs[low], xs[low + 2])
        return jnp.concatenate([first, xs[low + 1], last], 0)

    outside = jnp.concatenate([turned(at_top, 0), turned(at_bottom, 5)], 1)
    slope = gelu_parts(dot(weights, outside))[1]
    delta_ref[0] = (n_cot * slope[:, :COLS]).astype(bf16)
    delta_ref[3] = (s_cot * slope[:, COLS:]).astype(bf16)

    edge = edge_ref[pl.ds(0, CH), :].astype(f32)
    halo = jnp.concatenate([s, beyond], 1)
    low = jnp.where(lane < 4, roll(s_near, 2), roll(s_far, 6))
    high = jnp.where(lane >= 124, roll(n_near, 126), roll(n_far, 122))
    own = jnp.concatenate([edge, jnp.where(lane < 64, low, high)], 1)
    wide_lane = lanes(2 * COLS)
    kind = wide_lane % 4
    small = lane % 4
    outer_taps = jnp.concatenate(
        [roll(jnp.where(kind == 0, halo, own), 1), halo, roll(jnp.where(kind == 3, halo, own), -1)], 0
    )
    inner_taps = jnp.concatenate(
        [roll(jnp.where(small == 1, s, edge), 1), edge, roll(jnp.where(small == 2, s, edge), -1)], 0
    )
    y = dot(wa_ref[...], jnp.concatenate([outer_taps, inner_taps], 1).astype(bf16))
    y0, y1, y2 = [y[i * CH : (i + 1) * CH, : 2 * COLS] for i in range(3)]
    straight = roll(y0, 4) + y1 + roll(y2, -4)
    backward = roll(y2, 4) + y1 + roll(y0, -4)
    flip = ((wide_lane >= 252) & at_top) | ((wide_lane >= 128) & (wide_lane < 132) & at_bottom)
    y0, y1, y2 = [y[i * CH : (i + 1) * CH, 2 * COLS :] for i in range(3)]
    packed = [jnp.where(flip, backward, straight), roll(y0, 4) + y1 + roll(y2, -4)]
    value, slope = gelu_parts(jnp.concatenate(packed, 1))
    own_cot = edge_ref[pl.ds(CH, CH), :].astype(f32)
    outstrip_ref[...] = (edge + value[:, 2 * COLS :]).astype(bf16)
    dstrip = jnp.concatenate([gs, gbeyond, own_cot], 1) * slope
    dstrip_ref[...] = dstrip.astype(bf16)

    used = ((small == 1) | (small == 2)) & (lane >= 4) & (lane < 4 * end)
    side = jnp.where(used, dstrip[:, 2 * COLS :], 0.0).astype(bf16)
    shifted = jnp.concatenate([roll(inner_taps, 4), inner_taps, roll(inner_taps, -4)], 0).astype(bf16)
    left = jnp.concatenate([deltas[0], deltas[1], side], 1)
    total = part_ref[...] + dot_lanes(left, jnp.concatenate([window, shifted], 1))
    total = total * grad_scale()
    count = grad_ref.shape[0]
    pieces = []
    for p in range(5):
        piece = total[:, p * COLS : (p + 1) * COLS]
        pieces.append([piece[j * count : (j + 1) * count] for j in range(CH // count)])
    tiles = [piece[j] for j in range(CH // count) for piece in pieces[:4]]
    last = pieces[4]
    for j in range(0, len(last), 2):
        tiles.append(jnp.concatenate(last[j : j + 2], 1))
    for q, tile in enumerate(tiles):
        grad_ref[:, 0, pl.ds(q * COLS, COLS)] = tile


def patched(row, packed, r, lane):
    return jnp.where((lane == 0) | (lane == COLS - 1), roll(packed, -(4 * r + 2)), row.astype(f32))


def write_out(wide, out_hbm, out_ref, sems):
    part = CH * ROWS // PIECES
    copies = []
    for i in range(PIECES):
        at = pl.ds(i * part, part)
        out_ref[at, :] = wide[at, :].astype(bf16)
        copies.append(pltpu.make_async_copy(out_ref.at[at], out_hbm.at[at], sems.at[i]))
        copies[-1].start()
    for copy in copies:
        copy.wait()


def restore_body(mid_ref, rim_ref, strip_ref, out_hbm, wide, out_ref, sems):
    lane = lanes()
    packed = strip_ref[...].astype(f32)
    wide[pl.ds(0, CH, stride=ROWS), :] = rim_ref[0].astype(f32)
    for r in range(1, ROWS - 1):
        wide[pl.ds(r, CH, stride=ROWS), :] = patched(mid_ref[r - 1], packed, r, lane)
    wide[pl.ds(ROWS - 1, CH, stride=ROWS), :] = rim_ref[1].astype(f32)
    write_out(wide, out_hbm, out_ref, sems)


def grad_scale():
    return float(ROWS * COLS * lax.axis_size(EVERY)) ** (-0.5)


def backward_body(after_ref, mid_ref, rim_ref, dstrip_ref, gr_ref, wb_ref, wb3_ref, out_hbm, xs, wide, out_ref, sems):
    lat = lax.axis_index("lat")
    at_top = lat == 0
    at_bottom = lat == lax.axis_size("lat") - 1
    lane = lanes()
    s = dstrip_ref[:, :COLS].astype(f32)
    beyond = dstrip_ref[:, COLS : 2 * COLS].astype(f32)
    own = dstrip_ref[:, 2 * COLS :].astype(f32)
    stack_taps(xs, 0, rim_ref[0].astype(f32), roll(beyond, -126), lane)
    stack_taps(xs, 1, rim_ref[1].astype(f32), roll(s, -2), lane)
    for r in range(1, ROWS - 1):
        stack_taps(xs, r + 1, patched(mid_ref[r - 1], own, r, lane), roll(s, -(4 * r + 2)), lane)
    stack_taps(xs, ROWS, rim_ref[2].astype(f32), roll(s, -(4 * ROWS - 2)), lane)
    stack_taps(xs, ROWS + 1, rim_ref[3].astype(f32), roll(beyond, -2), lane)
    weights = wb_ref[...]

    def put(r, back):
        wide[pl.ds(r, CH, stride=ROWS), :] = gr_ref[r].astype(f32) + back

    upper = jnp.where(at_top, wb3_ref[2], wb3_ref[0])
    lower = jnp.where(at_bottom, wb3_ref[0], wb3_ref[2])
    put(0, dot(upper, xs[0]) + dot(wb3_ref[1], xs[1]) + dot(wb3_ref[2], xs[2]))
    end = ROWS - 1
    put(end, dot(wb3_ref[0], xs[end]) + dot(wb3_ref[1], xs[end + 1]) + dot(lower, xs[end + 2]))
    for r in range(1, ROWS - 1, 2):
        window = jnp.concatenate(
            [xs[r : r + 3].reshape(3 * TAPS, COLS), xs[r + 1 : r + 4].reshape(3 * TAPS, COLS)], 1
        )
        back = dot(weights, window)
        put(r, back[:, :COLS])
        put(r + 1, back[:, COLS:])
    write_out(wide, out_hbm, out_ref, sems)


def fold_body(parts_ref, out_ref):
    total = jnp.sum(parts_ref[...], 0)
    if out_ref.shape[1] == 2:
        width = out_ref.shape[2]
        rest = jnp.zeros((1, 2 * width - total.shape[1]), f32)
        total = jnp.concatenate([total, rest], 1)
        total = jnp.concatenate([total[:, :width], total[:, width:]], 0)
    total = total.astype(out_ref.dtype)
    for i in range(out_ref.shape[0]):
        out_ref[i] = total


def unpack_body(parts_ref, out_hbm, out_ref, sems):
    count = parts_ref.shape[0]
    half = parts_ref.shape[2] // COLS
    tiles = []
    for q in range(2 * half):
        tiles.append(parts_ref[:, q // half, pl.ds(q % half * COLS, COLS)].astype(f32))
    copies = []
    for tap in range(9):
        for j in range(CH // count):
            if tap < 8:
                tile, at = tiles[4 * j + tap // 2], tap % 2
            else:
                tile, at = tiles[4 * (CH // count) + j // 2], j % 2
            out_ref[tap, pl.ds(j * count, count), :] = tile[:, at * CH : (at + 1) * CH]
        copies.append(pltpu.make_async_copy(out_ref.at[tap], out_hbm.at[tap], sems.at[tap]))
        copies[-1].start()
    for copy in copies:
        copy.wait()


def outer_pairs(lat_count, lon_count):
    half = lon_count // 2
    pairs = []
    for l in range(lat_count):
        for m in range(lon_count):
            to = l - 1 if l % 2 == 0 else l + 1
            if 0 <= to < lat_count:
                pairs.append((l * lon_count + m, to * lon_count + m))
            else:
                pairs.append((l * lon_count + m, l * lon_count + (m + half) % lon_count))
    return pairs


def on_device(field, kernel, cotangent):
    lat_count = lax.axis_size("lat")
    lon_count = lax.axis_size(LON)
    plane = lax.axis_size(PLANE)
    flat = (CH * ROWS, COLS)
    rows_shape = (ROWS, CH, COLS)

    flat_field, flat_cotangent = field.reshape(flat), cotangent.reshape(flat)
    outer, inner, f_near, g_near = call(
        pack_body,
        [((TAPS, COLS), bf16), ((TAPS, COLS), bf16), (flat, bf16), (flat, bf16)],
        (flat_field, flat_cotangent),
        [pltpu.VMEM(flat, f32), pltpu.SemaphoreType.DMA((2, PIECES))],
        space=pl.ANY,
        limit=52.5,
    )
    outer = lax.ppermute(outer, EVERY, outer_pairs(lat_count, lon_count))
    inner = lax.ppermute(inner, "lat", [(i, i ^ 1) for i in range(lat_count)])
    fr, gr, edge = call(
        turn_body,
        [(rows_shape, bf16), (rows_shape, bf16), ((2 * CH, COLS), bf16)],
        (f_near, g_near),
        [pltpu.VMEM(flat, f32)],
    )

    w3 = jnp.transpose(kernel, (0, 2, 1, 3)).reshape(TAPS, TAPS)
    w = jnp.transpose(kernel, (2, 0, 1, 3)).reshape(CH, 3 * TAPS)
    turned = kernel[::-1, ::-1]
    wb3 = jnp.transpose(turned, (0, 3, 1, 2)).reshape(3, CH, TAPS)
    wb = jnp.transpose(turned, (3, 0, 1, 2)).reshape(CH, 3 * TAPS)
    piece = 9 * CH * CH // plane
    conv_flops = 2 * 9 * CH * CH * ROWS * COLS
    out_mid, delta_mid, grad_mid, token = call(
        interior_body,
        [
            ((ROWS - 2, CH, COLS), bf16),
            ((ROWS - 2, CH, COLS), bf16),
            ((CH, 3 * TAPS), f32),
            ((8, COLS), f32),
        ],
        (fr, gr, w),
        [pltpu.VMEM((ROWS, TAPS, COLS), bf16)],
        2 * conv_flops,
    )

    far, near = call(edge_body, [((CH, COLS), bf16)] * 2, (edge, outer, inner, token))
    swaps = [(i, (i + 1 if i % 2 else i - 1) % lon_count) for i in range(lon_count)]
    far = lax.ppermute(far, LON, swaps)
    near = lax.ppermute(near, "side", [(0, 1), (1, 0)])

    out_rim, out_strip, delta_rim, dstrip, grad = call(
        border_body,
        [
            ((2, CH, COLS), bf16),
            ((CH, COLS), bf16),
            ((4, CH, COLS), bf16),
            ((CH, 3 * COLS), bf16),
            ((plane, 1, piece), f32),
        ],
        (fr, gr, edge, far, near, outer, inner, w, w3, grad_mid),
        [pltpu.VMEM((8, TAPS, COLS), bf16)],
        conv_flops // 4,
    )

    def spread(parts, shape, dtype):
        return call(fold_body, [(shape, dtype)], (parts,))[0]

    writing = [pltpu.VMEM(flat, f32), pltpu.VMEM(flat, bf16), pltpu.SemaphoreType.DMA((PIECES,))]
    parts = lax.all_to_all(grad, PLANE, 0, 0)
    (output,) = call(restore_body, [(flat, bf16)], (out_mid, out_rim, out_strip), writing, out_space=pl.ANY)
    parts = lax.all_to_all(spread(parts, (lax.axis_size("z"), 1, piece), f32), "z", 0, 0)
    (grad_input,) = call(
        backward_body,
        [(flat, bf16)],
        (parts, delta_mid, delta_rim, dstrip, gr, wb, wb3),
        [pltpu.VMEM((ROWS + 2, TAPS, COLS), bf16)] + writing,
        conv_flops,
        out_space=pl.ANY,
    )
    parts = lax.all_to_all(spread(parts, (plane, 2, -(-piece // (2 * COLS)) * COLS), bf16), PLANE, 0, 0)
    (grad_kernel,) = call(
        unpack_body,
        [((9, CH, CH), f32)],
        (parts,),
        [pltpu.VMEM((9, CH, CH), f32), pltpu.SemaphoreType.DMA((9,))],
        out_space=pl.ANY,
    )
    shape = field.shape
    return (output.reshape(shape), grad_input.reshape(shape), grad_kernel.reshape(kernel.shape))


def solution(mesh):
    lat_count, lon_count = mesh.devices.shape
    split = Mesh(mesh.devices.reshape(lat_count, lon_count // 2, 2), EVERY)
    block = P(None, None, "lat", LON)
    return jax.shard_map(
        on_device,
        mesh=split,
        in_specs=(block, P(), block),
        out_specs=(block, block, P()),
        check_vma=False,
    )
```

```python
import math

import jax
import jax.numpy as jnp
from jax import lax
from jax.experimental import pallas as pl
from jax.experimental.pallas import tpu as pltpu
from jax.sharding import Mesh
from jax.sharding import PartitionSpec as P

gelu_scale = math.sqrt(2.0 / math.pi)
ROWS, COLS, CH = 32, 128, 64
TAPS = 3 * CH
PIECES = 4
f32, bf16 = jnp.float32, jnp.bfloat16
LON = ("z", "side")
PLANE = ("lat", "side")
EVERY = ("lat", "z", "side")


def gelu_parts(hidden):
    square = hidden * hidden
    half = 0.5 + 0.5 * jnp.tanh(gelu_scale * hidden * (1.0 + 0.044715 * square))
    steep = gelu_scale * (1.0 + 3.0 * 0.044715 * square)
    return (hidden * half, half + 2.0 * hidden * half * (1.0 - half) * steep)


def roll(x, shift):
    return pltpu.roll(x, shift % x.shape[1], 1)


def lanes(width=COLS):
    return lax.broadcasted_iota(jnp.int32, (CH, width), 1)


def call(body, out_shape, args, scratch=(), flops=0, space=pltpu.VMEM, out_space=pltpu.VMEM, limit=24):
    outs = [jax.ShapeDtypeStruct(s, d) for s, d in out_shape]
    size = sum(a.size * a.dtype.itemsize for a in list(args) + outs)
    return pl.pallas_call(
        body,
        out_shape=outs,
        in_specs=[pl.BlockSpec(memory_space=space)] * len(args),
        out_specs=[pl.BlockSpec(memory_space=out_space if i == 0 else pltpu.VMEM) for i in range(len(outs))],
        scratch_shapes=list(scratch),
        cost_estimate=pl.CostEstimate(flops=flops, bytes_accessed=size, transcendentals=0),
        compiler_params=pltpu.CompilerParams(vmem_limit_bytes=int(limit * 2**20)),
    )(*args)


def pack_body(f_hbm, g_hbm, outer_ref, inner_ref, f_ref, g_ref, wide, sems):
    part = CH * ROWS // PIECES
    copies = [
        [
            pltpu.make_async_copy(src.at[pl.ds(i * part, part)], dst.at[pl.ds(i * part, part)], sems.at[at, i])
            for i in range(PIECES)
        ]
        for at, (src, dst) in enumerate(((f_hbm, f_ref), (g_hbm, g_ref)))
    ]
    for copy in copies[0] + copies[1]:
        copy.start()
    even = lax.axis_index("lat") % 2 == 0
    end = ROWS - 1
    slots = (((0, 0, end), (1, 1, end - 1)), ((2, 0, end),))
    for at, src in enumerate((f_ref, g_ref)):
        for i, copy in enumerate(copies[at]):
            copy.wait()
            wide[pl.ds(i * part, part), :] = src[pl.ds(i * part, part), :].astype(f32)
        for slot, low, high in slots[at]:
            first = wide[pl.ds(low, CH, stride=ROWS), :]
            last = wide[pl.ds(high, CH, stride=ROWS), :]
            outer_ref[pl.ds(slot * CH, CH), :] = jnp.where(even, first, last).astype(bf16)
            inner_ref[pl.ds(slot * CH, CH), :] = jnp.where(even, last, first).astype(bf16)


def turn_body(f_ref, g_ref, fr_ref, gr_ref, edge_ref, wide):
    lane = lanes()
    for at, (src, dst) in enumerate(((f_ref, fr_ref), (g_ref, gr_ref))):
        wide[...] = src[...].astype(f32)
        edge = jnp.zeros((CH, COLS), f32)
        for r in range(ROWS):
            row = wide[pl.ds(r, CH, stride=ROWS), :]
            edge = jnp.where((lane >= 4 * r) & (lane < 4 * r + 4), roll(row, 4 * r + 2), edge)
            dst[r] = row.astype(bf16)
        edge_ref[pl.ds(at * CH, CH), :] = edge.astype(bf16)


def row_halos(outer_ref, inner_ref):
    even = lax.axis_index("lat") % 2 == 0
    north = jnp.where(even, outer_ref[...], inner_ref[...]).astype(f32)
    south = jnp.where(even, inner_ref[...], outer_ref[...]).astype(f32)
    return [half[i * CH : (i + 1) * CH] for half in (north, south) for i in range(3)]


CORNERS = (
    ("s_near", 0, 0), ("s_near", 0, 1), ("s_cot", 0, 2), ("s_far", 4, 0), ("s_far", 4, 1),
    ("n_far", 120, 0), ("n_far", 120, 1), ("n_near", 124, 0), ("n_near", 124, 1), ("n_cot", 124, 2),
)


def edge_body(edge_ref, outer_ref, inner_ref, token_ref, far_ref, near_ref):
    names = ("n_near", "n_far", "n_cot", "s_near", "s_far", "s_cot")
    halos = dict(zip(names, row_halos(outer_ref, inner_ref)))
    kind = lanes() % 4
    lane = lanes()
    field = edge_ref[pl.ds(0, CH), :].astype(f32)
    cot = edge_ref[pl.ds(CH, CH), :].astype(f32)
    east = jnp.where(kind < 2, field, roll(cot, 1))
    west = jnp.where(kind >= 2, field, roll(cot, -1))
    for slot, (row, _, column) in enumerate(CORNERS):
        value = halos[row]
        to = 4 * slot + 3
        east = jnp.where(lane == to, roll(value, to - (126, 127, 127)[column]), east)
        to = 4 * slot
        west = jnp.where(lane == to, roll(value, to - (0, 1, 0)[column]), west)
    even = lax.axis_index("side") == 0
    far_ref[...] = jnp.where(even, west, east).astype(bf16)
    near_ref[...] = jnp.where(even, east, west).astype(bf16)


def column_halos(far_ref, near_ref):
    even = lax.axis_index("side") == 0
    far = far_ref[...].astype(f32)
    near = near_ref[...].astype(f32)
    west = jnp.where(even, far, near)
    east = jnp.where(even, near, far)
    lane = lanes()
    low = lane % 4 < 2
    field = jnp.where(low, west, east)
    cot = jnp.where(low, roll(west, -1), roll(east, 1))
    beyond = [jnp.zeros((CH, COLS), f32), jnp.zeros((CH, COLS), f32)]
    for slot, (_, base, column) in enumerate(CORNERS):
        at = column // 2
        for src, start, to in (
            (west, 4 * slot + 3, base + (0, 1, 1)[column]),
            (east, 4 * slot, base + (2, 3, 2)[column]),
        ):
            beyond[at] = jnp.where(lane == to, roll(src, to - start), beyond[at])
    return field, cot, beyond[0], beyond[1]


def stack_taps(out_ref, at, own, halo, lane):
    out_ref[at, pl.ds(0, CH), :] = roll(jnp.where(lane == COLS - 1, halo, own), 1).astype(bf16)
    out_ref[at, pl.ds(CH, CH), :] = own.astype(bf16)
    out_ref[at, pl.ds(2 * CH, CH), :] = roll(jnp.where(lane == 0, halo, own), -1).astype(bf16)


def dot(a, b):
    return jnp.dot(a, b, preferred_element_type=f32)


def interior_body(fr_ref, gr_ref, w_ref, out_ref, delta_ref, grad_ref, token_ref, xs):
    lane = lanes()
    inner = (lane > 0) & (lane < COLS - 1)
    none = jnp.zeros((CH, COLS), f32)
    for r in range(ROWS):
        stack_taps(xs, r, fr_ref[r].astype(f32), none, lane)
    weights = w_ref[...]
    for r in range(1, ROWS - 1, 2):
        window = jnp.concatenate(
            [xs[r - 1 : r + 2].reshape(3 * TAPS, COLS), xs[r : r + 3].reshape(3 * TAPS, COLS)], 1
        )
        value, slope = gelu_parts(dot(weights, window))
        for k in range(2):
            cut = slice(k * COLS, (k + 1) * COLS)
            out_ref[r + k - 1] = (fr_ref[r + k].astype(f32) + value[:, cut]).astype(bf16)
            delta = gr_ref[r + k].astype(f32) * slope[:, cut]
            delta_ref[r + k - 1] = jnp.where(inner, delta, 0.0).astype(bf16)
    total = None
    group = 10
    for r in range(0, ROWS - 2, group):
        left = jnp.concatenate([delta_ref[r + k] for k in range(group)], 1)
        right = jnp.concatenate([xs[r + k : r + k + 3].reshape(3 * TAPS, COLS) for k in range(group)], 1)
        term = dot_lanes(left, right)
        total = term if total is None else total + term
    grad_ref[...] = total
    token_ref[...] = jnp.zeros(token_ref.shape, f32)


def dot_lanes(a, b):
    return lax.dot_general(a, b, (((1,), (1,)), ((), ())), preferred_element_type=f32)


def border_body(
    fr_ref, gr_ref, edge_ref, far_ref, near_ref, outer_ref, inner_ref, w_ref, wa_ref, part_ref,
    out_ref, outstrip_ref, delta_ref, dstrip_ref, grad_ref, xs,
):
    lat = lax.axis_index("lat")
    at_top = lat == 0
    at_bottom = lat == lax.axis_size("lat") - 1
    lane = lanes()
    n_near, n_far, n_cot, s_near, s_far, s_cot = row_halos(outer_ref, inner_ref)

    s, gs, beyond, gbeyond = column_halos(far_ref, near_ref)

    end = ROWS - 1
    stack_taps(xs, 0, n_far, roll(beyond, -122), lane)
    stack_taps(xs, 1, n_near, roll(beyond, -126), lane)
    for at, r in ((2, 0), (3, 1), (4, end - 1), (5, end)):
        stack_taps(xs, at, fr_ref[r].astype(f32), roll(s, -(4 * r + 2)), lane)
    stack_taps(xs, 6, s_near, roll(beyond, -2), lane)
    stack_taps(xs, 7, s_far, roll(beyond, -6), lane)

    weights = w_ref[...]
    window = jnp.concatenate([xs[1:4].reshape(3 * TAPS, COLS), xs[4:7].reshape(3 * TAPS, COLS)], 1)
    value, slope = gelu_parts(dot(weights, window))
    deltas = []
    for k, r in enumerate((0, end)):
        cut = slice(k * COLS, (k + 1) * COLS)
        out_ref[k] = (fr_ref[r].astype(f32) + value[:, cut]).astype(bf16)
        deltas.append((gr_ref[r].astype(f32) * slope[:, cut]).astype(bf16))
        delta_ref[k + 1] = deltas[k]

    def turned(flip, low):
        first = jnp.where(flip, xs[low + 2], xs[low])
        last = jnp.where(flip, xs[low], xs[low + 2])
        return jnp.concatenate([first, xs[low + 1], last], 0)

    outside = jnp.concatenate([turned(at_top, 0), turned(at_bottom, 5)], 1)
    slope = gelu_parts(dot(weights, outside))[1]
    delta_ref[0] = (n_cot * slope[:, :COLS]).astype(bf16)
    delta_ref[3] = (s_cot * slope[:, COLS:]).astype(bf16)

    edge = edge_ref[pl.ds(0, CH), :].astype(f32)
    halo = jnp.concatenate([s, beyond], 1)
    low = jnp.where(lane < 4, roll(s_near, 2), roll(s_far, 6))
    high = jnp.where(lane >= 124, roll(n_near, 126), roll(n_far, 122))
    own = jnp.concatenate([edge, jnp.where(lane < 64, low, high)], 1)
    wide_lane = lanes(2 * COLS)
    kind = wide_lane % 4
    small = lane % 4
    outer_taps = jnp.concatenate(
        [roll(jnp.where(kind == 0, halo, own), 1), halo, roll(jnp.where(kind == 3, halo, own), -1)], 0
    )
    inner_taps = jnp.concatenate(
        [roll(jnp.where(small == 1, s, edge), 1), edge, roll(jnp.where(small == 2, s, edge), -1)], 0
    )
    y = dot(wa_ref[...], jnp.concatenate([outer_taps, inner_taps], 1).astype(bf16))
    y0, y1, y2 = [y[i * CH : (i + 1) * CH, : 2 * COLS] for i in range(3)]
    straight = roll(y0, 4) + y1 + roll(y2, -4)
    backward = roll(y2, 4) + y1 + roll(y0, -4)
    flip = ((wide_lane >= 252) & at_top) | ((wide_lane >= 128) & (wide_lane < 132) & at_bottom)
    y0, y1, y2 = [y[i * CH : (i + 1) * CH, 2 * COLS :] for i in range(3)]
    packed = [jnp.where(flip, backward, straight), roll(y0, 4) + y1 + roll(y2, -4)]
    value, slope = gelu_parts(jnp.concatenate(packed, 1))
    own_cot = edge_ref[pl.ds(CH, CH), :].astype(f32)
    outstrip_ref[...] = (edge + value[:, 2 * COLS :]).astype(bf16)
    dstrip = jnp.concatenate([gs, gbeyond, own_cot], 1) * slope
    dstrip_ref[...] = dstrip.astype(bf16)

    used = ((small == 1) | (small == 2)) & (lane >= 4) & (lane < 4 * end)
    side = jnp.where(used, dstrip[:, 2 * COLS :], 0.0).astype(bf16)
    shifted = jnp.concatenate([roll(inner_taps, 4), inner_taps, roll(inner_taps, -4)], 0).astype(bf16)
    left = jnp.concatenate([deltas[0], deltas[1], side], 1)
    total = part_ref[...] + dot_lanes(left, jnp.concatenate([window, shifted], 1))
    total = total * grad_scale()
    count = grad_ref.shape[0]
    pieces = []
    for p in range(5):
        piece = total[:, p * COLS : (p + 1) * COLS]
        pieces.append([piece[j * count : (j + 1) * count] for j in range(CH // count)])
    tiles = [piece[j] for j in range(CH // count) for piece in pieces[:4]]
    last = pieces[4]
    for j in range(0, len(last), 2):
        tiles.append(jnp.concatenate(last[j : j + 2], 1))
    for q, tile in enumerate(tiles):
        grad_ref[:, 0, pl.ds(q * COLS, COLS)] = tile


def patched(row, packed, r, lane):
    return jnp.where((lane == 0) | (lane == COLS - 1), roll(packed, -(4 * r + 2)), row.astype(f32))


def write_out(wide, out_hbm, out_ref, sems):
    part = CH * ROWS // PIECES
    copies = []
    for i in range(PIECES):
        at = pl.ds(i * part, part)
        out_ref[at, :] = wide[at, :].astype(bf16)
        copies.append(pltpu.make_async_copy(out_ref.at[at], out_hbm.at[at], sems.at[i]))
        copies[-1].start()
    for copy in copies:
        copy.wait()


def restore_body(mid_ref, rim_ref, strip_ref, out_hbm, token_ref, wide, out_ref, sems):
    lane = lanes()
    packed = strip_ref[...].astype(f32)
    wide[pl.ds(0, CH, stride=ROWS), :] = rim_ref[0].astype(f32)
    for r in range(1, ROWS - 1):
        wide[pl.ds(r, CH, stride=ROWS), :] = patched(mid_ref[r - 1], packed, r, lane)
    wide[pl.ds(ROWS - 1, CH, stride=ROWS), :] = rim_ref[1].astype(f32)
    write_out(wide, out_hbm, out_ref, sems)
    token_ref[...] = jnp.zeros(token_ref.shape, f32)


def grad_scale():
    return float(ROWS * COLS * lax.axis_size(EVERY)) ** (-0.5)


def backward_body(after_ref, mid_ref, rim_ref, dstrip_ref, gr_ref, wb_ref, wb3_ref, out_hbm, token_ref, xs, wide, out_ref, sems):
    lat = lax.axis_index("lat")
    at_top = lat == 0
    at_bottom = lat == lax.axis_size("lat") - 1
    lane = lanes()
    s = dstrip_ref[:, :COLS].astype(f32)
    beyond = dstrip_ref[:, COLS : 2 * COLS].astype(f32)
    own = dstrip_ref[:, 2 * COLS :].astype(f32)
    stack_taps(xs, 0, rim_ref[0].astype(f32), roll(beyond, -126), lane)
    stack_taps(xs, 1, rim_ref[1].astype(f32), roll(s, -2), lane)
    for r in range(1, ROWS - 1):
        stack_taps(xs, r + 1, patched(mid_ref[r - 1], own, r, lane), roll(s, -(4 * r + 2)), lane)
    stack_taps(xs, ROWS, rim_ref[2].astype(f32), roll(s, -(4 * ROWS - 2)), lane)
    stack_taps(xs, ROWS + 1, rim_ref[3].astype(f32), roll(beyond, -2), lane)
    weights = wb_ref[...]

    def put(r, back):
        wide[pl.ds(r, CH, stride=ROWS), :] = gr_ref[r].astype(f32) + back

    upper = jnp.where(at_top, wb3_ref[2], wb3_ref[0])
    lower = jnp.where(at_bottom, wb3_ref[0], wb3_ref[2])
    put(0, dot(upper, xs[0]) + dot(wb3_ref[1], xs[1]) + dot(wb3_ref[2], xs[2]))
    end = ROWS - 1
    put(end, dot(wb3_ref[0], xs[end]) + dot(wb3_ref[1], xs[end + 1]) + dot(lower, xs[end + 2]))
    for r in range(1, ROWS - 1, 2):
        window = jnp.concatenate(
            [xs[r : r + 3].reshape(3 * TAPS, COLS), xs[r + 1 : r + 4].reshape(3 * TAPS, COLS)], 1
        )
        back = dot(weights, window)
        put(r, back[:, :COLS])
        put(r + 1, back[:, COLS:])
    write_out(wide, out_hbm, out_ref, sems)
    token_ref[...] = jnp.zeros(token_ref.shape, f32)


def fold_body(parts_ref, token_ref, out_ref):
    total = jnp.sum(parts_ref[...], 0)
    if out_ref.shape[1] == 2:
        width = out_ref.shape[2]
        rest = jnp.zeros((1, 2 * width - total.shape[1]), f32)
        total = jnp.concatenate([total, rest], 1)
        total = jnp.concatenate([total[:, :width], total[:, width:]], 0)
    total = total.astype(out_ref.dtype)
    for i in range(out_ref.shape[0]):
        out_ref[i] = total


def unpack_body(parts_ref, out_hbm, out_ref, sems):
    count = parts_ref.shape[0]
    half = parts_ref.shape[2] // COLS
    tiles = []
    for q in range(2 * half):
        tiles.append(parts_ref[:, q // half, pl.ds(q % half * COLS, COLS)].astype(f32))
    copies = []
    for tap in range(9):
        for j in range(CH // count):
            if tap < 8:
                tile, at = tiles[4 * j + tap // 2], tap % 2
            else:
                tile, at = tiles[4 * (CH // count) + j // 2], j % 2
            out_ref[tap, pl.ds(j * count, count), :] = tile[:, at * CH : (at + 1) * CH]
        copies.append(pltpu.make_async_copy(out_ref.at[tap], out_hbm.at[tap], sems.at[tap]))
        copies[-1].start()
    for copy in copies:
        copy.wait()


def outer_pairs(lat_count, lon_count):
    half = lon_count // 2
    pairs = []
    for l in range(lat_count):
        for m in range(lon_count):
            to = l - 1 if l % 2 == 0 else l + 1
            if 0 <= to < lat_count:
                pairs.append((l * lon_count + m, to * lon_count + m))
            else:
                pairs.append((l * lon_count + m, l * lon_count + (m + half) % lon_count))
    return pairs


def on_device(field, kernel, cotangent):
    lat_count = lax.axis_size("lat")
    lon_count = lax.axis_size(LON)
    plane = lax.axis_size(PLANE)
    flat = (CH * ROWS, COLS)
    rows_shape = (ROWS, CH, COLS)

    flat_field, flat_cotangent = field.reshape(flat), cotangent.reshape(flat)
    outer, inner, f_near, g_near = call(
        pack_body,
        [((TAPS, COLS), bf16), ((TAPS, COLS), bf16), (flat, bf16), (flat, bf16)],
        (flat_field, flat_cotangent),
        [pltpu.VMEM(flat, f32), pltpu.SemaphoreType.DMA((2, PIECES))],
        space=pl.ANY,
        limit=52.5,
    )
    outer = lax.ppermute(outer, EVERY, outer_pairs(lat_count, lon_count))
    inner = lax.ppermute(inner, "lat", [(i, i ^ 1) for i in range(lat_count)])
    fr, gr, edge = call(
        turn_body,
        [(rows_shape, bf16), (rows_shape, bf16), ((2 * CH, COLS), bf16)],
        (f_near, g_near),
        [pltpu.VMEM(flat, f32)],
    )

    w3 = jnp.transpose(kernel, (0, 2, 1, 3)).reshape(TAPS, TAPS)
    w = jnp.transpose(kernel, (2, 0, 1, 3)).reshape(CH, 3 * TAPS)
    turned = kernel[::-1, ::-1]
    wb3 = jnp.transpose(turned, (0, 3, 1, 2)).reshape(3, CH, TAPS)
    wb = jnp.transpose(turned, (3, 0, 1, 2)).reshape(CH, 3 * TAPS)
    piece = 9 * CH * CH // plane
    conv_flops = 2 * 9 * CH * CH * ROWS * COLS
    out_mid, delta_mid, grad_mid, token = call(
        interior_body,
        [
            ((ROWS - 2, CH, COLS), bf16),
            ((ROWS - 2, CH, COLS), bf16),
            ((CH, 3 * TAPS), f32),
            ((8, COLS), f32),
        ],
        (fr, gr, w),
        [pltpu.VMEM((ROWS, TAPS, COLS), bf16)],
        2 * conv_flops,
    )

    far, near = call(edge_body, [((CH, COLS), bf16)] * 2, (edge, outer, inner, token))
    swaps = [(i, (i + 1 if i % 2 else i - 1) % lon_count) for i in range(lon_count)]
    far = lax.ppermute(far, LON, swaps)
    near = lax.ppermute(near, "side", [(0, 1), (1, 0)])

    out_rim, out_strip, delta_rim, dstrip, grad = call(
        border_body,
        [
            ((2, CH, COLS), bf16),
            ((CH, COLS), bf16),
            ((4, CH, COLS), bf16),
            ((CH, 3 * COLS), bf16),
            ((plane, 1, piece), f32),
        ],
        (fr, gr, edge, far, near, outer, inner, w, w3, grad_mid),
        [pltpu.VMEM((8, TAPS, COLS), bf16)],
        conv_flops // 4,
    )

    def spread(parts, done, shape, dtype):
        return call(fold_body, [(shape, dtype)], (parts, done))[0]

    token = ((8, COLS), f32)
    writing = [pltpu.VMEM(flat, f32), pltpu.VMEM(flat, bf16), pltpu.SemaphoreType.DMA((PIECES,))]
    parts = lax.all_to_all(grad, PLANE, 0, 0)
    output, done = call(
        restore_body, [(flat, bf16), token], (out_mid, out_rim, out_strip), writing, out_space=pl.ANY
    )
    deep = spread(parts, done, (lax.axis_size("z"), 1, piece), f32)
    grad_input, done = call(
        backward_body,
        [(flat, bf16), token],
        (parts, delta_mid, delta_rim, dstrip, gr, wb, wb3),
        [pltpu.VMEM((ROWS + 2, TAPS, COLS), bf16)] + writing,
        conv_flops,
        out_space=pl.ANY,
    )
    parts = lax.all_to_all(deep, "z", 0, 0)
    parts = spread(parts, done, (plane, 2, -(-piece // (2 * COLS)) * COLS), bf16)
    parts = lax.all_to_all(parts, PLANE, 0, 0)
    (grad_kernel,) = call(
        unpack_body,
        [((9, CH, CH), f32)],
        (parts,),
        [pltpu.VMEM((9, CH, CH), f32), pltpu.SemaphoreType.DMA((9,))],
        out_space=pl.ANY,
    )
    shape = field.shape
    return (output.reshape(shape), grad_input.reshape(shape), grad_kernel.reshape(kernel.shape))


def solution(mesh):
    lat_count, lon_count = mesh.devices.shape
    split = Mesh(mesh.devices.reshape(lat_count, lon_count // 2, 2), EVERY)
    block = P(None, None, "lat", LON)
    return jax.shard_map(
        on_device,
        mesh=split,
        in_specs=(block, P(), block),
        out_specs=(block, block, P()),
        check_vma=False,
    )
```

```python
import math

import jax
import jax.numpy as jnp
from jax import lax
from jax.experimental import pallas as pl
from jax.experimental.pallas import tpu as pltpu
from jax.sharding import Mesh
from jax.sharding import PartitionSpec as P

gelu_scale = math.sqrt(2.0 / math.pi)
ROWS, COLS, CH = 32, 128, 64
TAPS = 3 * CH
PIECES = 4
f32, bf16 = jnp.float32, jnp.bfloat16
LON = ("z", "side")
PLANE = ("lat", "side")
EVERY = ("lat", "z", "side")


def gelu_parts(hidden):
    square = hidden * hidden
    half = 0.5 + 0.5 * jnp.tanh(gelu_scale * hidden * (1.0 + 0.044715 * square))
    steep = gelu_scale * (1.0 + 3.0 * 0.044715 * square)
    return (hidden * half, half + 2.0 * hidden * half * (1.0 - half) * steep)


def roll(x, shift):
    return pltpu.roll(x, shift % x.shape[1], 1)


def lanes(width=COLS):
    return lax.broadcasted_iota(jnp.int32, (CH, width), 1)


def call(body, out_shape, args, scratch=(), flops=0, space=pltpu.VMEM, out_space=pltpu.VMEM, limit=24):
    outs = [jax.ShapeDtypeStruct(s, d) for s, d in out_shape]
    size = sum(a.size * a.dtype.itemsize for a in list(args) + outs)
    return pl.pallas_call(
        body,
        out_shape=outs,
        in_specs=[pl.BlockSpec(memory_space=space)] * len(args),
        out_specs=[pl.BlockSpec(memory_space=out_space)] * len(outs),
        scratch_shapes=list(scratch),
        cost_estimate=pl.CostEstimate(flops=flops, bytes_accessed=size, transcendentals=0),
        compiler_params=pltpu.CompilerParams(vmem_limit_bytes=int(limit * 2**20)),
    )(*args)


def pack_body(f_hbm, g_hbm, outer_ref, inner_ref, f_ref, g_ref, wide, sems):
    part = CH * ROWS // PIECES
    copies = [
        [
            pltpu.make_async_copy(src.at[pl.ds(i * part, part)], dst.at[pl.ds(i * part, part)], sems.at[at, i])
            for i in range(PIECES)
        ]
        for at, (src, dst) in enumerate(((f_hbm, f_ref), (g_hbm, g_ref)))
    ]
    for copy in copies[0] + copies[1]:
        copy.start()
    even = lax.axis_index("lat") % 2 == 0
    end = ROWS - 1
    slots = (((0, 0, end), (1, 1, end - 1)), ((2, 0, end),))
    for at, src in enumerate((f_ref, g_ref)):
        for i, copy in enumerate(copies[at]):
            copy.wait()
            wide[pl.ds(i * part, part), :] = src[pl.ds(i * part, part), :].astype(f32)
        for slot, low, high in slots[at]:
            first = wide[pl.ds(low, CH, stride=ROWS), :]
            last = wide[pl.ds(high, CH, stride=ROWS), :]
            outer_ref[pl.ds(slot * CH, CH), :] = jnp.where(even, first, last).astype(bf16)
            inner_ref[pl.ds(slot * CH, CH), :] = jnp.where(even, last, first).astype(bf16)


def turn_body(f_ref, g_ref, fr_ref, gr_ref, edge_ref, wide):
    lane = lanes()
    for at, (src, dst) in enumerate(((f_ref, fr_ref), (g_ref, gr_ref))):
        wide[...] = src[...].astype(f32)
        edge = jnp.zeros((CH, COLS), f32)
        for r in range(ROWS):
            row = wide[pl.ds(r, CH, stride=ROWS), :]
            edge = jnp.where((lane >= 4 * r) & (lane < 4 * r + 4), roll(row, 4 * r + 2), edge)
            dst[r] = row.astype(bf16)
        edge_ref[pl.ds(at * CH, CH), :] = edge.astype(bf16)


def row_halos(outer_ref, inner_ref):
    even = lax.axis_index("lat") % 2 == 0
    north = jnp.where(even, outer_ref[...], inner_ref[...]).astype(f32)
    south = jnp.where(even, inner_ref[...], outer_ref[...]).astype(f32)
    return [half[i * CH : (i + 1) * CH] for half in (north, south) for i in range(3)]


CORNERS = (
    ("s_near", 0, 0), ("s_near", 0, 1), ("s_cot", 0, 2), ("s_far", 4, 0), ("s_far", 4, 1),
    ("n_far", 120, 0), ("n_far", 120, 1), ("n_near", 124, 0), ("n_near", 124, 1), ("n_cot", 124, 2),
)


def edge_body(edge_ref, outer_ref, inner_ref, token_ref, far_ref, near_ref):
    names = ("n_near", "n_far", "n_cot", "s_near", "s_far", "s_cot")
    halos = dict(zip(names, row_halos(outer_ref, inner_ref)))
    kind = lanes() % 4
    lane = lanes()
    field = edge_ref[pl.ds(0, CH), :].astype(f32)
    cot = edge_ref[pl.ds(CH, CH), :].astype(f32)
    east = jnp.where(kind < 2, field, roll(cot, 1))
    west = jnp.where(kind >= 2, field, roll(cot, -1))
    for slot, (row, _, column) in enumerate(CORNERS):
        value = halos[row]
        to = 4 * slot + 3
        east = jnp.where(lane == to, roll(value, to - (126, 127, 127)[column]), east)
        to = 4 * slot
        west = jnp.where(lane == to, roll(value, to - (0, 1, 0)[column]), west)
    even = lax.axis_index("side") == 0
    far_ref[...] = jnp.where(even, west, east).astype(bf16)
    near_ref[...] = jnp.where(even, east, west).astype(bf16)


def column_halos(far_ref, near_ref):
    even = lax.axis_index("side") == 0
    far = far_ref[...].astype(f32)
    near = near_ref[...].astype(f32)
    west = jnp.where(even, far, near)
    east = jnp.where(even, near, far)
    lane = lanes()
    low = lane % 4 < 2
    field = jnp.where(low, west, east)
    cot = jnp.where(low, roll(west, -1), roll(east, 1))
    beyond = [jnp.zeros((CH, COLS), f32), jnp.zeros((CH, COLS), f32)]
    for slot, (_, base, column) in enumerate(CORNERS):
        at = column // 2
        for src, start, to in (
            (west, 4 * slot + 3, base + (0, 1, 1)[column]),
            (east, 4 * slot, base + (2, 3, 2)[column]),
        ):
            beyond[at] = jnp.where(lane == to, roll(src, to - start), beyond[at])
    return field, cot, beyond[0], beyond[1]


def stack_taps(out_ref, at, own, halo, lane):
    out_ref[at, pl.ds(0, CH), :] = roll(jnp.where(lane == COLS - 1, halo, own), 1).astype(bf16)
    out_ref[at, pl.ds(CH, CH), :] = own.astype(bf16)
    out_ref[at, pl.ds(2 * CH, CH), :] = roll(jnp.where(lane == 0, halo, own), -1).astype(bf16)


def dot(a, b):
    return jnp.dot(a, b, preferred_element_type=f32)


def interior_body(fr_ref, gr_ref, w_ref, out_ref, delta_ref, grad_ref, token_ref, xs):
    lane = lanes()
    inner = (lane > 0) & (lane < COLS - 1)
    none = jnp.zeros((CH, COLS), f32)
    for r in range(ROWS):
        stack_taps(xs, r, fr_ref[r].astype(f32), none, lane)
    weights = w_ref[...]
    for r in range(1, ROWS - 1, 2):
        window = jnp.concatenate(
            [xs[r - 1 : r + 2].reshape(3 * TAPS, COLS), xs[r : r + 3].reshape(3 * TAPS, COLS)], 1
        )
        value, slope = gelu_parts(dot(weights, window))
        for k in range(2):
            cut = slice(k * COLS, (k + 1) * COLS)
            out_ref[r + k - 1] = (fr_ref[r + k].astype(f32) + value[:, cut]).astype(bf16)
            delta = gr_ref[r + k].astype(f32) * slope[:, cut]
            delta_ref[r + k - 1] = jnp.where(inner, delta, 0.0).astype(bf16)
    total = None
    group = 10
    for r in range(0, ROWS - 2, group):
        left = jnp.concatenate([delta_ref[r + k] for k in range(group)], 1)
        right = jnp.concatenate([xs[r + k : r + k + 3].reshape(3 * TAPS, COLS) for k in range(group)], 1)
        term = dot_lanes(left, right)
        total = term if total is None else total + term
    grad_ref[...] = total
    token_ref[...] = jnp.zeros(token_ref.shape, f32)


def dot_lanes(a, b):
    return lax.dot_general(a, b, (((1,), (1,)), ((), ())), preferred_element_type=f32)


def border_body(
    fr_ref, gr_ref, edge_ref, far_ref, near_ref, outer_ref, inner_ref, w_ref, wa_ref, part_ref,
    out_ref, outstrip_ref, delta_ref, dstrip_ref, grad_ref, xs,
):
    lat = lax.axis_index("lat")
    at_top = lat == 0
    at_bottom = lat == lax.axis_size("lat") - 1
    lane = lanes()
    n_near, n_far, n_cot, s_near, s_far, s_cot = row_halos(outer_ref, inner_ref)

    s, gs, beyond, gbeyond = column_halos(far_ref, near_ref)

    end = ROWS - 1
    stack_taps(xs, 0, n_far, roll(beyond, -122), lane)
    stack_taps(xs, 1, n_near, roll(beyond, -126), lane)
    for at, r in ((2, 0), (3, 1), (4, end - 1), (5, end)):
        stack_taps(xs, at, fr_ref[r].astype(f32), roll(s, -(4 * r + 2)), lane)
    stack_taps(xs, 6, s_near, roll(beyond, -2), lane)
    stack_taps(xs, 7, s_far, roll(beyond, -6), lane)

    weights = w_ref[...]
    window = jnp.concatenate([xs[1:4].reshape(3 * TAPS, COLS), xs[4:7].reshape(3 * TAPS, COLS)], 1)
    value, slope = gelu_parts(dot(weights, window))
    deltas = []
    for k, r in enumerate((0, end)):
        cut = slice(k * COLS, (k + 1) * COLS)
        out_ref[k] = (fr_ref[r].astype(f32) + value[:, cut]).astype(bf16)
        deltas.append((gr_ref[r].astype(f32) * slope[:, cut]).astype(bf16))
        delta_ref[k + 1] = deltas[k]

    def turned(flip, low):
        first = jnp.where(flip, xs[low + 2], xs[low])
        last = jnp.where(flip, xs[low], xs[low + 2])
        return jnp.concatenate([first, xs[low + 1], last], 0)

    outside = jnp.concatenate([turned(at_top, 0), turned(at_bottom, 5)], 1)
    slope = gelu_parts(dot(weights, outside))[1]
    delta_ref[0] = (n_cot * slope[:, :COLS]).astype(bf16)
    delta_ref[3] = (s_cot * slope[:, COLS:]).astype(bf16)

    edge = edge_ref[pl.ds(0, CH), :].astype(f32)
    halo = jnp.concatenate([s, beyond], 1)
    low = jnp.where(lane < 4, roll(s_near, 2), roll(s_far, 6))
    high = jnp.where(lane >= 124, roll(n_near, 126), roll(n_far, 122))
    own = jnp.concatenate([edge, jnp.where(lane < 64, low, high)], 1)
    wide_lane = lanes(2 * COLS)
    kind = wide_lane % 4
    small = lane % 4
    outer_taps = jnp.concatenate(
        [roll(jnp.where(kind == 0, halo, own), 1), halo, roll(jnp.where(kind == 3, halo, own), -1)], 0
    )
    inner_taps = jnp.concatenate(
        [roll(jnp.where(small == 1, s, edge), 1), edge, roll(jnp.where(small == 2, s, edge), -1)], 0
    )
    y = dot(wa_ref[...], jnp.concatenate([outer_taps, inner_taps], 1).astype(bf16))
    y0, y1, y2 = [y[i * CH : (i + 1) * CH, : 2 * COLS] for i in range(3)]
    straight = roll(y0, 4) + y1 + roll(y2, -4)
    backward = roll(y2, 4) + y1 + roll(y0, -4)
    flip = ((wide_lane >= 252) & at_top) | ((wide_lane >= 128) & (wide_lane < 132) & at_bottom)
    y0, y1, y2 = [y[i * CH : (i + 1) * CH, 2 * COLS :] for i in range(3)]
    packed = [jnp.where(flip, backward, straight), roll(y0, 4) + y1 + roll(y2, -4)]
    value, slope = gelu_parts(jnp.concatenate(packed, 1))
    own_cot = edge_ref[pl.ds(CH, CH), :].astype(f32)
    outstrip_ref[...] = (edge + value[:, 2 * COLS :]).astype(bf16)
    dstrip = jnp.concatenate([gs, gbeyond, own_cot], 1) * slope
    dstrip_ref[...] = dstrip.astype(bf16)

    used = ((small == 1) | (small == 2)) & (lane >= 4) & (lane < 4 * end)
    side = jnp.where(used, dstrip[:, 2 * COLS :], 0.0).astype(bf16)
    shifted = jnp.concatenate([roll(inner_taps, 4), inner_taps, roll(inner_taps, -4)], 0).astype(bf16)
    left = jnp.concatenate([deltas[0], deltas[1], side], 1)
    total = part_ref[...] + dot_lanes(left, jnp.concatenate([window, shifted], 1))
    total = total * grad_scale()
    count = grad_ref.shape[0]
    pieces = []
    for p in range(5):
        piece = total[:, p * COLS : (p + 1) * COLS]
        pieces.append([piece[j * count : (j + 1) * count] for j in range(CH // count)])
    tiles = [piece[j] for j in range(CH // count) for piece in pieces[:4]]
    last = pieces[4]
    for j in range(0, len(last), 2):
        tiles.append(jnp.concatenate(last[j : j + 2], 1))
    for q, tile in enumerate(tiles):
        grad_ref[:, 0, pl.ds(q * COLS, COLS)] = tile


def patched(row, packed, r, lane):
    return jnp.where((lane == 0) | (lane == COLS - 1), roll(packed, -(4 * r + 2)), row.astype(f32))


def write_out(wide, out_hbm, out_ref, sems):
    part = CH * ROWS // PIECES
    copies = []
    for i in range(PIECES):
        at = pl.ds(i * part, part)
        out_ref[at, :] = wide[at, :].astype(bf16)
        copies.append(pltpu.make_async_copy(out_ref.at[at], out_hbm.at[at], sems.at[i]))
        copies[-1].start()
    for copy in copies:
        copy.wait()


def restore_body(mid_ref, rim_ref, strip_ref, out_hbm, wide, out_ref, sems):
    lane = lanes()
    packed = strip_ref[...].astype(f32)
    wide[pl.ds(0, CH, stride=ROWS), :] = rim_ref[0].astype(f32)
    for r in range(1, ROWS - 1):
        wide[pl.ds(r, CH, stride=ROWS), :] = patched(mid_ref[r - 1], packed, r, lane)
    wide[pl.ds(ROWS - 1, CH, stride=ROWS), :] = rim_ref[1].astype(f32)
    write_out(wide, out_hbm, out_ref, sems)


def grad_scale():
    return float(ROWS * COLS * lax.axis_size(EVERY)) ** (-0.5)


def backward_body(after_ref, mid_ref, rim_ref, dstrip_ref, gr_ref, wb_ref, wb3_ref, out_hbm, xs, wide, out_ref, sems):
    lat = lax.axis_index("lat")
    at_top = lat == 0
    at_bottom = lat == lax.axis_size("lat") - 1
    lane = lanes()
    s = dstrip_ref[:, :COLS].astype(f32)
    beyond = dstrip_ref[:, COLS : 2 * COLS].astype(f32)
    own = dstrip_ref[:, 2 * COLS :].astype(f32)
    stack_taps(xs, 0, rim_ref[0].astype(f32), roll(beyond, -126), lane)
    stack_taps(xs, 1, rim_ref[1].astype(f32), roll(s, -2), lane)
    for r in range(1, ROWS - 1):
        stack_taps(xs, r + 1, patched(mid_ref[r - 1], own, r, lane), roll(s, -(4 * r + 2)), lane)
    stack_taps(xs, ROWS, rim_ref[2].astype(f32), roll(s, -(4 * ROWS - 2)), lane)
    stack_taps(xs, ROWS + 1, rim_ref[3].astype(f32), roll(beyond, -2), lane)
    weights = wb_ref[...]

    def put(r, back):
        wide[pl.ds(r, CH, stride=ROWS), :] = gr_ref[r].astype(f32) + back

    upper = jnp.where(at_top, wb3_ref[2], wb3_ref[0])
    lower = jnp.where(at_bottom, wb3_ref[0], wb3_ref[2])
    put(0, dot(upper, xs[0]) + dot(wb3_ref[1], xs[1]) + dot(wb3_ref[2], xs[2]))
    end = ROWS - 1
    put(end, dot(wb3_ref[0], xs[end]) + dot(wb3_ref[1], xs[end + 1]) + dot(lower, xs[end + 2]))
    for r in range(1, ROWS - 1, 2):
        window = jnp.concatenate(
            [xs[r : r + 3].reshape(3 * TAPS, COLS), xs[r + 1 : r + 4].reshape(3 * TAPS, COLS)], 1
        )
        back = dot(weights, window)
        put(r, back[:, :COLS])
        put(r + 1, back[:, COLS:])
    write_out(wide, out_hbm, out_ref, sems)


def fold_body(parts_ref, out_ref):
    total = jnp.sum(parts_ref[...], 0)
    if out_ref.shape[1] == 2:
        width = out_ref.shape[2]
        rest = jnp.zeros((1, 2 * width - total.shape[1]), f32)
        total = jnp.concatenate([total, rest], 1)
        total = jnp.concatenate([total[:, :width], total[:, width:]], 0)
    total = total.astype(out_ref.dtype)
    for i in range(out_ref.shape[0]):
        out_ref[i] = total


def unpack_body(parts_ref, out_hbm, out_ref, sems):
    count = parts_ref.shape[0]
    half = parts_ref.shape[2] // COLS
    tiles = []
    for q in range(2 * half):
        tiles.append(parts_ref[:, q // half, pl.ds(q % half * COLS, COLS)].astype(f32))
    copies = []
    for tap in range(9):
        for j in range(CH // count):
            if tap < 8:
                tile, at = tiles[4 * j + tap // 2], tap % 2
            else:
                tile, at = tiles[4 * (CH // count) + j // 2], j % 2
            out_ref[tap, pl.ds(j * count, count), :] = tile[:, at * CH : (at + 1) * CH]
        copies.append(pltpu.make_async_copy(out_ref.at[tap], out_hbm.at[tap], sems.at[tap]))
        copies[-1].start()
    for copy in copies:
        copy.wait()


def outer_pairs(lat_count, lon_count):
    half = lon_count // 2
    pairs = []
    for l in range(lat_count):
        for m in range(lon_count):
            to = l - 1 if l % 2 == 0 else l + 1
            if 0 <= to < lat_count:
                pairs.append((l * lon_count + m, to * lon_count + m))
            else:
                pairs.append((l * lon_count + m, l * lon_count + (m + half) % lon_count))
    return pairs


def on_device(field, kernel, cotangent):
    lat_count = lax.axis_size("lat")
    lon_count = lax.axis_size(LON)
    plane = lax.axis_size(PLANE)
    flat = (CH * ROWS, COLS)
    rows_shape = (ROWS, CH, COLS)

    flat_field, flat_cotangent = field.reshape(flat), cotangent.reshape(flat)
    outer, inner, f_near, g_near = call(
        pack_body,
        [((TAPS, COLS), bf16), ((TAPS, COLS), bf16), (flat, bf16), (flat, bf16)],
        (flat_field, flat_cotangent),
        [pltpu.VMEM(flat, f32), pltpu.SemaphoreType.DMA((2, PIECES))],
        space=pl.ANY,
        limit=52.5,
    )
    outer = lax.ppermute(outer, EVERY, outer_pairs(lat_count, lon_count))
    inner = lax.ppermute(inner, "lat", [(i, i ^ 1) for i in range(lat_count)])
    fr, gr, edge = call(
        turn_body,
        [(rows_shape, bf16), (rows_shape, bf16), ((2 * CH, COLS), bf16)],
        (f_near, g_near),
        [pltpu.VMEM(flat, f32)],
    )

    w3 = jnp.transpose(kernel, (0, 2, 1, 3)).reshape(TAPS, TAPS)
    w = jnp.transpose(kernel, (2, 0, 1, 3)).reshape(CH, 3 * TAPS)
    turned = kernel[::-1, ::-1]
    wb3 = jnp.transpose(turned, (0, 3, 1, 2)).reshape(3, CH, TAPS)
    wb = jnp.transpose(turned, (3, 0, 1, 2)).reshape(CH, 3 * TAPS)
    piece = 9 * CH * CH // plane
    conv_flops = 2 * 9 * CH * CH * ROWS * COLS
    out_mid, delta_mid, grad_mid, token = call(
        interior_body,
        [
            ((ROWS - 2, CH, COLS), bf16),
            ((ROWS - 2, CH, COLS), bf16),
            ((CH, 3 * TAPS), f32),
            ((8, COLS), f32),
        ],
        (fr, gr, w),
        [pltpu.VMEM((ROWS, TAPS, COLS), bf16)],
        2 * conv_flops,
    )

    far, near = call(edge_body, [((CH, COLS), bf16)] * 2, (edge, outer, inner, token))
    swaps = [(i, (i + 1 if i % 2 else i - 1) % lon_count) for i in range(lon_count)]
    far = lax.ppermute(far, LON, swaps)
    near = lax.ppermute(near, "side", [(0, 1), (1, 0)])

    out_rim, out_strip, delta_rim, dstrip, grad = call(
        border_body,
        [
            ((2, CH, COLS), bf16),
            ((CH, COLS), bf16),
            ((4, CH, COLS), bf16),
            ((CH, 3 * COLS), bf16),
            ((plane, 1, piece), f32),
        ],
        (fr, gr, edge, far, near, outer, inner, w, w3, grad_mid),
        [pltpu.VMEM((8, TAPS, COLS), bf16)],
        conv_flops // 4,
    )

    def exchange(parts, axes, first):
        count = lax.axis_size(axes)
        order = [(first + i) % count for i in range(count)]
        return lax.all_to_all(parts, axes, 0, 0, axis_index_groups=[order])

    def spread(parts, shape, dtype):
        return call(fold_body, [(shape, dtype)], (parts,))[0]

    writing = [pltpu.VMEM(flat, f32), pltpu.VMEM(flat, bf16), pltpu.SemaphoreType.DMA((PIECES,))]
    parts = exchange(grad, PLANE, plane // 4 + 1)
    (output,) = call(restore_body, [(flat, bf16)], (out_mid, out_rim, out_strip), writing, out_space=pl.ANY)
    parts = exchange(spread(parts, (lax.axis_size("z"), 1, piece), f32), "z", lax.axis_size("z") // 2)
    (grad_input,) = call(
        backward_body,
        [(flat, bf16)],
        (parts, delta_mid, delta_rim, dstrip, gr, wb, wb3),
        [pltpu.VMEM((ROWS + 2, TAPS, COLS), bf16)] + writing,
        conv_flops,
        out_space=pl.ANY,
    )
    packed = (plane, 2, -(-piece // (2 * COLS)) * COLS)
    parts = exchange(spread(parts, packed, bf16), PLANE, plane // 4 + 1)
    (grad_kernel,) = call(
        unpack_body,
        [((9, CH, CH), f32)],
        (parts,),
        [pltpu.VMEM((9, CH, CH), f32), pltpu.SemaphoreType.DMA((9,))],
        out_space=pl.ANY,
    )
    shape = field.shape
    return (output.reshape(shape), grad_input.reshape(shape), grad_kernel.reshape(kernel.shape))


def solution(mesh):
    lat_count, lon_count = mesh.devices.shape
    split = Mesh(mesh.devices.reshape(lat_count, lon_count // 2, 2), EVERY)
    block = P(None, None, "lat", LON)
    return jax.shard_map(
        on_device,
        mesh=split,
        in_specs=(block, P(), block),
        out_specs=(block, block, P()),
        check_vma=False,
    )
```

```python
import math

import jax
import jax.numpy as jnp
from jax import lax
from jax.experimental import pallas as pl
from jax.experimental.pallas import tpu as pltpu
from jax.sharding import Mesh
from jax.sharding import PartitionSpec as P

gelu_scale = math.sqrt(2.0 / math.pi)
ROWS, COLS, CH = 32, 128, 64
TAPS = 3 * CH
PIECES = 4
f32, bf16 = jnp.float32, jnp.bfloat16
LON = ("z", "side")
PLANE = ("lat", "side")
EVERY = ("lat", "z", "side")


def gelu_parts(hidden):
    square = hidden * hidden
    half = 0.5 + 0.5 * jnp.tanh(gelu_scale * hidden * (1.0 + 0.044715 * square))
    steep = gelu_scale * (1.0 + 3.0 * 0.044715 * square)
    return (hidden * half, half + 2.0 * hidden * half * (1.0 - half) * steep)


def roll(x, shift):
    return pltpu.roll(x, shift % x.shape[1], 1)


def lanes(width=COLS):
    return lax.broadcasted_iota(jnp.int32, (CH, width), 1)


def call(body, out_shape, args, scratch=(), flops=0, space=pltpu.VMEM, out_space=pltpu.VMEM, limit=24):
    outs = [jax.ShapeDtypeStruct(s, d) for s, d in out_shape]
    size = sum(a.size * a.dtype.itemsize for a in list(args) + outs)
    return pl.pallas_call(
        body,
        out_shape=outs,
        in_specs=[pl.BlockSpec(memory_space=space)] * len(args),
        out_specs=[pl.BlockSpec(memory_space=out_space)] * len(outs),
        scratch_shapes=list(scratch),
        cost_estimate=pl.CostEstimate(flops=flops, bytes_accessed=size, transcendentals=0),
        compiler_params=pltpu.CompilerParams(vmem_limit_bytes=int(limit * 2**20)),
    )(*args)


def pack_body(f_hbm, g_hbm, outer_ref, inner_ref, f_ref, g_ref, wide, sems):
    part = CH * ROWS // PIECES
    copies = [
        [
            pltpu.make_async_copy(src.at[pl.ds(i * part, part)], dst.at[pl.ds(i * part, part)], sems.at[at, i])
            for i in range(PIECES)
        ]
        for at, (src, dst) in enumerate(((f_hbm, f_ref), (g_hbm, g_ref)))
    ]
    for copy in copies[0] + copies[1]:
        copy.start()
    even = lax.axis_index("lat") % 2 == 0
    end = ROWS - 1
    slots = (((0, 0, end), (1, 1, end - 1)), ((2, 0, end),))
    for at, src in enumerate((f_ref, g_ref)):
        for i, copy in enumerate(copies[at]):
            copy.wait()
            wide[pl.ds(i * part, part), :] = src[pl.ds(i * part, part), :].astype(f32)
        for slot, low, high in slots[at]:
            first = wide[pl.ds(low, CH, stride=ROWS), :]
            last = wide[pl.ds(high, CH, stride=ROWS), :]
            outer_ref[pl.ds(slot * CH, CH), :] = jnp.where(even, first, last).astype(bf16)
            inner_ref[pl.ds(slot * CH, CH), :] = jnp.where(even, last, first).astype(bf16)


def turn_body(f_ref, g_ref, fr_ref, gr_ref, edge_ref, wide):
    lane = lanes()
    for at, (src, dst) in enumerate(((f_ref, fr_ref), (g_ref, gr_ref))):
        wide[...] = src[...].astype(f32)
        edge = jnp.zeros((CH, COLS), f32)
        for r in range(ROWS):
            row = wide[pl.ds(r, CH, stride=ROWS), :]
            edge = jnp.where((lane >= 4 * r) & (lane < 4 * r + 4), roll(row, 4 * r + 2), edge)
            dst[r] = row.astype(bf16)
        edge_ref[pl.ds(at * CH, CH), :] = edge.astype(bf16)


def row_halos(outer_ref, inner_ref):
    even = lax.axis_index("lat") % 2 == 0
    north = jnp.where(even, outer_ref[...], inner_ref[...]).astype(f32)
    south = jnp.where(even, inner_ref[...], outer_ref[...]).astype(f32)
    return [half[i * CH : (i + 1) * CH] for half in (north, south) for i in range(3)]


CORNERS = (
    ("s_near", 0, 0), ("s_near", 0, 1), ("s_cot", 0, 2), ("s_far", 4, 0), ("s_far", 4, 1),
    ("n_far", 120, 0), ("n_far", 120, 1), ("n_near", 124, 0), ("n_near", 124, 1), ("n_cot", 124, 2),
)


def edge_body(edge_ref, outer_ref, inner_ref, token_ref, far_ref, near_ref):
    names = ("n_near", "n_far", "n_cot", "s_near", "s_far", "s_cot")
    halos = dict(zip(names, row_halos(outer_ref, inner_ref)))
    kind = lanes() % 4
    lane = lanes()
    field = edge_ref[pl.ds(0, CH), :].astype(f32)
    cot = edge_ref[pl.ds(CH, CH), :].astype(f32)
    east = jnp.where(kind < 2, field, roll(cot, 1))
    west = jnp.where(kind >= 2, field, roll(cot, -1))
    for slot, (row, _, column) in enumerate(CORNERS):
        value = halos[row]
        to = 4 * slot + 3
        east = jnp.where(lane == to, roll(value, to - (126, 127, 127)[column]), east)
        to = 4 * slot
        west = jnp.where(lane == to, roll(value, to - (0, 1, 0)[column]), west)
    even = lax.axis_index("side") == 0
    far_ref[...] = jnp.where(even, west, east).astype(bf16)
    near_ref[...] = jnp.where(even, east, west).astype(bf16)


def column_halos(far_ref, near_ref):
    even = lax.axis_index("side") == 0
    far = far_ref[...].astype(f32)
    near = near_ref[...].astype(f32)
    west = jnp.where(even, far, near)
    east = jnp.where(even, near, far)
    lane = lanes()
    low = lane % 4 < 2
    field = jnp.where(low, west, east)
    cot = jnp.where(low, roll(west, -1), roll(east, 1))
    beyond = [jnp.zeros((CH, COLS), f32), jnp.zeros((CH, COLS), f32)]
    for slot, (_, base, column) in enumerate(CORNERS):
        at = column // 2
        for src, start, to in (
            (west, 4 * slot + 3, base + (0, 1, 1)[column]),
            (east, 4 * slot, base + (2, 3, 2)[column]),
        ):
            beyond[at] = jnp.where(lane == to, roll(src, to - start), beyond[at])
    return field, cot, beyond[0], beyond[1]


def stack_taps(out_ref, at, own, halo, lane):
    out_ref[at, pl.ds(0, CH), :] = roll(jnp.where(lane == COLS - 1, halo, own), 1).astype(bf16)
    out_ref[at, pl.ds(CH, CH), :] = own.astype(bf16)
    out_ref[at, pl.ds(2 * CH, CH), :] = roll(jnp.where(lane == 0, halo, own), -1).astype(bf16)


def dot(a, b):
    return jnp.dot(a, b, preferred_element_type=f32)


def interior_body(fr_ref, gr_ref, w_ref, out_ref, delta_ref, grad_ref, token_ref, xs):
    lane = lanes()
    inner = (lane > 0) & (lane < COLS - 1)
    none = jnp.zeros((CH, COLS), f32)
    for r in range(ROWS):
        stack_taps(xs, r, fr_ref[r].astype(f32), none, lane)
    weights = w_ref[...]
    for r in range(1, ROWS - 1, 2):
        window = jnp.concatenate(
            [xs[r - 1 : r + 2].reshape(3 * TAPS, COLS), xs[r : r + 3].reshape(3 * TAPS, COLS)], 1
        )
        value, slope = gelu_parts(dot(weights, window))
        for k in range(2):
            cut = slice(k * COLS, (k + 1) * COLS)
            out_ref[r + k - 1] = (fr_ref[r + k].astype(f32) + value[:, cut]).astype(bf16)
            delta = gr_ref[r + k].astype(f32) * slope[:, cut]
            delta_ref[r + k - 1] = jnp.where(inner, delta, 0.0).astype(bf16)
    total = None
    group = 10
    for r in range(0, ROWS - 2, group):
        left = jnp.concatenate([delta_ref[r + k] for k in range(group)], 1)
        right = jnp.concatenate([xs[r + k : r + k + 3].reshape(3 * TAPS, COLS) for k in range(group)], 1)
        term = dot_lanes(left, right)
        total = term if total is None else total + term
    grad_ref[...] = total
    token_ref[...] = jnp.zeros(token_ref.shape, f32)


def dot_lanes(a, b):
    return lax.dot_general(a, b, (((1,), (1,)), ((), ())), preferred_element_type=f32)


def border_body(
    fr_ref, gr_ref, edge_ref, far_ref, near_ref, outer_ref, inner_ref, w_ref, wa_ref, part_ref, wb_ref, wb3_ref,
    out_ref, outstrip_ref, delta_ref, dstrip_ref, grad_ref, xs,
):
    lat = lax.axis_index("lat")
    at_top = lat == 0
    at_bottom = lat == lax.axis_size("lat") - 1
    lane = lanes()
    n_near, n_far, n_cot, s_near, s_far, s_cot = row_halos(outer_ref, inner_ref)

    s, gs, beyond, gbeyond = column_halos(far_ref, near_ref)

    end = ROWS - 1
    stack_taps(xs, 0, n_far, roll(beyond, -122), lane)
    stack_taps(xs, 1, n_near, roll(beyond, -126), lane)
    for at, r in ((2, 0), (3, 1), (4, end - 1), (5, end)):
        stack_taps(xs, at, fr_ref[r].astype(f32), roll(s, -(4 * r + 2)), lane)
    stack_taps(xs, 6, s_near, roll(beyond, -2), lane)
    stack_taps(xs, 7, s_far, roll(beyond, -6), lane)

    weights = w_ref[...]
    window = jnp.concatenate([xs[1:4].reshape(3 * TAPS, COLS), xs[4:7].reshape(3 * TAPS, COLS)], 1)
    value, slope = gelu_parts(dot(weights, window))
    deltas = []
    for k, r in enumerate((0, end)):
        cut = slice(k * COLS, (k + 1) * COLS)
        out_ref[k] = (fr_ref[r].astype(f32) + value[:, cut]).astype(bf16)
        deltas.append((gr_ref[r].astype(f32) * slope[:, cut]).astype(bf16))
        delta_ref[k + 1] = deltas[k]

    def turned(flip, low):
        first = jnp.where(flip, xs[low + 2], xs[low])
        last = jnp.where(flip, xs[low], xs[low + 2])
        return jnp.concatenate([first, xs[low + 1], last], 0)

    outside = jnp.concatenate([turned(at_top, 0), turned(at_bottom, 5)], 1)
    slope = gelu_parts(dot(weights, outside))[1]
    delta_ref[0] = (n_cot * slope[:, :COLS]).astype(bf16)
    delta_ref[3] = (s_cot * slope[:, COLS:]).astype(bf16)

    edge = edge_ref[pl.ds(0, CH), :].astype(f32)
    halo = jnp.concatenate([s, beyond], 1)
    low = jnp.where(lane < 4, roll(s_near, 2), roll(s_far, 6))
    high = jnp.where(lane >= 124, roll(n_near, 126), roll(n_far, 122))
    own = jnp.concatenate([edge, jnp.where(lane < 64, low, high)], 1)
    wide_lane = lanes(2 * COLS)
    kind = wide_lane % 4
    small = lane % 4
    outer_taps = jnp.concatenate(
        [roll(jnp.where(kind == 0, halo, own), 1), halo, roll(jnp.where(kind == 3, halo, own), -1)], 0
    )
    inner_taps = jnp.concatenate(
        [roll(jnp.where(small == 1, s, edge), 1), edge, roll(jnp.where(small == 2, s, edge), -1)], 0
    )
    y = dot(wa_ref[...], jnp.concatenate([outer_taps, inner_taps], 1).astype(bf16))
    y0, y1, y2 = [y[i * CH : (i + 1) * CH, : 2 * COLS] for i in range(3)]
    straight = roll(y0, 4) + y1 + roll(y2, -4)
    backward = roll(y2, 4) + y1 + roll(y0, -4)
    flip = ((wide_lane >= 252) & at_top) | ((wide_lane >= 128) & (wide_lane < 132) & at_bottom)
    y0, y1, y2 = [y[i * CH : (i + 1) * CH, 2 * COLS :] for i in range(3)]
    packed = [jnp.where(flip, backward, straight), roll(y0, 4) + y1 + roll(y2, -4)]
    value, slope = gelu_parts(jnp.concatenate(packed, 1))
    own_cot = edge_ref[pl.ds(CH, CH), :].astype(f32)
    outstrip_ref[...] = (edge + value[:, 2 * COLS :]).astype(bf16)
    dstrip = jnp.concatenate([gs, gbeyond, own_cot], 1) * slope
    dstrip_ref[...] = dstrip.astype(bf16)

    used = ((small == 1) | (small == 2)) & (lane >= 4) & (lane < 4 * end)
    side = jnp.where(used, dstrip[:, 2 * COLS :], 0.0).astype(bf16)
    shifted = jnp.concatenate([roll(inner_taps, 4), inner_taps, roll(inner_taps, -4)], 0).astype(bf16)
    left = jnp.concatenate([deltas[0], deltas[1], side], 1)
    total = part_ref[...] + dot_lanes(left, jnp.concatenate([window, shifted], 1))
    total = total * grad_scale()
    count = grad_ref.shape[0]
    pieces = []
    for p in range(5):
        piece = total[:, p * COLS : (p + 1) * COLS]
        pieces.append([piece[j * count : (j + 1) * count] for j in range(CH // count)])
    tiles = [piece[j] for j in range(CH // count) for piece in pieces[:4]]
    last = pieces[4]
    for j in range(0, len(last), 2):
        tiles.append(jnp.concatenate(last[j : j + 2], 1))
    for q, tile in enumerate(tiles):
        grad_ref[:, 0, pl.ds(q * COLS, COLS)] = tile


def patched(row, packed, r, lane):
    return jnp.where((lane == 0) | (lane == COLS - 1), roll(packed, -(4 * r + 2)), row.astype(f32))


def write_out(wide, out_hbm, out_ref, sems):
    part = CH * ROWS // PIECES
    copies = []
    for i in range(PIECES):
        at = pl.ds(i * part, part)
        out_ref[at, :] = wide[at, :].astype(bf16)
        copies.append(pltpu.make_async_copy(out_ref.at[at], out_hbm.at[at], sems.at[i]))
        copies[-1].start()
    for copy in copies:
        copy.wait()


def restore_body(mid_ref, rim_ref, strip_ref, out_hbm, wide, out_ref, sems):
    lane = lanes()
    packed = strip_ref[...].astype(f32)
    wide[pl.ds(0, CH, stride=ROWS), :] = rim_ref[0].astype(f32)
    for r in range(1, ROWS - 1):
        wide[pl.ds(r, CH, stride=ROWS), :] = patched(mid_ref[r - 1], packed, r, lane)
    wide[pl.ds(ROWS - 1, CH, stride=ROWS), :] = rim_ref[1].astype(f32)
    write_out(wide, out_hbm, out_ref, sems)


def grad_scale():
    return float(ROWS * COLS * lax.axis_size(EVERY)) ** (-0.5)


def backward_body(after_ref, mid_ref, rim_ref, dstrip_ref, gr_ref, wb_ref, wb3_ref, out_hbm, xs, wide, out_ref, sems):
    lat = lax.axis_index("lat")
    at_top = lat == 0
    at_bottom = lat == lax.axis_size("lat") - 1
    lane = lanes()
    s = dstrip_ref[:, :COLS].astype(f32)
    beyond = dstrip_ref[:, COLS : 2 * COLS].astype(f32)
    own = dstrip_ref[:, 2 * COLS :].astype(f32)
    stack_taps(xs, 0, rim_ref[0].astype(f32), roll(beyond, -126), lane)
    stack_taps(xs, 1, rim_ref[1].astype(f32), roll(s, -2), lane)
    for r in range(1, ROWS - 1):
        stack_taps(xs, r + 1, patched(mid_ref[r - 1], own, r, lane), roll(s, -(4 * r + 2)), lane)
    stack_taps(xs, ROWS, rim_ref[2].astype(f32), roll(s, -(4 * ROWS - 2)), lane)
    stack_taps(xs, ROWS + 1, rim_ref[3].astype(f32), roll(beyond, -2), lane)
    weights = wb_ref[...]

    def put(r, back):
        wide[pl.ds(r, CH, stride=ROWS), :] = gr_ref[r].astype(f32) + back

    upper = jnp.where(at_top, wb3_ref[2], wb3_ref[0])
    lower = jnp.where(at_bottom, wb3_ref[0], wb3_ref[2])
    put(0, dot(upper, xs[0]) + dot(wb3_ref[1], xs[1]) + dot(wb3_ref[2], xs[2]))
    end = ROWS - 1
    put(end, dot(wb3_ref[0], xs[end]) + dot(wb3_ref[1], xs[end + 1]) + dot(lower, xs[end + 2]))
    for r in range(1, ROWS - 1, 2):
        window = jnp.concatenate(
            [xs[r : r + 3].reshape(3 * TAPS, COLS), xs[r + 1 : r + 4].reshape(3 * TAPS, COLS)], 1
        )
        back = dot(weights, window)
        put(r, back[:, :COLS])
        put(r + 1, back[:, COLS:])
    write_out(wide, out_hbm, out_ref, sems)


def fold_body(parts_ref, out_ref):
    total = jnp.sum(parts_ref[...], 0)
    if out_ref.shape[1] == 2:
        width = out_ref.shape[2]
        rest = jnp.zeros((1, 2 * width - total.shape[1]), f32)
        total = jnp.concatenate([total, rest], 1)
        total = jnp.concatenate([total[:, :width], total[:, width:]], 0)
    total = total.astype(out_ref.dtype)
    for i in range(out_ref.shape[0]):
        out_ref[i] = total


def unpack_body(parts_ref, out_hbm, out_ref, sems):
    count = parts_ref.shape[0]
    half = parts_ref.shape[2] // COLS
    tiles = []
    for q in range(2 * half):
        tiles.append(parts_ref[:, q // half, pl.ds(q % half * COLS, COLS)].astype(f32))
    copies = []
    for tap in range(9):
        for j in range(CH // count):
            if tap < 8:
                tile, at = tiles[4 * j + tap // 2], tap % 2
            else:
                tile, at = tiles[4 * (CH // count) + j // 2], j % 2
            out_ref[tap, pl.ds(j * count, count), :] = tile[:, at * CH : (at + 1) * CH]
        copies.append(pltpu.make_async_copy(out_ref.at[tap], out_hbm.at[tap], sems.at[tap]))
        copies[-1].start()
    for copy in copies:
        copy.wait()


def outer_pairs(lat_count, lon_count):
    half = lon_count // 2
    pairs = []
    for l in range(lat_count):
        for m in range(lon_count):
            to = l - 1 if l % 2 == 0 else l + 1
            if 0 <= to < lat_count:
                pairs.append((l * lon_count + m, to * lon_count + m))
            else:
                pairs.append((l * lon_count + m, l * lon_count + (m + half) % lon_count))
    return pairs


def on_device(field, kernel, cotangent):
    lat_count = lax.axis_size("lat")
    lon_count = lax.axis_size(LON)
    plane = lax.axis_size(PLANE)
    flat = (CH * ROWS, COLS)
    rows_shape = (ROWS, CH, COLS)

    flat_field, flat_cotangent = field.reshape(flat), cotangent.reshape(flat)
    outer, inner, f_near, g_near = call(
        pack_body,
        [((TAPS, COLS), bf16), ((TAPS, COLS), bf16), (flat, bf16), (flat, bf16)],
        (flat_field, flat_cotangent),
        [pltpu.VMEM(flat, f32), pltpu.SemaphoreType.DMA((2, PIECES))],
        space=pl.ANY,
        limit=52.5,
    )
    outer = lax.ppermute(outer, EVERY, outer_pairs(lat_count, lon_count))
    inner = lax.ppermute(inner, "lat", [(i, i ^ 1) for i in range(lat_count)])
    fr, gr, edge = call(
        turn_body,
        [(rows_shape, bf16), (rows_shape, bf16), ((2 * CH, COLS), bf16)],
        (f_near, g_near),
        [pltpu.VMEM(flat, f32)],
    )

    w3 = jnp.transpose(kernel, (0, 2, 1, 3)).reshape(TAPS, TAPS)
    w = jnp.transpose(kernel, (2, 0, 1, 3)).reshape(CH, 3 * TAPS)
    turned = kernel[::-1, ::-1]
    wb3 = jnp.transpose(turned, (0, 3, 1, 2)).reshape(3, CH, TAPS)
    wb = jnp.transpose(turned, (3, 0, 1, 2)).reshape(CH, 3 * TAPS)
    piece = 9 * CH * CH // plane
    conv_flops = 2 * 9 * CH * CH * ROWS * COLS
    out_mid, delta_mid, grad_mid, token = call(
        interior_body,
        [
            ((ROWS - 2, CH, COLS), bf16),
            ((ROWS - 2, CH, COLS), bf16),
            ((CH, 3 * TAPS), f32),
            ((8, COLS), f32),
        ],
        (fr, gr, w),
        [pltpu.VMEM((ROWS, TAPS, COLS), bf16)],
        2 * conv_flops,
    )

    far, near = call(edge_body, [((CH, COLS), bf16)] * 2, (edge, outer, inner, token))
    swaps = [(i, (i + 1 if i % 2 else i - 1) % lon_count) for i in range(lon_count)]
    far = lax.ppermute(far, LON, swaps)
    near = lax.ppermute(near, "side", [(0, 1), (1, 0)])

    out_rim, out_strip, delta_rim, dstrip, grad = call(
        border_body,
        [
            ((2, CH, COLS), bf16),
            ((CH, COLS), bf16),
            ((4, CH, COLS), bf16),
            ((CH, 3 * COLS), bf16),
            ((plane, 1, piece), f32),
        ],
        (fr, gr, edge, far, near, outer, inner, w, w3, grad_mid, wb, wb3),
        [pltpu.VMEM((8, TAPS, COLS), bf16)],
        conv_flops // 4,
    )

    root = (5 * plane // 8) % plane
    def exchange(parts, axes, first):
        count = lax.axis_size(axes)
        order = [(first + i) % count for i in range(count)]
        return lax.all_to_all(parts, axes, 0, 0, axis_index_groups=[order])

    def spread(parts, shape, dtype):
        return call(fold_body, [(shape, dtype)], (parts,))[0]

    writing = [pltpu.VMEM(flat, f32), pltpu.VMEM(flat, bf16), pltpu.SemaphoreType.DMA((PIECES,))]
    parts = exchange(grad, PLANE, root)
    (output,) = call(restore_body, [(flat, bf16)], (out_mid, out_rim, out_strip), writing, out_space=pl.ANY)
    parts = exchange(spread(parts, (lax.axis_size("z"), 1, piece), f32), "z", lax.axis_size("z") // 2)
    (grad_input,) = call(
        backward_body,
        [(flat, bf16)],
        (parts, delta_mid, delta_rim, dstrip, gr, wb, wb3),
        [pltpu.VMEM((ROWS + 2, TAPS, COLS), bf16)] + writing,
        conv_flops,
        out_space=pl.ANY,
    )
    packed = (plane, 2, -(-piece // (2 * COLS)) * COLS)
    parts = exchange(spread(parts, packed, bf16), PLANE, root)
    (grad_kernel,) = call(
        unpack_body,
        [((9, CH, CH), f32)],
        (parts,),
        [pltpu.VMEM((9, CH, CH), f32), pltpu.SemaphoreType.DMA((9,))],
        out_space=pl.ANY,
    )
    shape = field.shape
    return (output.reshape(shape), grad_input.reshape(shape), grad_kernel.reshape(kernel.shape))


def solution(mesh):
    lat_count, lon_count = mesh.devices.shape
    split = Mesh(mesh.devices.reshape(lat_count, lon_count // 2, 2), EVERY)
    block = P(None, None, "lat", LON)
    return jax.shard_map(
        on_device,
        mesh=split,
        in_specs=(block, P(), block),
        out_specs=(block, block, P()),
        check_vma=False,
    )
```

```python
import math

import jax
import jax.numpy as jnp
from jax import lax
from jax.experimental import pallas as pl
from jax.experimental.pallas import tpu as pltpu
from jax.sharding import Mesh
from jax.sharding import PartitionSpec as P

gelu_scale = math.sqrt(2.0 / math.pi)
ROWS, COLS, CH = 32, 128, 64
TAPS = 3 * CH
PIECES = 4
f32, bf16 = jnp.float32, jnp.bfloat16
LON = ("z", "side")
PLANE = ("lat", "side")
EVERY = ("lat", "z", "side")


def gelu_parts(hidden):
    square = hidden * hidden
    half = 0.5 + 0.5 * jnp.tanh(gelu_scale * hidden * (1.0 + 0.044715 * square))
    steep = gelu_scale * (1.0 + 3.0 * 0.044715 * square)
    return (hidden * half, half + 2.0 * hidden * half * (1.0 - half) * steep)


def roll(x, shift):
    return pltpu.roll(x, shift % x.shape[1], 1)


def lanes(width=COLS):
    return lax.broadcasted_iota(jnp.int32, (CH, width), 1)


def call(body, out_shape, args, scratch=(), flops=0, space=pltpu.VMEM, out_space=pltpu.VMEM, limit=24):
    outs = [jax.ShapeDtypeStruct(s, d) for s, d in out_shape]
    size = sum(a.size * a.dtype.itemsize for a in list(args) + outs)
    return pl.pallas_call(
        body,
        out_shape=outs,
        in_specs=[pl.BlockSpec(memory_space=space)] * len(args),
        out_specs=[pl.BlockSpec(memory_space=out_space)] * len(outs),
        scratch_shapes=list(scratch),
        cost_estimate=pl.CostEstimate(flops=flops, bytes_accessed=size, transcendentals=0),
        compiler_params=pltpu.CompilerParams(vmem_limit_bytes=int(limit * 2**20)),
    )(*args)


def pack_body(f_hbm, g_hbm, outer_ref, inner_ref, f_ref, g_ref, wide, sems):
    part = CH * ROWS // PIECES
    copies = [
        [
            pltpu.make_async_copy(src.at[pl.ds(i * part, part)], dst.at[pl.ds(i * part, part)], sems.at[at, i])
            for i in range(PIECES)
        ]
        for at, (src, dst) in enumerate(((f_hbm, f_ref), (g_hbm, g_ref)))
    ]
    for copy in copies[0] + copies[1]:
        copy.start()
    even = lax.axis_index("lat") % 2 == 0
    end = ROWS - 1
    slots = (((0, 0, end), (1, 1, end - 1)), ((2, 0, end),))
    for at, src in enumerate((f_ref, g_ref)):
        for i, copy in enumerate(copies[at]):
            copy.wait()
            wide[pl.ds(i * part, part), :] = src[pl.ds(i * part, part), :].astype(f32)
        for slot, low, high in slots[at]:
            first = wide[pl.ds(low, CH, stride=ROWS), :]
            last = wide[pl.ds(high, CH, stride=ROWS), :]
            outer_ref[pl.ds(slot * CH, CH), :] = jnp.where(even, first, last).astype(bf16)
            inner_ref[pl.ds(slot * CH, CH), :] = jnp.where(even, last, first).astype(bf16)


def turn_body(f_ref, g_ref, fr_ref, gr_ref, edge_ref, wide):
    lane = lanes()
    for at, (src, dst) in enumerate(((f_ref, fr_ref), (g_ref, gr_ref))):
        wide[...] = src[...].astype(f32)
        edge = jnp.zeros((CH, COLS), f32)
        for r in range(ROWS):
            row = wide[pl.ds(r, CH, stride=ROWS), :]
            edge = jnp.where((lane >= 4 * r) & (lane < 4 * r + 4), roll(row, 4 * r + 2), edge)
            dst[r] = row.astype(bf16)
        edge_ref[pl.ds(at * CH, CH), :] = edge.astype(bf16)


def row_halos(outer_ref, inner_ref):
    even = lax.axis_index("lat") % 2 == 0
    north = jnp.where(even, outer_ref[...], inner_ref[...]).astype(f32)
    south = jnp.where(even, inner_ref[...], outer_ref[...]).astype(f32)
    return [half[i * CH : (i + 1) * CH] for half in (north, south) for i in range(3)]


CORNERS = (
    ("s_near", 0, 0), ("s_near", 0, 1), ("s_cot", 0, 2), ("s_far", 4, 0), ("s_far", 4, 1),
    ("n_far", 120, 0), ("n_far", 120, 1), ("n_near", 124, 0), ("n_near", 124, 1), ("n_cot", 124, 2),
)


def edge_body(edge_ref, outer_ref, inner_ref, token_ref, far_ref, near_ref):
    names = ("n_near", "n_far", "n_cot", "s_near", "s_far", "s_cot")
    halos = dict(zip(names, row_halos(outer_ref, inner_ref)))
    kind = lanes() % 4
    lane = lanes()
    field = edge_ref[pl.ds(0, CH), :].astype(f32)
    cot = edge_ref[pl.ds(CH, CH), :].astype(f32)
    east = jnp.where(kind < 2, field, roll(cot, 1))
    west = jnp.where(kind >= 2, field, roll(cot, -1))
    for slot, (row, _, column) in enumerate(CORNERS):
        value = halos[row]
        to = 4 * slot + 3
        east = jnp.where(lane == to, roll(value, to - (126, 127, 127)[column]), east)
        to = 4 * slot
        west = jnp.where(lane == to, roll(value, to - (0, 1, 0)[column]), west)
    even = lax.axis_index("side") == 0
    far_ref[...] = jnp.where(even, west, east).astype(bf16)
    near_ref[...] = jnp.where(even, east, west).astype(bf16)


def column_halos(far_ref, near_ref):
    even = lax.axis_index("side") == 0
    far = far_ref[...].astype(f32)
    near = near_ref[...].astype(f32)
    west = jnp.where(even, far, near)
    east = jnp.where(even, near, far)
    lane = lanes()
    low = lane % 4 < 2
    field = jnp.where(low, west, east)
    cot = jnp.where(low, roll(west, -1), roll(east, 1))
    beyond = [jnp.zeros((CH, COLS), f32), jnp.zeros((CH, COLS), f32)]
    for slot, (_, base, column) in enumerate(CORNERS):
        at = column // 2
        for src, start, to in (
            (west, 4 * slot + 3, base + (0, 1, 1)[column]),
            (east, 4 * slot, base + (2, 3, 2)[column]),
        ):
            beyond[at] = jnp.where(lane == to, roll(src, to - start), beyond[at])
    return field, cot, beyond[0], beyond[1]


def stack_taps(out_ref, at, own, halo, lane):
    out_ref[at, pl.ds(0, CH), :] = roll(jnp.where(lane == COLS - 1, halo, own), 1).astype(bf16)
    out_ref[at, pl.ds(CH, CH), :] = own.astype(bf16)
    out_ref[at, pl.ds(2 * CH, CH), :] = roll(jnp.where(lane == 0, halo, own), -1).astype(bf16)


def dot(a, b):
    return jnp.dot(a, b, preferred_element_type=f32)


def interior_body(fr_ref, gr_ref, w_ref, out_ref, delta_ref, grad_ref, token_ref, xs):
    lane = lanes()
    inner = (lane > 0) & (lane < COLS - 1)
    none = jnp.zeros((CH, COLS), f32)
    for r in range(ROWS):
        stack_taps(xs, r, fr_ref[r].astype(f32), none, lane)
    weights = w_ref[...]
    for r in range(1, ROWS - 1, 2):
        window = jnp.concatenate(
            [xs[r - 1 : r + 2].reshape(3 * TAPS, COLS), xs[r : r + 3].reshape(3 * TAPS, COLS)], 1
        )
        value, slope = gelu_parts(dot(weights, window))
        for k in range(2):
            cut = slice(k * COLS, (k + 1) * COLS)
            out_ref[r + k - 1] = (fr_ref[r + k].astype(f32) + value[:, cut]).astype(bf16)
            delta = gr_ref[r + k].astype(f32) * slope[:, cut]
            delta_ref[r + k - 1] = jnp.where(inner, delta, 0.0).astype(bf16)
    total = None
    group = 10
    for r in range(0, ROWS - 2, group):
        left = jnp.concatenate([delta_ref[r + k] for k in range(group)], 1)
        right = jnp.concatenate([xs[r + k : r + k + 3].reshape(3 * TAPS, COLS) for k in range(group)], 1)
        term = dot_lanes(left, right)
        total = term if total is None else total + term
    grad_ref[...] = total
    token_ref[...] = jnp.zeros(token_ref.shape, f32)


def dot_lanes(a, b):
    return lax.dot_general(a, b, (((1,), (1,)), ((), ())), preferred_element_type=f32)


def border_body(
    fr_ref, gr_ref, edge_ref, far_ref, near_ref, outer_ref, inner_ref, w_ref, wa_ref, part_ref, wb_ref, wb3_ref,
    out_ref, outstrip_ref, delta_ref, dstrip_ref, grad_ref, xs,
):
    lat = lax.axis_index("lat")
    at_top = lat == 0
    at_bottom = lat == lax.axis_size("lat") - 1
    lane = lanes()
    n_near, n_far, n_cot, s_near, s_far, s_cot = row_halos(outer_ref, inner_ref)

    s, gs, beyond, gbeyond = column_halos(far_ref, near_ref)

    end = ROWS - 1
    stack_taps(xs, 0, n_far, roll(beyond, -122), lane)
    stack_taps(xs, 1, n_near, roll(beyond, -126), lane)
    for at, r in ((2, 0), (3, 1), (4, end - 1), (5, end)):
        stack_taps(xs, at, fr_ref[r].astype(f32), roll(s, -(4 * r + 2)), lane)
    stack_taps(xs, 6, s_near, roll(beyond, -2), lane)
    stack_taps(xs, 7, s_far, roll(beyond, -6), lane)

    weights = w_ref[...]
    window = jnp.concatenate([xs[1:4].reshape(3 * TAPS, COLS), xs[4:7].reshape(3 * TAPS, COLS)], 1)
    value, slope = gelu_parts(dot(weights, window))
    deltas = []
    for k, r in enumerate((0, end)):
        cut = slice(k * COLS, (k + 1) * COLS)
        out_ref[k] = (fr_ref[r].astype(f32) + value[:, cut]).astype(bf16)
        deltas.append((gr_ref[r].astype(f32) * slope[:, cut]).astype(bf16))
        delta_ref[k + 1] = deltas[k]

    def turned(flip, low):
        first = jnp.where(flip, xs[low + 2], xs[low])
        last = jnp.where(flip, xs[low], xs[low + 2])
        return jnp.concatenate([first, xs[low + 1], last], 0)

    outside = jnp.concatenate([turned(at_top, 0), turned(at_bottom, 5)], 1)
    slope = gelu_parts(dot(weights, outside))[1]
    delta_ref[0] = (n_cot * slope[:, :COLS]).astype(bf16)
    delta_ref[3] = (s_cot * slope[:, COLS:]).astype(bf16)

    edge = edge_ref[pl.ds(0, CH), :].astype(f32)
    halo = jnp.concatenate([s, beyond], 1)
    low = jnp.where(lane < 4, roll(s_near, 2), roll(s_far, 6))
    high = jnp.where(lane >= 124, roll(n_near, 126), roll(n_far, 122))
    own = jnp.concatenate([edge, jnp.where(lane < 64, low, high)], 1)
    wide_lane = lanes(2 * COLS)
    kind = wide_lane % 4
    small = lane % 4
    outer_taps = jnp.concatenate(
        [roll(jnp.where(kind == 0, halo, own), 1), halo, roll(jnp.where(kind == 3, halo, own), -1)], 0
    )
    inner_taps = jnp.concatenate(
        [roll(jnp.where(small == 1, s, edge), 1), edge, roll(jnp.where(small == 2, s, edge), -1)], 0
    )
    y = dot(wa_ref[...], jnp.concatenate([outer_taps, inner_taps], 1).astype(bf16))
    y0, y1, y2 = [y[i * CH : (i + 1) * CH, : 2 * COLS] for i in range(3)]
    straight = roll(y0, 4) + y1 + roll(y2, -4)
    backward = roll(y2, 4) + y1 + roll(y0, -4)
    flip = ((wide_lane >= 252) & at_top) | ((wide_lane >= 128) & (wide_lane < 132) & at_bottom)
    y0, y1, y2 = [y[i * CH : (i + 1) * CH, 2 * COLS :] for i in range(3)]
    packed = [jnp.where(flip, backward, straight), roll(y0, 4) + y1 + roll(y2, -4)]
    value, slope = gelu_parts(jnp.concatenate(packed, 1))
    own_cot = edge_ref[pl.ds(CH, CH), :].astype(f32)
    outstrip_ref[...] = (edge + value[:, 2 * COLS :]).astype(bf16)
    dstrip = jnp.concatenate([gs, gbeyond, own_cot], 1) * slope
    dstrip_ref[...] = dstrip.astype(bf16)

    used = ((small == 1) | (small == 2)) & (lane >= 4) & (lane < 4 * end)
    side = jnp.where(used, dstrip[:, 2 * COLS :], 0.0).astype(bf16)
    shifted = jnp.concatenate([roll(inner_taps, 4), inner_taps, roll(inner_taps, -4)], 0).astype(bf16)
    left = jnp.concatenate([deltas[0], deltas[1], side], 1)
    total = part_ref[...] + dot_lanes(left, jnp.concatenate([window, shifted], 1))
    total = total * grad_scale()
    count = grad_ref.shape[0]
    pieces = []
    for p in range(5):
        piece = total[:, p * COLS : (p + 1) * COLS]
        pieces.append([piece[j * count : (j + 1) * count] for j in range(CH // count)])
    tiles = [piece[j] for j in range(CH // count) for piece in pieces[:4]]
    last = pieces[4]
    for j in range(0, len(last), 2):
        tiles.append(jnp.concatenate(last[j : j + 2], 1))
    for q, tile in enumerate(tiles):
        grad_ref[:, 0, pl.ds(q * COLS, COLS)] = tile


def patched(row, packed, r, lane):
    return jnp.where((lane == 0) | (lane == COLS - 1), roll(packed, -(4 * r + 2)), row.astype(f32))


def write_out(wide, out_hbm, out_ref, sems):
    part = CH * ROWS // PIECES
    copies = []
    for i in range(PIECES):
        at = pl.ds(i * part, part)
        out_ref[at, :] = wide[at, :].astype(bf16)
        copies.append(pltpu.make_async_copy(out_ref.at[at], out_hbm.at[at], sems.at[i]))
        copies[-1].start()
    for copy in copies:
        copy.wait()


def restore_body(mid_ref, rim_ref, strip_ref, out_hbm, wide, out_ref, sems):
    lane = lanes()
    packed = strip_ref[...].astype(f32)
    wide[pl.ds(0, CH, stride=ROWS), :] = rim_ref[0].astype(f32)
    for r in range(1, ROWS - 1):
        wide[pl.ds(r, CH, stride=ROWS), :] = patched(mid_ref[r - 1], packed, r, lane)
    wide[pl.ds(ROWS - 1, CH, stride=ROWS), :] = rim_ref[1].astype(f32)
    write_out(wide, out_hbm, out_ref, sems)


def grad_scale():
    return float(ROWS * COLS * lax.axis_size(EVERY)) ** (-0.5)


def backward_body(after_ref, mid_ref, rim_ref, dstrip_ref, gr_ref, wb_ref, wb3_ref, out_hbm, xs, wide, out_ref, sems):
    lat = lax.axis_index("lat")
    at_top = lat == 0
    at_bottom = lat == lax.axis_size("lat") - 1
    lane = lanes()
    s = dstrip_ref[:, :COLS].astype(f32)
    beyond = dstrip_ref[:, COLS : 2 * COLS].astype(f32)
    own = dstrip_ref[:, 2 * COLS :].astype(f32)
    stack_taps(xs, 0, rim_ref[0].astype(f32), roll(beyond, -126), lane)
    stack_taps(xs, 1, rim_ref[1].astype(f32), roll(s, -2), lane)
    for r in range(1, ROWS - 1):
        stack_taps(xs, r + 1, patched(mid_ref[r - 1], own, r, lane), roll(s, -(4 * r + 2)), lane)
    stack_taps(xs, ROWS, rim_ref[2].astype(f32), roll(s, -(4 * ROWS - 2)), lane)
    stack_taps(xs, ROWS + 1, rim_ref[3].astype(f32), roll(beyond, -2), lane)
    weights = wb_ref[...]

    def put(r, back):
        wide[pl.ds(r, CH, stride=ROWS), :] = gr_ref[r].astype(f32) + back

    upper = jnp.where(at_top, wb3_ref[2], wb3_ref[0])
    lower = jnp.where(at_bottom, wb3_ref[0], wb3_ref[2])
    put(0, dot(upper, xs[0]) + dot(wb3_ref[1], xs[1]) + dot(wb3_ref[2], xs[2]))
    end = ROWS - 1
    put(end, dot(wb3_ref[0], xs[end]) + dot(wb3_ref[1], xs[end + 1]) + dot(lower, xs[end + 2]))
    for r in range(1, ROWS - 1, 2):
        window = jnp.concatenate(
            [xs[r : r + 3].reshape(3 * TAPS, COLS), xs[r + 1 : r + 4].reshape(3 * TAPS, COLS)], 1
        )
        back = dot(weights, window)
        put(r, back[:, :COLS])
        put(r + 1, back[:, COLS:])
    write_out(wide, out_hbm, out_ref, sems)


def fold_body(parts_ref, out_ref):
    total = jnp.sum(parts_ref[...], 0)
    if out_ref.shape[1] == 2:
        width = out_ref.shape[2]
        rest = jnp.zeros((1, 2 * width - total.shape[1]), f32)
        total = jnp.concatenate([total, rest], 1)
        total = jnp.concatenate([total[:, :width], total[:, width:]], 0)
    total = total.astype(out_ref.dtype)
    for i in range(out_ref.shape[0]):
        out_ref[i] = total


def unpack_body(parts_ref, out_hbm, out_ref, sems):
    count = parts_ref.shape[0]
    half = parts_ref.shape[2] // COLS
    parts = parts_ref[...].astype(f32)
    tiles = [parts[:, q // half, q % half * COLS : (q % half + 1) * COLS] for q in range(2 * half)]
    copies = []
    for tap in range(9):
        for j in range(CH // count):
            if tap < 8:
                tile, at = tiles[4 * j + tap // 2], tap % 2
            else:
                tile, at = tiles[4 * (CH // count) + j // 2], j % 2
            out_ref[tap, pl.ds(j * count, count), :] = tile[:, at * CH : (at + 1) * CH]
        copies.append(pltpu.make_async_copy(out_ref.at[tap], out_hbm.at[tap], sems.at[tap]))
        copies[-1].start()
    for copy in copies:
        copy.wait()


def outer_pairs(lat_count, lon_count):
    half = lon_count // 2
    pairs = []
    for l in range(lat_count):
        for m in range(lon_count):
            to = l - 1 if l % 2 == 0 else l + 1
            if 0 <= to < lat_count:
                pairs.append((l * lon_count + m, to * lon_count + m))
            else:
                pairs.append((l * lon_count + m, l * lon_count + (m + half) % lon_count))
    return pairs


def on_device(field, kernel, cotangent):
    lat_count = lax.axis_size("lat")
    lon_count = lax.axis_size(LON)
    plane = lax.axis_size(PLANE)
    flat = (CH * ROWS, COLS)
    rows_shape = (ROWS, CH, COLS)

    flat_field, flat_cotangent = field.reshape(flat), cotangent.reshape(flat)
    outer, inner, f_near, g_near = call(
        pack_body,
        [((TAPS, COLS), bf16), ((TAPS, COLS), bf16), (flat, bf16), (flat, bf16)],
        (flat_field, flat_cotangent),
        [pltpu.VMEM(flat, f32), pltpu.SemaphoreType.DMA((2, PIECES))],
        space=pl.ANY,
        limit=52.5,
    )
    outer = lax.ppermute(outer, EVERY, outer_pairs(lat_count, lon_count))
    inner = lax.ppermute(inner, "lat", [(i, i ^ 1) for i in range(lat_count)])
    fr, gr, edge = call(
        turn_body,
        [(rows_shape, bf16), (rows_shape, bf16), ((2 * CH, COLS), bf16)],
        (f_near, g_near),
        [pltpu.VMEM(flat, f32)],
    )

    w3 = jnp.transpose(kernel, (0, 2, 1, 3)).reshape(TAPS, TAPS)
    w = jnp.transpose(kernel, (2, 0, 1, 3)).reshape(CH, 3 * TAPS)
    turned = kernel[::-1, ::-1]
    wb3 = jnp.transpose(turned, (0, 3, 1, 2)).reshape(3, CH, TAPS)
    wb = jnp.transpose(turned, (3, 0, 1, 2)).reshape(CH, 3 * TAPS)
    piece = 9 * CH * CH // plane
    conv_flops = 2 * 9 * CH * CH * ROWS * COLS
    out_mid, delta_mid, grad_mid, token = call(
        interior_body,
        [
            ((ROWS - 2, CH, COLS), bf16),
            ((ROWS - 2, CH, COLS), bf16),
            ((CH, 3 * TAPS), f32),
            ((8, COLS), f32),
        ],
        (fr, gr, w),
        [pltpu.VMEM((ROWS, TAPS, COLS), bf16)],
        2 * conv_flops,
    )

    far, near = call(edge_body, [((CH, COLS), bf16)] * 2, (edge, outer, inner, token))
    swaps = [(i, (i + 1 if i % 2 else i - 1) % lon_count) for i in range(lon_count)]
    far = lax.ppermute(far, LON, swaps)
    near = lax.ppermute(near, "side", [(0, 1), (1, 0)])

    out_rim, out_strip, delta_rim, dstrip, grad = call(
        border_body,
        [
            ((2, CH, COLS), bf16),
            ((CH, COLS), bf16),
            ((4, CH, COLS), bf16),
            ((CH, 3 * COLS), bf16),
            ((plane, 1, piece), f32),
        ],
        (fr, gr, edge, far, near, outer, inner, w, w3, grad_mid, wb, wb3),
        [pltpu.VMEM((8, TAPS, COLS), bf16)],
        conv_flops // 4,
    )

    root = (5 * plane // 8) % plane
    def exchange(parts, axes, first):
        count = lax.axis_size(axes)
        order = [(first + i) % count for i in range(count)]
        return lax.all_to_all(parts, axes, 0, 0, axis_index_groups=[order])

    def spread(parts, shape, dtype):
        return call(fold_body, [(shape, dtype)], (parts,))[0]

    writing = [pltpu.VMEM(flat, f32), pltpu.VMEM(flat, bf16), pltpu.SemaphoreType.DMA((PIECES,))]
    parts = exchange(grad, PLANE, root)
    (output,) = call(restore_body, [(flat, bf16)], (out_mid, out_rim, out_strip), writing, out_space=pl.ANY)
    parts = exchange(spread(parts, (lax.axis_size("z"), 1, piece), f32), "z", lax.axis_size("z") // 2)
    (grad_input,) = call(
        backward_body,
        [(flat, bf16)],
        (parts, delta_mid, delta_rim, dstrip, gr, wb, wb3),
        [pltpu.VMEM((ROWS + 2, TAPS, COLS), bf16)] + writing,
        conv_flops,
        out_space=pl.ANY,
    )
    packed = (plane, 2, -(-piece // (2 * COLS)) * COLS)
    parts = exchange(spread(parts, packed, bf16), PLANE, root)
    (grad_kernel,) = call(
        unpack_body,
        [((9, CH, CH), f32)],
        (parts,),
        [pltpu.VMEM((9, CH, CH), f32), pltpu.SemaphoreType.DMA((9,))],
        out_space=pl.ANY,
    )
    shape = field.shape
    return (output.reshape(shape), grad_input.reshape(shape), grad_kernel.reshape(kernel.shape))


def solution(mesh):
    lat_count, lon_count = mesh.devices.shape
    split = Mesh(mesh.devices.reshape(lat_count, lon_count // 2, 2), EVERY)
    block = P(None, None, "lat", LON)
    return jax.shard_map(
        on_device,
        mesh=split,
        in_specs=(block, P(), block),
        out_specs=(block, block, P()),
        check_vma=False,
    )
```

```python
import math

import jax
import jax.numpy as jnp
from jax import lax
from jax.experimental import pallas as pl
from jax.experimental.pallas import tpu as pltpu
from jax.sharding import Mesh
from jax.sharding import PartitionSpec as P

gelu_scale = math.sqrt(2.0 / math.pi)
ROWS, COLS, CH = 32, 128, 64
TAPS = 3 * CH
PIECES = 4
f32, bf16 = jnp.float32, jnp.bfloat16
LON = ("z", "side")
PLANE = ("lat", "side")
EVERY = ("lat", "z", "side")


def gelu_parts(hidden):
    square = hidden * hidden
    half = 0.5 + 0.5 * jnp.tanh(gelu_scale * hidden * (1.0 + 0.044715 * square))
    steep = gelu_scale * (1.0 + 3.0 * 0.044715 * square)
    return (hidden * half, half + 2.0 * hidden * half * (1.0 - half) * steep)


def roll(x, shift):
    return pltpu.roll(x, shift % x.shape[1], 1)


def lanes(width=COLS):
    return lax.broadcasted_iota(jnp.int32, (CH, width), 1)


def call(body, out_shape, args, scratch=(), flops=0, space=pltpu.VMEM, out_space=pltpu.VMEM, limit=24):
    outs = [jax.ShapeDtypeStruct(s, d) for s, d in out_shape]
    size = sum(a.size * a.dtype.itemsize for a in list(args) + outs)
    return pl.pallas_call(
        body,
        out_shape=outs,
        in_specs=[pl.BlockSpec(memory_space=space)] * len(args),
        out_specs=[pl.BlockSpec(memory_space=out_space)] * len(outs),
        scratch_shapes=list(scratch),
        cost_estimate=pl.CostEstimate(flops=flops, bytes_accessed=size, transcendentals=0),
        compiler_params=pltpu.CompilerParams(vmem_limit_bytes=int(limit * 2**20)),
    )(*args)


def pack_body(f_hbm, g_hbm, outer_ref, inner_ref, f_ref, g_ref, wide, sems):
    part = CH * ROWS // PIECES
    copies = [
        [
            pltpu.make_async_copy(src.at[pl.ds(i * part, part)], dst.at[pl.ds(i * part, part)], sems.at[at, i])
            for i in range(PIECES)
        ]
        for at, (src, dst) in enumerate(((f_hbm, f_ref), (g_hbm, g_ref)))
    ]
    for copy in copies[0] + copies[1]:
        copy.start()
    even = lax.axis_index("lat") % 2 == 0
    end = ROWS - 1
    slots = (((0, 0, end), (1, 1, end - 1)), ((2, 0, end),))
    for at, src in enumerate((f_ref, g_ref)):
        for i, copy in enumerate(copies[at]):
            copy.wait()
            wide[pl.ds(i * part, part), :] = src[pl.ds(i * part, part), :].astype(f32)
        for slot, low, high in slots[at]:
            first = wide[pl.ds(low, CH, stride=ROWS), :]
            last = wide[pl.ds(high, CH, stride=ROWS), :]
            outer_ref[pl.ds(slot * CH, CH), :] = jnp.where(even, first, last).astype(bf16)
            inner_ref[pl.ds(slot * CH, CH), :] = jnp.where(even, last, first).astype(bf16)


def turn_body(f_ref, g_ref, fr_ref, gr_ref, edge_ref, wide):
    lane = lanes()
    for at, (src, dst) in enumerate(((f_ref, fr_ref), (g_ref, gr_ref))):
        wide[...] = src[...].astype(f32)
        edge = jnp.zeros((CH, COLS), f32)
        for r in range(ROWS):
            row = wide[pl.ds(r, CH, stride=ROWS), :]
            edge = jnp.where((lane >= 4 * r) & (lane < 4 * r + 4), roll(row, 4 * r + 2), edge)
            dst[r] = row.astype(bf16)
        edge_ref[pl.ds(at * CH, CH), :] = edge.astype(bf16)


def row_halos(outer_ref, inner_ref):
    even = lax.axis_index("lat") % 2 == 0
    north = jnp.where(even, outer_ref[...], inner_ref[...]).astype(f32)
    south = jnp.where(even, inner_ref[...], outer_ref[...]).astype(f32)
    return [half[i * CH : (i + 1) * CH] for half in (north, south) for i in range(3)]


CORNERS = (
    ("s_near", 0, 0), ("s_near", 0, 1), ("s_cot", 0, 2), ("s_far", 4, 0), ("s_far", 4, 1),
    ("n_far", 120, 0), ("n_far", 120, 1), ("n_near", 124, 0), ("n_near", 124, 1), ("n_cot", 124, 2),
)


def edge_body(edge_ref, outer_ref, inner_ref, token_ref, far_ref, near_ref):
    names = ("n_near", "n_far", "n_cot", "s_near", "s_far", "s_cot")
    halos = dict(zip(names, row_halos(outer_ref, inner_ref)))
    kind = lanes() % 4
    lane = lanes()
    field = edge_ref[pl.ds(0, CH), :].astype(f32)
    cot = edge_ref[pl.ds(CH, CH), :].astype(f32)
    east = jnp.where(kind < 2, field, roll(cot, 1))
    west = jnp.where(kind >= 2, field, roll(cot, -1))
    for slot, (row, _, column) in enumerate(CORNERS):
        value = halos[row]
        to = 4 * slot + 3
        east = jnp.where(lane == to, roll(value, to - (126, 127, 127)[column]), east)
        to = 4 * slot
        west = jnp.where(lane == to, roll(value, to - (0, 1, 0)[column]), west)
    even = lax.axis_index("side") == 0
    far_ref[...] = jnp.where(even, west, east).astype(bf16)
    near_ref[...] = jnp.where(even, east, west).astype(bf16)


def column_halos(far_ref, near_ref):
    even = lax.axis_index("side") == 0
    far = far_ref[...].astype(f32)
    near = near_ref[...].astype(f32)
    west = jnp.where(even, far, near)
    east = jnp.where(even, near, far)
    lane = lanes()
    low = lane % 4 < 2
    field = jnp.where(low, west, east)
    cot = jnp.where(low, roll(west, -1), roll(east, 1))
    beyond = [jnp.zeros((CH, COLS), f32), jnp.zeros((CH, COLS), f32)]
    for slot, (_, base, column) in enumerate(CORNERS):
        at = column // 2
        for src, start, to in (
            (west, 4 * slot + 3, base + (0, 1, 1)[column]),
            (east, 4 * slot, base + (2, 3, 2)[column]),
        ):
            beyond[at] = jnp.where(lane == to, roll(src, to - start), beyond[at])
    return field, cot, beyond[0], beyond[1]


def stack_taps(out_ref, at, own, halo, lane):
    out_ref[at, pl.ds(0, CH), :] = roll(jnp.where(lane == COLS - 1, halo, own), 1).astype(bf16)
    out_ref[at, pl.ds(CH, CH), :] = own.astype(bf16)
    out_ref[at, pl.ds(2 * CH, CH), :] = roll(jnp.where(lane == 0, halo, own), -1).astype(bf16)


def dot(a, b):
    return jnp.dot(a, b, preferred_element_type=f32)


def interior_body(fr_ref, gr_ref, w_ref, out_ref, delta_ref, grad_ref, token_ref, xs):
    lane = lanes()
    inner = (lane > 0) & (lane < COLS - 1)
    none = jnp.zeros((CH, COLS), f32)
    for r in range(ROWS):
        stack_taps(xs, r, fr_ref[r].astype(f32), none, lane)
    weights = w_ref[...]
    for r in range(1, ROWS - 1, 2):
        window = jnp.concatenate(
            [xs[r - 1 : r + 2].reshape(3 * TAPS, COLS), xs[r : r + 3].reshape(3 * TAPS, COLS)], 1
        )
        value, slope = gelu_parts(dot(weights, window))
        for k in range(2):
            cut = slice(k * COLS, (k + 1) * COLS)
            out_ref[r + k - 1] = (fr_ref[r + k].astype(f32) + value[:, cut]).astype(bf16)
            delta = gr_ref[r + k].astype(f32) * slope[:, cut]
            delta_ref[r + k - 1] = jnp.where(inner, delta, 0.0).astype(bf16)
    total = None
    group = 10
    for r in range(0, ROWS - 2, group):
        left = jnp.concatenate([delta_ref[r + k] for k in range(group)], 1)
        right = jnp.concatenate([xs[r + k : r + k + 3].reshape(3 * TAPS, COLS) for k in range(group)], 1)
        term = dot_lanes(left, right)
        total = term if total is None else total + term
    grad_ref[...] = total
    token_ref[...] = jnp.zeros(token_ref.shape, f32)


def dot_lanes(a, b):
    return lax.dot_general(a, b, (((1,), (1,)), ((), ())), preferred_element_type=f32)


def border_body(
    fr_ref, gr_ref, edge_ref, far_ref, near_ref, outer_ref, inner_ref, w_ref, wa_ref, part_ref, wb_ref, wb3_ref,
    out_ref, outstrip_ref, delta_ref, dstrip_ref, grad_ref, xs,
):
    lat = lax.axis_index("lat")
    at_top = lat == 0
    at_bottom = lat == lax.axis_size("lat") - 1
    lane = lanes()
    n_near, n_far, n_cot, s_near, s_far, s_cot = row_halos(outer_ref, inner_ref)

    s, gs, beyond, gbeyond = column_halos(far_ref, near_ref)

    end = ROWS - 1
    stack_taps(xs, 0, n_far, roll(beyond, -122), lane)
    stack_taps(xs, 1, n_near, roll(beyond, -126), lane)
    for at, r in ((2, 0), (3, 1), (4, end - 1), (5, end)):
        stack_taps(xs, at, fr_ref[r].astype(f32), roll(s, -(4 * r + 2)), lane)
    stack_taps(xs, 6, s_near, roll(beyond, -2), lane)
    stack_taps(xs, 7, s_far, roll(beyond, -6), lane)

    weights = w_ref[...]
    window = jnp.concatenate([xs[1:4].reshape(3 * TAPS, COLS), xs[4:7].reshape(3 * TAPS, COLS)], 1)
    value, slope = gelu_parts(dot(weights, window))
    deltas = []
    for k, r in enumerate((0, end)):
        cut = slice(k * COLS, (k + 1) * COLS)
        out_ref[k] = (fr_ref[r].astype(f32) + value[:, cut]).astype(bf16)
        deltas.append((gr_ref[r].astype(f32) * slope[:, cut]).astype(bf16))
        delta_ref[k + 1] = deltas[k]

    def turned(flip, low):
        first = jnp.where(flip, xs[low + 2], xs[low])
        last = jnp.where(flip, xs[low], xs[low + 2])
        return jnp.concatenate([first, xs[low + 1], last], 0)

    outside = jnp.concatenate([turned(at_top, 0), turned(at_bottom, 5)], 1)
    slope = gelu_parts(dot(weights, outside))[1]
    delta_ref[0] = (n_cot * slope[:, :COLS]).astype(bf16)
    delta_ref[3] = (s_cot * slope[:, COLS:]).astype(bf16)

    edge = edge_ref[pl.ds(0, CH), :].astype(f32)
    halo = jnp.concatenate([s, beyond], 1)
    low = jnp.where(lane < 4, roll(s_near, 2), roll(s_far, 6))
    high = jnp.where(lane >= 124, roll(n_near, 126), roll(n_far, 122))
    own = jnp.concatenate([edge, jnp.where(lane < 64, low, high)], 1)
    wide_lane = lanes(2 * COLS)
    kind = wide_lane % 4
    small = lane % 4
    outer_taps = jnp.concatenate(
        [roll(jnp.where(kind == 0, halo, own), 1), halo, roll(jnp.where(kind == 3, halo, own), -1)], 0
    )
    inner_taps = jnp.concatenate(
        [roll(jnp.where(small == 1, s, edge), 1), edge, roll(jnp.where(small == 2, s, edge), -1)], 0
    )
    y = dot(wa_ref[...], jnp.concatenate([outer_taps, inner_taps], 1).astype(bf16))
    y0, y1, y2 = [y[i * CH : (i + 1) * CH, : 2 * COLS] for i in range(3)]
    straight = roll(y0, 4) + y1 + roll(y2, -4)
    backward = roll(y2, 4) + y1 + roll(y0, -4)
    flip = ((wide_lane >= 252) & at_top) | ((wide_lane >= 128) & (wide_lane < 132) & at_bottom)
    y0, y1, y2 = [y[i * CH : (i + 1) * CH, 2 * COLS :] for i in range(3)]
    packed = [jnp.where(flip, backward, straight), roll(y0, 4) + y1 + roll(y2, -4)]
    value, slope = gelu_parts(jnp.concatenate(packed, 1))
    own_cot = edge_ref[pl.ds(CH, CH), :].astype(f32)
    outstrip_ref[...] = (edge + value[:, 2 * COLS :]).astype(bf16)
    dstrip = jnp.concatenate([gs, gbeyond, own_cot], 1) * slope
    dstrip_ref[...] = dstrip.astype(bf16)

    used = ((small == 1) | (small == 2)) & (lane >= 4) & (lane < 4 * end)
    side = jnp.where(used, dstrip[:, 2 * COLS :], 0.0).astype(bf16)
    shifted = jnp.concatenate([roll(inner_taps, 4), inner_taps, roll(inner_taps, -4)], 0).astype(bf16)
    left = jnp.concatenate([deltas[0], deltas[1], side], 1)
    total = part_ref[...] + dot_lanes(left, jnp.concatenate([window, shifted], 1))
    total = total * grad_scale()
    count = grad_ref.shape[0]
    pieces = []
    for p in range(5):
        piece = total[:, p * COLS : (p + 1) * COLS]
        pieces.append([piece[j * count : (j + 1) * count] for j in range(CH // count)])
    tiles = [piece[j] for j in range(CH // count) for piece in pieces[:4]]
    last = pieces[4]
    for j in range(0, len(last), 2):
        tiles.append(jnp.concatenate(last[j : j + 2], 1))
    for q, tile in enumerate(tiles):
        grad_ref[:, 0, pl.ds(q * COLS, COLS)] = tile


def patched(row, packed, r, lane):
    return jnp.where((lane == 0) | (lane == COLS - 1), roll(packed, -(4 * r + 2)), row.astype(f32))


def write_out(wide, out_hbm, out_ref, sems):
    part = CH * ROWS // PIECES
    copies = []
    for i in range(PIECES):
        at = pl.ds(i * part, part)
        out_ref[at, :] = wide[at, :].astype(bf16)
        copies.append(pltpu.make_async_copy(out_ref.at[at], out_hbm.at[at], sems.at[i]))
        copies[-1].start()
    for copy in copies:
        copy.wait()


def restore_body(mid_ref, rim_ref, strip_ref, out_hbm, wide, out_ref, sems):
    lane = lanes()
    packed = strip_ref[...].astype(f32)
    wide[pl.ds(0, CH, stride=ROWS), :] = rim_ref[0].astype(f32)
    for r in range(1, ROWS - 1):
        wide[pl.ds(r, CH, stride=ROWS), :] = patched(mid_ref[r - 1], packed, r, lane)
    wide[pl.ds(ROWS - 1, CH, stride=ROWS), :] = rim_ref[1].astype(f32)
    write_out(wide, out_hbm, out_ref, sems)


def grad_scale():
    return float(ROWS * COLS * lax.axis_size(EVERY)) ** (-0.5)


def backward_body(after_ref, mid_ref, rim_ref, dstrip_ref, gr_ref, wb_ref, wb3_ref, out_hbm, xs, wide, out_ref, sems):
    lat = lax.axis_index("lat")
    at_top = lat == 0
    at_bottom = lat == lax.axis_size("lat") - 1
    lane = lanes()
    s = dstrip_ref[:, :COLS].astype(f32)
    beyond = dstrip_ref[:, COLS : 2 * COLS].astype(f32)
    own = dstrip_ref[:, 2 * COLS :].astype(f32)
    stack_taps(xs, 0, rim_ref[0].astype(f32), roll(beyond, -126), lane)
    stack_taps(xs, 1, rim_ref[1].astype(f32), roll(s, -2), lane)
    for r in range(1, ROWS - 1):
        stack_taps(xs, r + 1, patched(mid_ref[r - 1], own, r, lane), roll(s, -(4 * r + 2)), lane)
    stack_taps(xs, ROWS, rim_ref[2].astype(f32), roll(s, -(4 * ROWS - 2)), lane)
    stack_taps(xs, ROWS + 1, rim_ref[3].astype(f32), roll(beyond, -2), lane)
    weights = wb_ref[...]

    def put(r, back):
        wide[pl.ds(r, CH, stride=ROWS), :] = gr_ref[r].astype(f32) + back

    upper = jnp.where(at_top, wb3_ref[2], wb3_ref[0])
    lower = jnp.where(at_bottom, wb3_ref[0], wb3_ref[2])
    put(0, dot(upper, xs[0]) + dot(wb3_ref[1], xs[1]) + dot(wb3_ref[2], xs[2]))
    end = ROWS - 1
    put(end, dot(wb3_ref[0], xs[end]) + dot(wb3_ref[1], xs[end + 1]) + dot(lower, xs[end + 2]))
    for r in range(1, ROWS - 1, 2):
        window = jnp.concatenate(
            [xs[r : r + 3].reshape(3 * TAPS, COLS), xs[r + 1 : r + 4].reshape(3 * TAPS, COLS)], 1
        )
        back = dot(weights, window)
        put(r, back[:, :COLS])
        put(r + 1, back[:, COLS:])
    write_out(wide, out_hbm, out_ref, sems)


def fold_body(parts_ref, out_ref):
    total = jnp.sum(parts_ref[...], 0)
    if out_ref.shape[1] == 2:
        width = out_ref.shape[2]
        rest = jnp.zeros((1, 2 * width - total.shape[1]), f32)
        total = jnp.concatenate([total, rest], 1)
        total = jnp.concatenate([total[:, :width], total[:, width:]], 0)
    total = total.astype(out_ref.dtype)
    for i in range(out_ref.shape[0]):
        out_ref[i] = total


def unpack_body(parts_ref, out_hbm, out_ref, sems):
    count = parts_ref.shape[0]
    half = parts_ref.shape[2] // COLS
    parts = parts_ref[...].astype(f32)
    tiles = [parts[:, q // half, q % half * COLS : (q % half + 1) * COLS] for q in range(2 * half)]
    copies = []
    for tap in range(9):
        for j in range(CH // count):
            if tap < 8:
                tile, at = tiles[4 * j + tap // 2], tap % 2
            else:
                tile, at = tiles[4 * (CH // count) + j // 2], j % 2
            out_ref[tap, pl.ds(j * count, count), :] = tile[:, at * CH : (at + 1) * CH]
        copies.append(pltpu.make_async_copy(out_ref.at[tap], out_hbm.at[tap], sems.at[tap]))
        copies[-1].start()
    for copy in copies:
        copy.wait()


def outer_pairs(lat_count, lon_count):
    half = lon_count // 2
    pairs = []
    for l in range(lat_count):
        for m in range(lon_count):
            to = l - 1 if l % 2 == 0 else l + 1
            if 0 <= to < lat_count:
                pairs.append((l * lon_count + m, to * lon_count + m))
            else:
                pairs.append((l * lon_count + m, l * lon_count + (m + half) % lon_count))
    return pairs


def on_device(field, kernel, cotangent):
    lat_count = lax.axis_size("lat")
    lon_count = lax.axis_size(LON)
    plane = lax.axis_size(PLANE)
    flat = (CH * ROWS, COLS)
    rows_shape = (ROWS, CH, COLS)

    flat_field, flat_cotangent = field.reshape(flat), cotangent.reshape(flat)
    outer, inner, f_near, g_near = call(
        pack_body,
        [((TAPS, COLS), bf16), ((TAPS, COLS), bf16), (flat, bf16), (flat, bf16)],
        (flat_field, flat_cotangent),
        [pltpu.VMEM(flat, f32), pltpu.SemaphoreType.DMA((2, PIECES))],
        space=pl.ANY,
        limit=52.5,
    )
    outer = lax.ppermute(outer, EVERY, outer_pairs(lat_count, lon_count))
    inner = lax.ppermute(inner, "lat", [(i, i ^ 1) for i in range(lat_count)])
    fr, gr, edge = call(
        turn_body,
        [(rows_shape, bf16), (rows_shape, bf16), ((2 * CH, COLS), bf16)],
        (f_near, g_near),
        [pltpu.VMEM(flat, f32)],
    )

    w3 = jnp.transpose(kernel, (0, 2, 1, 3)).reshape(TAPS, TAPS)
    w = jnp.transpose(kernel, (2, 0, 1, 3)).reshape(CH, 3 * TAPS)
    turned = kernel[::-1, ::-1]
    wb3 = jnp.transpose(turned, (0, 3, 1, 2)).reshape(3, CH, TAPS)
    wb = jnp.transpose(turned, (3, 0, 1, 2)).reshape(CH, 3 * TAPS)
    piece = 9 * CH * CH // plane
    conv_flops = 2 * 9 * CH * CH * ROWS * COLS
    out_mid, delta_mid, grad_mid, token = call(
        interior_body,
        [
            ((ROWS - 2, CH, COLS), bf16),
            ((ROWS - 2, CH, COLS), bf16),
            ((CH, 3 * TAPS), f32),
            ((8, COLS), f32),
        ],
        (fr, gr, w),
        [pltpu.VMEM((ROWS, TAPS, COLS), bf16)],
        2 * conv_flops,
    )

    far, near = call(edge_body, [((CH, COLS), bf16)] * 2, (edge, outer, inner, token))
    swaps = [(i, (i + 1 if i % 2 else i - 1) % lon_count) for i in range(lon_count)]
    far = lax.ppermute(far, LON, swaps)
    near = lax.ppermute(near, "side", [(0, 1), (1, 0)])

    out_rim, out_strip, delta_rim, dstrip, grad = call(
        border_body,
        [
            ((2, CH, COLS), bf16),
            ((CH, COLS), bf16),
            ((4, CH, COLS), bf16),
            ((CH, 3 * COLS), bf16),
            ((plane, 1, piece), f32),
        ],
        (fr, gr, edge, far, near, outer, inner, w, w3, grad_mid, wb, wb3),
        [pltpu.VMEM((8, TAPS, COLS), bf16)],
        conv_flops // 4,
    )

    root = 6 * plane // 8
    def exchange(parts, axes, first):
        count = lax.axis_size(axes)
        order = [(first + i) % count for i in range(count)]
        return lax.all_to_all(parts, axes, 0, 0, axis_index_groups=[order])

    def spread(parts, shape, dtype):
        return call(fold_body, [(shape, dtype)], (parts,))[0]

    writing = [pltpu.VMEM(flat, f32), pltpu.VMEM(flat, bf16), pltpu.SemaphoreType.DMA((PIECES,))]
    parts = exchange(grad, PLANE, root)
    (output,) = call(restore_body, [(flat, bf16)], (out_mid, out_rim, out_strip), writing, out_space=pl.ANY)
    parts = exchange(spread(parts, (lax.axis_size("z"), 1, piece), f32), "z", lax.axis_size("z") // 2)
    (grad_input,) = call(
        backward_body,
        [(flat, bf16)],
        (parts, delta_mid, delta_rim, dstrip, gr, wb, wb3),
        [pltpu.VMEM((ROWS + 2, TAPS, COLS), bf16)] + writing,
        conv_flops,
        out_space=pl.ANY,
    )
    packed = (plane, 2, -(-piece // (2 * COLS)) * COLS)
    parts = exchange(spread(parts, packed, bf16), PLANE, root)
    (grad_kernel,) = call(
        unpack_body,
        [((9, CH, CH), f32)],
        (parts,),
        [pltpu.VMEM((9, CH, CH), f32), pltpu.SemaphoreType.DMA((9,))],
        out_space=pl.ANY,
    )
    shape = field.shape
    return (output.reshape(shape), grad_input.reshape(shape), grad_kernel.reshape(kernel.shape))


def solution(mesh):
    lat_count, lon_count = mesh.devices.shape
    split = Mesh(mesh.devices.reshape(lat_count, lon_count // 2, 2), EVERY)
    block = P(None, None, "lat", LON)
    return jax.shard_map(
        on_device,
        mesh=split,
        in_specs=(block, P(), block),
        out_specs=(block, block, P()),
        check_vma=False,
    )
```

```python
import math

import jax
import jax.numpy as jnp
from jax import lax
from jax.experimental import pallas as pl
from jax.experimental.pallas import tpu as pltpu
from jax.sharding import Mesh
from jax.sharding import PartitionSpec as P

gelu_scale = math.sqrt(2.0 / math.pi)
ROWS, COLS, CH = 32, 128, 64
TAPS = 3 * CH
PIECES = 4
f32, bf16 = jnp.float32, jnp.bfloat16
LON = ("z", "side")
PLANE = ("lat", "side")
EVERY = ("lat", "z", "side")


def gelu_parts(hidden):
    square = hidden * hidden
    half = 0.5 + 0.5 * jnp.tanh(gelu_scale * hidden * (1.0 + 0.044715 * square))
    steep = gelu_scale * (1.0 + 3.0 * 0.044715 * square)
    return (hidden * half, half + 2.0 * hidden * half * (1.0 - half) * steep)


def roll(x, shift):
    return pltpu.roll(x, shift % x.shape[1], 1)


def lanes(width=COLS):
    return lax.broadcasted_iota(jnp.int32, (CH, width), 1)


def call(body, out_shape, args, scratch=(), flops=0, space=pltpu.VMEM, out_space=pltpu.VMEM, limit=24):
    outs = [jax.ShapeDtypeStruct(s, d) for s, d in out_shape]
    size = sum(a.size * a.dtype.itemsize for a in list(args) + outs)
    return pl.pallas_call(
        body,
        out_shape=outs,
        in_specs=[pl.BlockSpec(memory_space=space)] * len(args),
        out_specs=[pl.BlockSpec(memory_space=out_space)] * len(outs),
        scratch_shapes=list(scratch),
        cost_estimate=pl.CostEstimate(flops=flops, bytes_accessed=size, transcendentals=0),
        compiler_params=pltpu.CompilerParams(vmem_limit_bytes=int(limit * 2**20)),
    )(*args)


def pack_body(f_hbm, g_hbm, outer_ref, inner_ref, f_ref, g_ref, wide, sems):
    part = CH * ROWS // PIECES
    copies = [
        [
            pltpu.make_async_copy(src.at[pl.ds(i * part, part)], dst.at[pl.ds(i * part, part)], sems.at[at, i])
            for i in range(PIECES)
        ]
        for at, (src, dst) in enumerate(((f_hbm, f_ref), (g_hbm, g_ref)))
    ]
    for copy in copies[0] + copies[1]:
        copy.start()
    even = lax.axis_index("lat") % 2 == 0
    end = ROWS - 1
    slots = (((0, 0, end), (1, 1, end - 1)), ((2, 0, end),))
    for at, src in enumerate((f_ref, g_ref)):
        for i, copy in enumerate(copies[at]):
            copy.wait()
            wide[pl.ds(i * part, part), :] = src[pl.ds(i * part, part), :].astype(f32)
        for slot, low, high in slots[at]:
            first = wide[pl.ds(low, CH, stride=ROWS), :]
            last = wide[pl.ds(high, CH, stride=ROWS), :]
            outer_ref[pl.ds(slot * CH, CH), :] = jnp.where(even, first, last).astype(bf16)
            inner_ref[pl.ds(slot * CH, CH), :] = jnp.where(even, last, first).astype(bf16)


def turn_body(f_ref, g_ref, fr_ref, gr_ref, edge_ref, wide):
    lane = lanes()
    for at, (src, dst) in enumerate(((f_ref, fr_ref), (g_ref, gr_ref))):
        wide[...] = src[...].astype(f32)
        edge = jnp.zeros((CH, COLS), f32)
        for r in range(ROWS):
            row = wide[pl.ds(r, CH, stride=ROWS), :]
            edge = jnp.where((lane >= 4 * r) & (lane < 4 * r + 4), roll(row, 4 * r + 2), edge)
            dst[r] = row.astype(bf16)
        edge_ref[pl.ds(at * CH, CH), :] = edge.astype(bf16)


def row_halos(outer_ref, inner_ref):
    even = lax.axis_index("lat") % 2 == 0
    north = jnp.where(even, outer_ref[...], inner_ref[...]).astype(f32)
    south = jnp.where(even, inner_ref[...], outer_ref[...]).astype(f32)
    return [half[i * CH : (i + 1) * CH] for half in (north, south) for i in range(3)]


CORNERS = (
    ("s_near", 0, 0), ("s_near", 0, 1), ("s_cot", 0, 2), ("s_far", 4, 0), ("s_far", 4, 1),
    ("n_far", 120, 0), ("n_far", 120, 1), ("n_near", 124, 0), ("n_near", 124, 1), ("n_cot", 124, 2),
)


def edge_body(edge_ref, outer_ref, inner_ref, token_ref, far_ref, near_ref):
    names = ("n_near", "n_far", "n_cot", "s_near", "s_far", "s_cot")
    halos = dict(zip(names, row_halos(outer_ref, inner_ref)))
    kind = lanes() % 4
    lane = lanes()
    field = edge_ref[pl.ds(0, CH), :].astype(f32)
    cot = edge_ref[pl.ds(CH, CH), :].astype(f32)
    east = jnp.where(kind < 2, field, roll(cot, 1))
    west = jnp.where(kind >= 2, field, roll(cot, -1))
    for slot, (row, _, column) in enumerate(CORNERS):
        value = halos[row]
        to = 4 * slot + 3
        east = jnp.where(lane == to, roll(value, to - (126, 127, 127)[column]), east)
        to = 4 * slot
        west = jnp.where(lane == to, roll(value, to - (0, 1, 0)[column]), west)
    even = lax.axis_index("side") == 0
    far_ref[...] = jnp.where(even, west, east).astype(bf16)
    near_ref[...] = jnp.where(even, east, west).astype(bf16)


def column_halos(far_ref, near_ref):
    even = lax.axis_index("side") == 0
    far = far_ref[...].astype(f32)
    near = near_ref[...].astype(f32)
    west = jnp.where(even, far, near)
    east = jnp.where(even, near, far)
    lane = lanes()
    low = lane % 4 < 2
    field = jnp.where(low, west, east)
    cot = jnp.where(low, roll(west, -1), roll(east, 1))
    beyond = [jnp.zeros((CH, COLS), f32), jnp.zeros((CH, COLS), f32)]
    for slot, (_, base, column) in enumerate(CORNERS):
        at = column // 2
        for src, start, to in (
            (west, 4 * slot + 3, base + (0, 1, 1)[column]),
            (east, 4 * slot, base + (2, 3, 2)[column]),
        ):
            beyond[at] = jnp.where(lane == to, roll(src, to - start), beyond[at])
    return field, cot, beyond[0], beyond[1]


def stack_taps(out_ref, at, own, halo, lane):
    out_ref[at, pl.ds(0, CH), :] = roll(jnp.where(lane == COLS - 1, halo, own), 1).astype(bf16)
    out_ref[at, pl.ds(CH, CH), :] = own.astype(bf16)
    out_ref[at, pl.ds(2 * CH, CH), :] = roll(jnp.where(lane == 0, halo, own), -1).astype(bf16)


def dot(a, b):
    return jnp.dot(a, b, preferred_element_type=f32)


def interior_body(fr_ref, gr_ref, w_ref, out_ref, delta_ref, grad_ref, token_ref, xs):
    lane = lanes()
    inner = (lane > 0) & (lane < COLS - 1)
    none = jnp.zeros((CH, COLS), f32)
    for r in range(ROWS):
        stack_taps(xs, r, fr_ref[r].astype(f32), none, lane)
    weights = w_ref[...]
    for r in range(1, ROWS - 1, 2):
        window = jnp.concatenate(
            [xs[r - 1 : r + 2].reshape(3 * TAPS, COLS), xs[r : r + 3].reshape(3 * TAPS, COLS)], 1
        )
        value, slope = gelu_parts(dot(weights, window))
        for k in range(2):
            cut = slice(k * COLS, (k + 1) * COLS)
            out_ref[r + k - 1] = (fr_ref[r + k].astype(f32) + value[:, cut]).astype(bf16)
            delta = gr_ref[r + k].astype(f32) * slope[:, cut]
            delta_ref[r + k - 1] = jnp.where(inner, delta, 0.0).astype(bf16)
    total = None
    group = 10
    for r in range(0, ROWS - 2, group):
        left = jnp.concatenate([delta_ref[r + k] for k in range(group)], 1)
        right = jnp.concatenate([xs[r + k : r + k + 3].reshape(3 * TAPS, COLS) for k in range(group)], 1)
        term = dot_lanes(left, right)
        total = term if total is None else total + term
    grad_ref[...] = total
    token_ref[...] = jnp.zeros(token_ref.shape, f32)


def dot_lanes(a, b):
    return lax.dot_general(a, b, (((1,), (1,)), ((), ())), preferred_element_type=f32)


def border_body(
    fr_ref, gr_ref, edge_ref, far_ref, near_ref, outer_ref, inner_ref, w_ref, wa_ref, part_ref, wb_ref, wb3_ref,
    out_ref, outstrip_ref, delta_ref, dstrip_ref, grad_ref, xs,
):
    lat = lax.axis_index("lat")
    at_top = lat == 0
    at_bottom = lat == lax.axis_size("lat") - 1
    lane = lanes()
    n_near, n_far, n_cot, s_near, s_far, s_cot = row_halos(outer_ref, inner_ref)

    s, gs, beyond, gbeyond = column_halos(far_ref, near_ref)

    end = ROWS - 1
    stack_taps(xs, 0, n_far, roll(beyond, -122), lane)
    stack_taps(xs, 1, n_near, roll(beyond, -126), lane)
    for at, r in ((2, 0), (3, 1), (4, end - 1), (5, end)):
        stack_taps(xs, at, fr_ref[r].astype(f32), roll(s, -(4 * r + 2)), lane)
    stack_taps(xs, 6, s_near, roll(beyond, -2), lane)
    stack_taps(xs, 7, s_far, roll(beyond, -6), lane)

    weights = w_ref[...]
    window = jnp.concatenate([xs[1:4].reshape(3 * TAPS, COLS), xs[4:7].reshape(3 * TAPS, COLS)], 1)
    value, slope = gelu_parts(dot(weights, window))
    deltas = []
    for k, r in enumerate((0, end)):
        cut = slice(k * COLS, (k + 1) * COLS)
        out_ref[k] = (fr_ref[r].astype(f32) + value[:, cut]).astype(bf16)
        deltas.append((gr_ref[r].astype(f32) * slope[:, cut]).astype(bf16))
        delta_ref[k + 1] = deltas[k]

    def turned(flip, low):
        first = jnp.where(flip, xs[low + 2], xs[low])
        last = jnp.where(flip, xs[low], xs[low + 2])
        return jnp.concatenate([first, xs[low + 1], last], 0)

    outside = jnp.concatenate([turned(at_top, 0), turned(at_bottom, 5)], 1)
    slope = gelu_parts(dot(weights, outside))[1]
    delta_ref[0] = (n_cot * slope[:, :COLS]).astype(bf16)
    delta_ref[3] = (s_cot * slope[:, COLS:]).astype(bf16)

    edge = edge_ref[pl.ds(0, CH), :].astype(f32)
    halo = jnp.concatenate([s, beyond], 1)
    low = jnp.where(lane < 4, roll(s_near, 2), roll(s_far, 6))
    high = jnp.where(lane >= 124, roll(n_near, 126), roll(n_far, 122))
    own = jnp.concatenate([edge, jnp.where(lane < 64, low, high)], 1)
    wide_lane = lanes(2 * COLS)
    kind = wide_lane % 4
    small = lane % 4
    outer_taps = jnp.concatenate(
        [roll(jnp.where(kind == 0, halo, own), 1), halo, roll(jnp.where(kind == 3, halo, own), -1)], 0
    )
    inner_taps = jnp.concatenate(
        [roll(jnp.where(small == 1, s, edge), 1), edge, roll(jnp.where(small == 2, s, edge), -1)], 0
    )
    y = dot(wa_ref[...], jnp.concatenate([outer_taps, inner_taps], 1).astype(bf16))
    y0, y1, y2 = [y[i * CH : (i + 1) * CH, : 2 * COLS] for i in range(3)]
    straight = roll(y0, 4) + y1 + roll(y2, -4)
    backward = roll(y2, 4) + y1 + roll(y0, -4)
    flip = ((wide_lane >= 252) & at_top) | ((wide_lane >= 128) & (wide_lane < 132) & at_bottom)
    y0, y1, y2 = [y[i * CH : (i + 1) * CH, 2 * COLS :] for i in range(3)]
    packed = [jnp.where(flip, backward, straight), roll(y0, 4) + y1 + roll(y2, -4)]
    value, slope = gelu_parts(jnp.concatenate(packed, 1))
    own_cot = edge_ref[pl.ds(CH, CH), :].astype(f32)
    outstrip_ref[...] = (edge + value[:, 2 * COLS :]).astype(bf16)
    dstrip = jnp.concatenate([gs, gbeyond, own_cot], 1) * slope
    dstrip_ref[...] = dstrip.astype(bf16)

    used = ((small == 1) | (small == 2)) & (lane >= 4) & (lane < 4 * end)
    side = jnp.where(used, dstrip[:, 2 * COLS :], 0.0).astype(bf16)
    shifted = jnp.concatenate([roll(inner_taps, 4), inner_taps, roll(inner_taps, -4)], 0).astype(bf16)
    left = jnp.concatenate([deltas[0], deltas[1], side], 1)
    total = part_ref[...] + dot_lanes(left, jnp.concatenate([window, shifted], 1))
    total = total * grad_scale()
    count = grad_ref.shape[0]
    pieces = []
    for p in range(5):
        piece = total[:, p * COLS : (p + 1) * COLS]
        pieces.append([piece[j * count : (j + 1) * count] for j in range(CH // count)])
    tiles = [piece[j] for j in range(CH // count) for piece in pieces[:4]]
    last = pieces[4]
    for j in range(0, len(last), 2):
        tiles.append(jnp.concatenate(last[j : j + 2], 1))
    for q, tile in enumerate(tiles):
        grad_ref[:, 0, pl.ds(q * COLS, COLS)] = tile


def patched(row, packed, r, lane):
    return jnp.where((lane == 0) | (lane == COLS - 1), roll(packed, -(4 * r + 2)), row.astype(f32))


def write_out(wide, out_hbm, out_ref, sems):
    part = CH * ROWS // PIECES
    copies = []
    for i in range(PIECES):
        at = pl.ds(i * part, part)
        out_ref[at, :] = wide[at, :].astype(bf16)
        copies.append(pltpu.make_async_copy(out_ref.at[at], out_hbm.at[at], sems.at[i]))
        copies[-1].start()
    for copy in copies:
        copy.wait()


def restore_body(mid_ref, rim_ref, strip_ref, out_hbm, wide, out_ref, sems):
    lane = lanes()
    packed = strip_ref[...].astype(f32)
    wide[pl.ds(0, CH, stride=ROWS), :] = rim_ref[0].astype(f32)
    for r in range(1, ROWS - 1):
        wide[pl.ds(r, CH, stride=ROWS), :] = patched(mid_ref[r - 1], packed, r, lane)
    wide[pl.ds(ROWS - 1, CH, stride=ROWS), :] = rim_ref[1].astype(f32)
    write_out(wide, out_hbm, out_ref, sems)


def grad_scale():
    return float(ROWS * COLS * lax.axis_size(EVERY)) ** (-0.5)


def backward_body(after_ref, mid_ref, rim_ref, dstrip_ref, gr_ref, wb_ref, wb3_ref, out_hbm, xs, wide, out_ref, sems):
    lat = lax.axis_index("lat")
    at_top = lat == 0
    at_bottom = lat == lax.axis_size("lat") - 1
    lane = lanes()
    s = dstrip_ref[:, :COLS].astype(f32)
    beyond = dstrip_ref[:, COLS : 2 * COLS].astype(f32)
    own = dstrip_ref[:, 2 * COLS :].astype(f32)
    stack_taps(xs, 0, rim_ref[0].astype(f32), roll(beyond, -126), lane)
    stack_taps(xs, 1, rim_ref[1].astype(f32), roll(s, -2), lane)
    for r in range(1, ROWS - 1):
        stack_taps(xs, r + 1, patched(mid_ref[r - 1], own, r, lane), roll(s, -(4 * r + 2)), lane)
    stack_taps(xs, ROWS, rim_ref[2].astype(f32), roll(s, -(4 * ROWS - 2)), lane)
    stack_taps(xs, ROWS + 1, rim_ref[3].astype(f32), roll(beyond, -2), lane)
    weights = wb_ref[...]

    def put(r, back):
        wide[pl.ds(r, CH, stride=ROWS), :] = gr_ref[r].astype(f32) + back

    upper = jnp.where(at_top, wb3_ref[2], wb3_ref[0])
    lower = jnp.where(at_bottom, wb3_ref[0], wb3_ref[2])
    put(0, dot(upper, xs[0]) + dot(wb3_ref[1], xs[1]) + dot(wb3_ref[2], xs[2]))
    end = ROWS - 1
    put(end, dot(wb3_ref[0], xs[end]) + dot(wb3_ref[1], xs[end + 1]) + dot(lower, xs[end + 2]))
    for r in range(1, ROWS - 1, 2):
        window = jnp.concatenate(
            [xs[r : r + 3].reshape(3 * TAPS, COLS), xs[r + 1 : r + 4].reshape(3 * TAPS, COLS)], 1
        )
        back = dot(weights, window)
        put(r, back[:, :COLS])
        put(r + 1, back[:, COLS:])
    write_out(wide, out_hbm, out_ref, sems)


def fold_body(parts_ref, out_ref):
    total = jnp.sum(parts_ref[...], 0)
    total = total.astype(out_ref.dtype)
    for i in range(out_ref.shape[0]):
        out_ref[i] = total


def pack_chunk_body(parts_ref, out_hbm, few_ref, sems):
    width = few_ref.shape[2]
    total = jnp.sum(parts_ref[...], 0)
    rest = jnp.zeros((1, 2 * width - total.shape[1]), f32)
    total = jnp.concatenate([total, rest], 1)
    total = jnp.concatenate([total[:, :width], total[:, width:]], 0).astype(bf16)
    few = few_ref.shape[0]
    for i in range(few):
        few_ref[i] = total
    copies = [
        pltpu.make_async_copy(few_ref, out_hbm.at[pl.ds(i * few, few)], sems.at[i])
        for i in range(out_hbm.shape[0] // few)
    ]
    for copy in copies:
        copy.start()
    for copy in copies:
        copy.wait()


def unpack_body(parts_ref, out_hbm, out_ref, sems):
    count = parts_ref.shape[0]
    half = parts_ref.shape[2] // COLS
    parts = parts_ref[...].astype(f32)
    tiles = [parts[:, q // half, q % half * COLS : (q % half + 1) * COLS] for q in range(2 * half)]
    copies = []
    for tap in range(9):
        for j in range(CH // count):
            if tap < 8:
                tile, at = tiles[4 * j + tap // 2], tap % 2
            else:
                tile, at = tiles[4 * (CH // count) + j // 2], j % 2
            out_ref[tap, pl.ds(j * count, count), :] = tile[:, at * CH : (at + 1) * CH]
        copies.append(pltpu.make_async_copy(out_ref.at[tap], out_hbm.at[tap], sems.at[tap]))
        copies[-1].start()
    for copy in copies:
        copy.wait()


def outer_pairs(lat_count, lon_count):
    half = lon_count // 2
    pairs = []
    for l in range(lat_count):
        for m in range(lon_count):
            to = l - 1 if l % 2 == 0 else l + 1
            if 0 <= to < lat_count:
                pairs.append((l * lon_count + m, to * lon_count + m))
            else:
                pairs.append((l * lon_count + m, l * lon_count + (m + half) % lon_count))
    return pairs


def on_device(field, kernel, cotangent):
    lat_count = lax.axis_size("lat")
    lon_count = lax.axis_size(LON)
    plane = lax.axis_size(PLANE)
    flat = (CH * ROWS, COLS)
    rows_shape = (ROWS, CH, COLS)

    flat_field, flat_cotangent = field.reshape(flat), cotangent.reshape(flat)
    outer, inner, f_near, g_near = call(
        pack_body,
        [((TAPS, COLS), bf16), ((TAPS, COLS), bf16), (flat, bf16), (flat, bf16)],
        (flat_field, flat_cotangent),
        [pltpu.VMEM(flat, f32), pltpu.SemaphoreType.DMA((2, PIECES))],
        space=pl.ANY,
        limit=52.5,
    )
    outer = lax.ppermute(outer, EVERY, outer_pairs(lat_count, lon_count))
    inner = lax.ppermute(inner, "lat", [(i, i ^ 1) for i in range(lat_count)])
    fr, gr, edge = call(
        turn_body,
        [(rows_shape, bf16), (rows_shape, bf16), ((2 * CH, COLS), bf16)],
        (f_near, g_near),
        [pltpu.VMEM(flat, f32)],
    )

    w3 = jnp.transpose(kernel, (0, 2, 1, 3)).reshape(TAPS, TAPS)
    w = jnp.transpose(kernel, (2, 0, 1, 3)).reshape(CH, 3 * TAPS)
    turned = kernel[::-1, ::-1]
    wb3 = jnp.transpose(turned, (0, 3, 1, 2)).reshape(3, CH, TAPS)
    wb = jnp.transpose(turned, (3, 0, 1, 2)).reshape(CH, 3 * TAPS)
    piece = 9 * CH * CH // plane
    conv_flops = 2 * 9 * CH * CH * ROWS * COLS
    out_mid, delta_mid, grad_mid, token = call(
        interior_body,
        [
            ((ROWS - 2, CH, COLS), bf16),
            ((ROWS - 2, CH, COLS), bf16),
            ((CH, 3 * TAPS), f32),
            ((8, COLS), f32),
        ],
        (fr, gr, w),
        [pltpu.VMEM((ROWS, TAPS, COLS), bf16)],
        2 * conv_flops,
    )

    far, near = call(edge_body, [((CH, COLS), bf16)] * 2, (edge, outer, inner, token))
    swaps = [(i, (i + 1 if i % 2 else i - 1) % lon_count) for i in range(lon_count)]
    far = lax.ppermute(far, LON, swaps)
    near = lax.ppermute(near, "side", [(0, 1), (1, 0)])

    out_rim, out_strip, delta_rim, dstrip, grad = call(
        border_body,
        [
            ((2, CH, COLS), bf16),
            ((CH, COLS), bf16),
            ((4, CH, COLS), bf16),
            ((CH, 3 * COLS), bf16),
            ((plane, 1, piece), f32),
        ],
        (fr, gr, edge, far, near, outer, inner, w, w3, grad_mid, wb, wb3),
        [pltpu.VMEM((8, TAPS, COLS), bf16)],
        conv_flops // 4,
    )

    root = (5 * plane // 8) % plane
    def exchange(parts, axes, first):
        count = lax.axis_size(axes)
        order = [(first + i) % count for i in range(count)]
        return lax.all_to_all(parts, axes, 0, 0, axis_index_groups=[order])

    def spread(parts, shape, dtype):
        return call(fold_body, [(shape, dtype)], (parts,))[0]

    writing = [pltpu.VMEM(flat, f32), pltpu.VMEM(flat, bf16), pltpu.SemaphoreType.DMA((PIECES,))]
    parts = exchange(grad, PLANE, root)
    (output,) = call(restore_body, [(flat, bf16)], (out_mid, out_rim, out_strip), writing, out_space=pl.ANY)
    parts = exchange(spread(parts, (lax.axis_size("z"), 1, piece), f32), "z", lax.axis_size("z") // 2)
    (grad_input,) = call(
        backward_body,
        [(flat, bf16)],
        (parts, delta_mid, delta_rim, dstrip, gr, wb, wb3),
        [pltpu.VMEM((ROWS + 2, TAPS, COLS), bf16)] + writing,
        conv_flops,
        out_space=pl.ANY,
    )
    packed = (plane, 2, -(-piece // (2 * COLS)) * COLS)
    few = plane // PIECES
    (parts,) = call(
        pack_chunk_body,
        [(packed, bf16)],
        (parts,),
        [pltpu.VMEM((few,) + packed[1:], bf16), pltpu.SemaphoreType.DMA((PIECES,))],
        out_space=pl.ANY,
    )
    parts = exchange(parts, PLANE, root)
    (grad_kernel,) = call(
        unpack_body,
        [((9, CH, CH), f32)],
        (parts,),
        [pltpu.VMEM((9, CH, CH), f32), pltpu.SemaphoreType.DMA((9,))],
        out_space=pl.ANY,
    )
    shape = field.shape
    return (output.reshape(shape), grad_input.reshape(shape), grad_kernel.reshape(kernel.shape))


def solution(mesh):
    lat_count, lon_count = mesh.devices.shape
    split = Mesh(mesh.devices.reshape(lat_count, lon_count // 2, 2), EVERY)
    block = P(None, None, "lat", LON)
    return jax.shard_map(
        on_device,
        mesh=split,
        in_specs=(block, P(), block),
        out_specs=(block, block, P()),
        check_vma=False,
    )
```

```python
import math

import jax
import jax.numpy as jnp
from jax import lax
from jax.experimental import pallas as pl
from jax.experimental.pallas import tpu as pltpu
from jax.sharding import Mesh
from jax.sharding import PartitionSpec as P

gelu_scale = math.sqrt(2.0 / math.pi)
ROWS, COLS, CH = 32, 128, 64
TAPS = 3 * CH
PIECES = 8
f32, bf16 = jnp.float32, jnp.bfloat16
LON = ("z", "side")
PLANE = ("lat", "side")
EVERY = ("lat", "z", "side")


def gelu_parts(hidden):
    square = hidden * hidden
    half = 0.5 + 0.5 * jnp.tanh(gelu_scale * hidden * (1.0 + 0.044715 * square))
    steep = gelu_scale * (1.0 + 3.0 * 0.044715 * square)
    return (hidden * half, half + 2.0 * hidden * half * (1.0 - half) * steep)


def roll(x, shift):
    return pltpu.roll(x, shift % x.shape[1], 1)


def lanes(width=COLS):
    return lax.broadcasted_iota(jnp.int32, (CH, width), 1)


def call(body, out_shape, args, scratch=(), flops=0, space=pltpu.VMEM, out_space=pltpu.VMEM, limit=24):
    outs = [jax.ShapeDtypeStruct(s, d) for s, d in out_shape]
    size = sum(a.size * a.dtype.itemsize for a in list(args) + outs)
    return pl.pallas_call(
        body,
        out_shape=outs,
        in_specs=[pl.BlockSpec(memory_space=space)] * len(args),
        out_specs=[pl.BlockSpec(memory_space=out_space)] * len(outs),
        scratch_shapes=list(scratch),
        cost_estimate=pl.CostEstimate(flops=flops, bytes_accessed=size, transcendentals=0),
        compiler_params=pltpu.CompilerParams(vmem_limit_bytes=int(limit * 2**20)),
    )(*args)


def pack_body(f_hbm, g_hbm, outer_ref, inner_ref, f_ref, g_ref, wide, sems):
    part = CH * ROWS // PIECES
    copies = [
        [
            pltpu.make_async_copy(src.at[pl.ds(i * part, part)], dst.at[pl.ds(i * part, part)], sems.at[at, i])
            for i in range(PIECES)
        ]
        for at, (src, dst) in enumerate(((f_hbm, f_ref), (g_hbm, g_ref)))
    ]
    for copy in copies[0] + copies[1]:
        copy.start()
    even = lax.axis_index("lat") % 2 == 0
    end = ROWS - 1
    slots = (((0, 0, end), (1, 1, end - 1)), ((2, 0, end),))
    for at, src in enumerate((f_ref, g_ref)):
        for i, copy in enumerate(copies[at]):
            copy.wait()
            wide[pl.ds(i * part, part), :] = src[pl.ds(i * part, part), :].astype(f32)
        for slot, low, high in slots[at]:
            first = wide[pl.ds(low, CH, stride=ROWS), :]
            last = wide[pl.ds(high, CH, stride=ROWS), :]
            outer_ref[pl.ds(slot * CH, CH), :] = jnp.where(even, first, last).astype(bf16)
            inner_ref[pl.ds(slot * CH, CH), :] = jnp.where(even, last, first).astype(bf16)


def turn_body(f_ref, g_ref, fr_ref, gr_ref, edge_ref, wide):
    lane = lanes()
    for at, (src, dst) in enumerate(((f_ref, fr_ref), (g_ref, gr_ref))):
        wide[...] = src[...].astype(f32)
        edge = jnp.zeros((CH, COLS), f32)
        for r in range(ROWS):
            row = wide[pl.ds(r, CH, stride=ROWS), :]
            edge = jnp.where((lane >= 4 * r) & (lane < 4 * r + 4), roll(row, 4 * r + 2), edge)
            dst[r] = row.astype(bf16)
        edge_ref[pl.ds(at * CH, CH), :] = edge.astype(bf16)


def row_halos(outer_ref, inner_ref):
    even = lax.axis_index("lat") % 2 == 0
    north = jnp.where(even, outer_ref[...], inner_ref[...]).astype(f32)
    south = jnp.where(even, inner_ref[...], outer_ref[...]).astype(f32)
    return [half[i * CH : (i + 1) * CH] for half in (north, south) for i in range(3)]


CORNERS = (
    ("s_near", 0, 0), ("s_near", 0, 1), ("s_cot", 0, 2), ("s_far", 4, 0), ("s_far", 4, 1),
    ("n_far", 120, 0), ("n_far", 120, 1), ("n_near", 124, 0), ("n_near", 124, 1), ("n_cot", 124, 2),
)


def edge_body(edge_ref, outer_ref, inner_ref, token_ref, far_ref, near_ref):
    names = ("n_near", "n_far", "n_cot", "s_near", "s_far", "s_cot")
    halos = dict(zip(names, row_halos(outer_ref, inner_ref)))
    kind = lanes() % 4
    lane = lanes()
    field = edge_ref[pl.ds(0, CH), :].astype(f32)
    cot = edge_ref[pl.ds(CH, CH), :].astype(f32)
    east = jnp.where(kind < 2, field, roll(cot, 1))
    west = jnp.where(kind >= 2, field, roll(cot, -1))
    for slot, (row, _, column) in enumerate(CORNERS):
        value = halos[row]
        to = 4 * slot + 3
        east = jnp.where(lane == to, roll(value, to - (126, 127, 127)[column]), east)
        to = 4 * slot
        west = jnp.where(lane == to, roll(value, to - (0, 1, 0)[column]), west)
    even = lax.axis_index("side") == 0
    far_ref[...] = jnp.where(even, west, east).astype(bf16)
    near_ref[...] = jnp.where(even, east, west).astype(bf16)


def column_halos(far_ref, near_ref):
    even = lax.axis_index("side") == 0
    far = far_ref[...].astype(f32)
    near = near_ref[...].astype(f32)
    west = jnp.where(even, far, near)
    east = jnp.where(even, near, far)
    lane = lanes()
    low = lane % 4 < 2
    field = jnp.where(low, west, east)
    cot = jnp.where(low, roll(west, -1), roll(east, 1))
    beyond = [jnp.zeros((CH, COLS), f32), jnp.zeros((CH, COLS), f32)]
    for slot, (_, base, column) in enumerate(CORNERS):
        at = column // 2
        for src, start, to in (
            (west, 4 * slot + 3, base + (0, 1, 1)[column]),
            (east, 4 * slot, base + (2, 3, 2)[column]),
        ):
            beyond[at] = jnp.where(lane == to, roll(src, to - start), beyond[at])
    return field, cot, beyond[0], beyond[1]


def stack_taps(out_ref, at, own, halo, lane):
    out_ref[at, pl.ds(0, CH), :] = roll(jnp.where(lane == COLS - 1, halo, own), 1).astype(bf16)
    out_ref[at, pl.ds(CH, CH), :] = own.astype(bf16)
    out_ref[at, pl.ds(2 * CH, CH), :] = roll(jnp.where(lane == 0, halo, own), -1).astype(bf16)


def dot(a, b):
    return jnp.dot(a, b, preferred_element_type=f32)


def interior_body(fr_ref, gr_ref, w_ref, out_ref, delta_ref, grad_ref, token_ref, xs):
    lane = lanes()
    inner = (lane > 0) & (lane < COLS - 1)
    none = jnp.zeros((CH, COLS), f32)
    for r in range(ROWS):
        stack_taps(xs, r, fr_ref[r].astype(f32), none, lane)
    weights = w_ref[...]
    for r in range(1, ROWS - 1, 2):
        window = jnp.concatenate(
            [xs[r - 1 : r + 2].reshape(3 * TAPS, COLS), xs[r : r + 3].reshape(3 * TAPS, COLS)], 1
        )
        value, slope = gelu_parts(dot(weights, window))
        for k in range(2):
            cut = slice(k * COLS, (k + 1) * COLS)
            out_ref[r + k - 1] = (fr_ref[r + k].astype(f32) + value[:, cut]).astype(bf16)
            delta = gr_ref[r + k].astype(f32) * slope[:, cut]
            delta_ref[r + k - 1] = jnp.where(inner, delta, 0.0).astype(bf16)
    total = None
    group = 10
    for r in range(0, ROWS - 2, group):
        left = jnp.concatenate([delta_ref[r + k] for k in range(group)], 1)
        right = jnp.concatenate([xs[r + k : r + k + 3].reshape(3 * TAPS, COLS) for k in range(group)], 1)
        term = dot_lanes(left, right)
        total = term if total is None else total + term
    grad_ref[...] = total
    token_ref[...] = jnp.zeros(token_ref.shape, f32)


def dot_lanes(a, b):
    return lax.dot_general(a, b, (((1,), (1,)), ((), ())), preferred_element_type=f32)


def border_body(
    fr_ref, gr_ref, edge_ref, far_ref, near_ref, outer_ref, inner_ref, w_ref, wa_ref, part_ref, wb_ref, wb3_ref,
    out_ref, outstrip_ref, delta_ref, dstrip_ref, grad_ref, xs,
):
    lat = lax.axis_index("lat")
    at_top = lat == 0
    at_bottom = lat == lax.axis_size("lat") - 1
    lane = lanes()
    n_near, n_far, n_cot, s_near, s_far, s_cot = row_halos(outer_ref, inner_ref)

    s, gs, beyond, gbeyond = column_halos(far_ref, near_ref)

    end = ROWS - 1
    stack_taps(xs, 0, n_far, roll(beyond, -122), lane)
    stack_taps(xs, 1, n_near, roll(beyond, -126), lane)
    for at, r in ((2, 0), (3, 1), (4, end - 1), (5, end)):
        stack_taps(xs, at, fr_ref[r].astype(f32), roll(s, -(4 * r + 2)), lane)
    stack_taps(xs, 6, s_near, roll(beyond, -2), lane)
    stack_taps(xs, 7, s_far, roll(beyond, -6), lane)

    weights = w_ref[...]
    window = jnp.concatenate([xs[1:4].reshape(3 * TAPS, COLS), xs[4:7].reshape(3 * TAPS, COLS)], 1)
    value, slope = gelu_parts(dot(weights, window))
    deltas = []
    for k, r in enumerate((0, end)):
        cut = slice(k * COLS, (k + 1) * COLS)
        out_ref[k] = (fr_ref[r].astype(f32) + value[:, cut]).astype(bf16)
        deltas.append((gr_ref[r].astype(f32) * slope[:, cut]).astype(bf16))
        delta_ref[k + 1] = deltas[k]

    def turned(flip, low):
        first = jnp.where(flip, xs[low + 2], xs[low])
        last = jnp.where(flip, xs[low], xs[low + 2])
        return jnp.concatenate([first, xs[low + 1], last], 0)

    outside = jnp.concatenate([turned(at_top, 0), turned(at_bottom, 5)], 1)
    slope = gelu_parts(dot(weights, outside))[1]
    delta_ref[0] = (n_cot * slope[:, :COLS]).astype(bf16)
    delta_ref[3] = (s_cot * slope[:, COLS:]).astype(bf16)

    edge = edge_ref[pl.ds(0, CH), :].astype(f32)
    halo = jnp.concatenate([s, beyond], 1)
    low = jnp.where(lane < 4, roll(s_near, 2), roll(s_far, 6))
    high = jnp.where(lane >= 124, roll(n_near, 126), roll(n_far, 122))
    own = jnp.concatenate([edge, jnp.where(lane < 64, low, high)], 1)
    wide_lane = lanes(2 * COLS)
    kind = wide_lane % 4
    small = lane % 4
    outer_taps = jnp.concatenate(
        [roll(jnp.where(kind == 0, halo, own), 1), halo, roll(jnp.where(kind == 3, halo, own), -1)], 0
    )
    inner_taps = jnp.concatenate(
        [roll(jnp.where(small == 1, s, edge), 1), edge, roll(jnp.where(small == 2, s, edge), -1)], 0
    )
    y = dot(wa_ref[...], jnp.concatenate([outer_taps, inner_taps], 1).astype(bf16))
    y0, y1, y2 = [y[i * CH : (i + 1) * CH, : 2 * COLS] for i in range(3)]
    straight = roll(y0, 4) + y1 + roll(y2, -4)
    backward = roll(y2, 4) + y1 + roll(y0, -4)
    flip = ((wide_lane >= 252) & at_top) | ((wide_lane >= 128) & (wide_lane < 132) & at_bottom)
    y0, y1, y2 = [y[i * CH : (i + 1) * CH, 2 * COLS :] for i in range(3)]
    packed = [jnp.where(flip, backward, straight), roll(y0, 4) + y1 + roll(y2, -4)]
    value, slope = gelu_parts(jnp.concatenate(packed, 1))
    own_cot = edge_ref[pl.ds(CH, CH), :].astype(f32)
    outstrip_ref[...] = (edge + value[:, 2 * COLS :]).astype(bf16)
    dstrip = jnp.concatenate([gs, gbeyond, own_cot], 1) * slope
    dstrip_ref[...] = dstrip.astype(bf16)

    used = ((small == 1) | (small == 2)) & (lane >= 4) & (lane < 4 * end)
    side = jnp.where(used, dstrip[:, 2 * COLS :], 0.0).astype(bf16)
    shifted = jnp.concatenate([roll(inner_taps, 4), inner_taps, roll(inner_taps, -4)], 0).astype(bf16)
    left = jnp.concatenate([deltas[0], deltas[1], side], 1)
    total = part_ref[...] + dot_lanes(left, jnp.concatenate([window, shifted], 1))
    total = total * grad_scale()
    count = grad_ref.shape[0]
    pieces = []
    for p in range(5):
        piece = total[:, p * COLS : (p + 1) * COLS]
        pieces.append([piece[j * count : (j + 1) * count] for j in range(CH // count)])
    tiles = [piece[j] for j in range(CH // count) for piece in pieces[:4]]
    last = pieces[4]
    for j in range(0, len(last), 2):
        tiles.append(jnp.concatenate(last[j : j + 2], 1))
    for q, tile in enumerate(tiles):
        grad_ref[:, 0, pl.ds(q * COLS, COLS)] = tile


def patched(row, packed, r, lane):
    return jnp.where((lane == 0) | (lane == COLS - 1), roll(packed, -(4 * r + 2)), row.astype(f32))


def write_out(wide, out_hbm, out_ref, sems):
    part = CH * ROWS // PIECES
    copies = []
    for i in range(PIECES):
        at = pl.ds(i * part, part)
        out_ref[at, :] = wide[at, :].astype(bf16)
        copies.append(pltpu.make_async_copy(out_ref.at[at], out_hbm.at[at], sems.at[i]))
        copies[-1].start()
    for copy in copies:
        copy.wait()


def restore_body(mid_ref, rim_ref, strip_ref, out_hbm, wide, out_ref, sems):
    lane = lanes()
    packed = strip_ref[...].astype(f32)
    wide[pl.ds(0, CH, stride=ROWS), :] = rim_ref[0].astype(f32)
    for r in range(1, ROWS - 1):
        wide[pl.ds(r, CH, stride=ROWS), :] = patched(mid_ref[r - 1], packed, r, lane)
    wide[pl.ds(ROWS - 1, CH, stride=ROWS), :] = rim_ref[1].astype(f32)
    write_out(wide, out_hbm, out_ref, sems)


def grad_scale():
    return float(ROWS * COLS * lax.axis_size(EVERY)) ** (-0.5)


def backward_body(after_ref, mid_ref, rim_ref, dstrip_ref, gr_ref, wb_ref, wb3_ref, out_hbm, xs, wide, out_ref, sems):
    lat = lax.axis_index("lat")
    at_top = lat == 0
    at_bottom = lat == lax.axis_size("lat") - 1
    lane = lanes()
    s = dstrip_ref[:, :COLS].astype(f32)
    beyond = dstrip_ref[:, COLS : 2 * COLS].astype(f32)
    own = dstrip_ref[:, 2 * COLS :].astype(f32)
    stack_taps(xs, 0, rim_ref[0].astype(f32), roll(beyond, -126), lane)
    stack_taps(xs, 1, rim_ref[1].astype(f32), roll(s, -2), lane)
    for r in range(1, ROWS - 1):
        stack_taps(xs, r + 1, patched(mid_ref[r - 1], own, r, lane), roll(s, -(4 * r + 2)), lane)
    stack_taps(xs, ROWS, rim_ref[2].astype(f32), roll(s, -(4 * ROWS - 2)), lane)
    stack_taps(xs, ROWS + 1, rim_ref[3].astype(f32), roll(beyond, -2), lane)
    weights = wb_ref[...]

    def put(r, back):
        wide[pl.ds(r, CH, stride=ROWS), :] = gr_ref[r].astype(f32) + back

    upper = jnp.where(at_top, wb3_ref[2], wb3_ref[0])
    lower = jnp.where(at_bottom, wb3_ref[0], wb3_ref[2])
    put(0, dot(upper, xs[0]) + dot(wb3_ref[1], xs[1]) + dot(wb3_ref[2], xs[2]))
    end = ROWS - 1
    put(end, dot(wb3_ref[0], xs[end]) + dot(wb3_ref[1], xs[end + 1]) + dot(lower, xs[end + 2]))
    for r in range(1, ROWS - 1, 2):
        window = jnp.concatenate(
            [xs[r : r + 3].reshape(3 * TAPS, COLS), xs[r + 1 : r + 4].reshape(3 * TAPS, COLS)], 1
        )
        back = dot(weights, window)
        put(r, back[:, :COLS])
        put(r + 1, back[:, COLS:])
    write_out(wide, out_hbm, out_ref, sems)


def fold_body(parts_ref, out_ref):
    total = jnp.sum(parts_ref[...], 0)
    if out_ref.shape[1] == 2:
        width = out_ref.shape[2]
        rest = jnp.zeros((1, 2 * width - total.shape[1]), f32)
        total = jnp.concatenate([total, rest], 1)
        total = jnp.concatenate([total[:, :width], total[:, width:]], 0)
    total = total.astype(out_ref.dtype)
    for i in range(out_ref.shape[0]):
        out_ref[i] = total


def unpack_body(parts_ref, out_hbm, out_ref, sems):
    count = parts_ref.shape[0]
    half = parts_ref.shape[2] // COLS
    parts = parts_ref[...].astype(f32)
    tiles = [parts[:, q // half, q % half * COLS : (q % half + 1) * COLS] for q in range(2 * half)]
    copies = []
    for tap in range(9):
        for j in range(CH // count):
            if tap < 8:
                tile, at = tiles[4 * j + tap // 2], tap % 2
            else:
                tile, at = tiles[4 * (CH // count) + j // 2], j % 2
            out_ref[tap, pl.ds(j * count, count), :] = tile[:, at * CH : (at + 1) * CH]
        copies.append(pltpu.make_async_copy(out_ref.at[tap], out_hbm.at[tap], sems.at[tap]))
        copies[-1].start()
    for copy in copies:
        copy.wait()


def outer_pairs(lat_count, lon_count):
    half = lon_count // 2
    pairs = []
    for l in range(lat_count):
        for m in range(lon_count):
            to = l - 1 if l % 2 == 0 else l + 1
            if 0 <= to < lat_count:
                pairs.append((l * lon_count + m, to * lon_count + m))
            else:
                pairs.append((l * lon_count + m, l * lon_count + (m + half) % lon_count))
    return pairs


def on_device(field, kernel, cotangent):
    lat_count = lax.axis_size("lat")
    lon_count = lax.axis_size(LON)
    plane = lax.axis_size(PLANE)
    flat = (CH * ROWS, COLS)
    rows_shape = (ROWS, CH, COLS)

    flat_field, flat_cotangent = field.reshape(flat), cotangent.reshape(flat)
    outer, inner, f_near, g_near = call(
        pack_body,
        [((TAPS, COLS), bf16), ((TAPS, COLS), bf16), (flat, bf16), (flat, bf16)],
        (flat_field, flat_cotangent),
        [pltpu.VMEM(flat, f32), pltpu.SemaphoreType.DMA((2, PIECES))],
        space=pl.ANY,
        limit=52.5,
    )
    outer = lax.ppermute(outer, EVERY, outer_pairs(lat_count, lon_count))
    inner = lax.ppermute(inner, "lat", [(i, i ^ 1) for i in range(lat_count)])
    fr, gr, edge = call(
        turn_body,
        [(rows_shape, bf16), (rows_shape, bf16), ((2 * CH, COLS), bf16)],
        (f_near, g_near),
        [pltpu.VMEM(flat, f32)],
    )

    w3 = jnp.transpose(kernel, (0, 2, 1, 3)).reshape(TAPS, TAPS)
    w = jnp.transpose(kernel, (2, 0, 1, 3)).reshape(CH, 3 * TAPS)
    turned = kernel[::-1, ::-1]
    wb3 = jnp.transpose(turned, (0, 3, 1, 2)).reshape(3, CH, TAPS)
    wb = jnp.transpose(turned, (3, 0, 1, 2)).reshape(CH, 3 * TAPS)
    piece = 9 * CH * CH // plane
    conv_flops = 2 * 9 * CH * CH * ROWS * COLS
    out_mid, delta_mid, grad_mid, token = call(
        interior_body,
        [
            ((ROWS - 2, CH, COLS), bf16),
            ((ROWS - 2, CH, COLS), bf16),
            ((CH, 3 * TAPS), f32),
            ((8, COLS), f32),
        ],
        (fr, gr, w),
        [pltpu.VMEM((ROWS, TAPS, COLS), bf16)],
        2 * conv_flops,
    )

    far, near = call(edge_body, [((CH, COLS), bf16)] * 2, (edge, outer, inner, token))
    swaps = [(i, (i + 1 if i % 2 else i - 1) % lon_count) for i in range(lon_count)]
    far = lax.ppermute(far, LON, swaps)
    near = lax.ppermute(near, "side", [(0, 1), (1, 0)])

    out_rim, out_strip, delta_rim, dstrip, grad = call(
        border_body,
        [
            ((2, CH, COLS), bf16),
            ((CH, COLS), bf16),
            ((4, CH, COLS), bf16),
            ((CH, 3 * COLS), bf16),
            ((plane, 1, piece), f32),
        ],
        (fr, gr, edge, far, near, outer, inner, w, w3, grad_mid, wb, wb3),
        [pltpu.VMEM((8, TAPS, COLS), bf16)],
        conv_flops // 4,
    )

    root = (5 * plane // 8) % plane
    def exchange(parts, axes, first):
        count = lax.axis_size(axes)
        order = [(first + i) % count for i in range(count)]
        return lax.all_to_all(parts, axes, 0, 0, axis_index_groups=[order])

    def spread(parts, shape, dtype):
        return call(fold_body, [(shape, dtype)], (parts,))[0]

    writing = [pltpu.VMEM(flat, f32), pltpu.VMEM(flat, bf16), pltpu.SemaphoreType.DMA((PIECES,))]
    parts = exchange(grad, PLANE, root)
    (output,) = call(restore_body, [(flat, bf16)], (out_mid, out_rim, out_strip), writing, out_space=pl.ANY)
    parts = exchange(spread(parts, (lax.axis_size("z"), 1, piece), f32), "z", lax.axis_size("z") // 2)
    (grad_input,) = call(
        backward_body,
        [(flat, bf16)],
        (parts, delta_mid, delta_rim, dstrip, gr, wb, wb3),
        [pltpu.VMEM((ROWS + 2, TAPS, COLS), bf16)] + writing,
        conv_flops,
        out_space=pl.ANY,
    )
    packed = (plane, 2, -(-piece // (2 * COLS)) * COLS)
    parts = exchange(spread(parts, packed, bf16), PLANE, root)
    (grad_kernel,) = call(
        unpack_body,
        [((9, CH, CH), f32)],
        (parts,),
        [pltpu.VMEM((9, CH, CH), f32), pltpu.SemaphoreType.DMA((9,))],
        out_space=pl.ANY,
    )
    shape = field.shape
    return (output.reshape(shape), grad_input.reshape(shape), grad_kernel.reshape(kernel.shape))


def solution(mesh):
    lat_count, lon_count = mesh.devices.shape
    split = Mesh(mesh.devices.reshape(lat_count, lon_count // 2, 2), EVERY)
    block = P(None, None, "lat", LON)
    return jax.shard_map(
        on_device,
        mesh=split,
        in_specs=(block, P(), block),
        out_specs=(block, block, P()),
        check_vma=False,
    )
```
